32 devices in a mesh: dp: 16 (over z, x, core), pair: 2 (over y).
Axes of the slice: x: 2, y: 2, z: 4, core: 2. Of those that a mesh axis runs over, the one named last changes fastest.
Arguments:
- tokens: bfloat16 [2, 4096, 768], P('pair', 'dp'), may hold values from -6 to 6
- cotangent: bfloat16 [2, 4096, 768], P('pair', 'dp'), may hold values from -6 to 6
- lengths: int32 [2, 16, 2], P('pair', 'dp'), may hold values from 1 to 192, 256 in all within a row
- mats: float32 [2, 7077888], P(None, ('dp', 'pair')), may hold values from -1.6329932 to 1.6329932, as said below
- mats_m: float32 [2, 7077888], P(None, ('dp', 'pair')), may hold values from -0.5 to 0.5
- mats_v: float32 [2, 7077888], P(None, ('dp', 'pair')), may hold values from 0.0005 to 0.008
- vecs: float32 [2, 9216], P(None, ('dp', 'pair')), may hold values from -1.2 to 2.2, as said below
- vecs_m: float32 [2, 9216], P(None, ('dp', 'pair')), may hold values from -0.5 to 0.5
- vecs_v: float32 [2, 9216], P(None, ('dp', 'pair')), may hold values from 0.0005 to 0.008
Outputs:
- head_out: bfloat16 [2, 4096, 768], P('pair', 'dp')
- token_grad: float32 [2, 4096, 768], P('pair', 'dp')
- contrastive: float32 [], replicated
- grad_norm: float32 [], replicated
- new_mats: float32 [2, 7077888], P(None, ('dp', 'pair'))
- new_mats_m: float32 [2, 7077888], P(None, ('dp', 'pair'))
- new_mats_v: float32 [2, 7077888], P(None, ('dp', 'pair'))
- new_vecs: float32 [2, 9216], P(None, ('dp', 'pair'))
- new_vecs_m: float32 [2, 9216], P(None, ('dp', 'pair'))
- new_vecs_v: float32 [2, 9216], P(None, ('dp', 'pair'))
The draws below stay inside these ranges and needn't reach their ends.
Inputs may be any that keep to these rules, and one draw needn't show every extreme that they name: Each row of 2 lengths sums to 256; its longest span has at most 192 tokens. `mats`: Real-valued entries. `vecs`: Real-valued entries.
All inputs are finite; a program needn't handle non-finite values.
Results may differ from the reference program's by a relative error of at most 0.017.
Values may be sent and summed in bfloat16 or wider, within the bound.
No kernel may reach another device: no remote copies, remote signals or barrier semaphores. Data moves between devices by JAX's collectives and lax.ppermute only.
A program may use at most 256 MiB of HBM per device.

```python
import math
import jax
import jax.numpy as jnp
import numpy as np
from jax import lax

D = 768
HEADS = 12
HEAD_DIM = 64
FF = 3072
SPAN = 128
SPANS_DEV = 2
LAYERS = 2
STEP = 10
TOK_DEV = 256
MOST_SPAN = 192
NDOC = 32
PL = 7077888
QL = 9216
N_DP = 16
N_PAIR = 2


def draw_mats(key, part):
    key = jax.random.fold_in(key, 11)
    normal_draw = jnp.clip(jax.random.normal(key, (LAYERS, PL), jnp.float32), -4.0, 4.0)
    scales = jnp.concatenate([jnp.full((3 * D * D,), D ** (-0.5), jnp.float32), jnp.full((D * D,), (SPAN / D) ** 0.5, jnp.float32), jnp.full((D * FF,), D ** (-0.5), jnp.float32), jnp.full((FF * D,), FF ** (-0.5), jnp.float32)])
    return normal_draw * scales[None, :]


def draw_vecs(key, part):
    key = jax.random.fold_in(key, 23)
    normal_draw = 0.3 * jnp.clip(jax.random.normal(key, (LAYERS, QL), jnp.float32), -4.0, 4.0)
    gains_mark = jnp.concatenate([jnp.zeros((3 * D,), jnp.float32), jnp.ones((D,), jnp.float32), jnp.zeros((2 * D + FF,), jnp.float32), jnp.ones((D,), jnp.float32), jnp.zeros((D,), jnp.float32)])
    return normal_draw + gains_mark[None, :]


def shard_levels(rng, extent, split, smallest, high):
    level, own = 1.0, jax.random.fold_in(rng, 6)
    for position, shards_of in split:
        draws = jnp.exp(jax.random.uniform(jax.random.fold_in(own, position), (shards_of,), jnp.float32, smallest / len(split), high / len(split)))
        level = level * jnp.repeat(draws, extent[position] // shards_of).reshape([-1 if axis == position else 1 for axis in range(len(extent))])
    return level


def profile(amount, total, limit, slope):
    weights = [(1 << 20) // math.isqrt(rank ** slope) + 1 for rank in range(2, amount + 1)]
    spare, given = total - limit - (amount - 1), [1] * (amount - 1)
    while spare > 0:
        candidates = [i for i in range(amount - 1) if given[i] < limit]
        mass, left = sum([weights[i] for i in candidates]), spare
        for i in candidates:
            more = min(limit - given[i], max(1, left * weights[i] // mass), spare)
            given[i] = given[i] + more
            spare = spare - more
    return np.array([limit] + given)


def uneven(key, count, total, limit, skew):
    if count == 2:
        one = jax.random.randint(key, (), max(1, total - limit), min(limit, total - 1) + 1)
        return jnp.stack([one, total - one])
    tallies = jnp.asarray(profile(count, total, limit, skew), jnp.int32)
    twos = (count - 1) // 2
    donor, receiver = tallies[1:1 + 2 * twos:2], tallies[2:2 + 2 * twos:2]
    room = jnp.minimum(donor - 1, limit - receiver)
    shifted = jax.random.randint(jax.random.fold_in(key, 1), (twos,), 0, 1 << 20) % (room + 1)
    tallies = tallies.at[1:1 + 2 * twos:2].set(donor - shifted).at[2:2 + 2 * twos:2].set(receiver + shifted)
    return tallies[jax.random.permutation(jax.random.fold_in(key, 2), count)]


def scatter_about(own_key, dims, scale, reach, cuts=(), kind=jnp.bfloat16):
    level = shard_levels(own_key, dims, cuts, -0.22, 0.18) if cuts else 1.0
    entries = jax.random.normal(own_key, dims, jnp.float32) * scale * level
    return jnp.minimum(jnp.maximum(entries, -reach), reach).astype(kind)


def setup_inputs(seed: int = 0) -> dict:
    keys = jax.random.split(jax.random.key(seed), 10)
    tokens = scatter_about(keys[0], (N_PAIR, N_DP * TOK_DEV, D), 1.0, 6.0, ((0, 2), (1, 16)))
    cotangent = scatter_about(keys[1], (N_PAIR, N_DP * TOK_DEV, D), 1.0, 6.0, ((0, 2), (1, 16)))
    lengths = jax.vmap(lambda own: uneven(own, SPANS_DEV, TOK_DEV, MOST_SPAN, 1))(jax.random.split(keys[2], N_PAIR * N_DP)).reshape((N_PAIR, N_DP, SPANS_DEV)).astype(jnp.int32)
    mats = draw_mats(jax.random.fold_in(keys[9], 71), 0)
    mats_m = scatter_about(keys[4], (LAYERS, PL), 0.11, 0.5, ((1, 32),), jnp.float32)
    mats_v = jnp.clip(jnp.exp(math.log(0.008) - 2.7725887 * jax.random.uniform(keys[5], (LAYERS, PL), jnp.float32) ** shard_levels(keys[5], (LAYERS, PL), ((1, 32),), -0.2, 0.2)), 0.0005, 0.008)
    vecs = draw_vecs(jax.random.fold_in(keys[9], 71), 0)
    vecs_m = scatter_about(keys[7], (LAYERS, QL), 0.11, 0.5, ((1, 32),), jnp.float32)
    vecs_v = jnp.clip(jnp.exp(math.log(0.008) - 2.7725887 * jax.random.uniform(keys[8], (LAYERS, QL), jnp.float32) ** shard_levels(keys[8], (LAYERS, QL), ((1, 32),), -0.2, 0.2)), 0.0005, 0.008)
    return {"tokens": tokens, "cotangent": cotangent, "lengths": lengths, "mats": mats, "mats_m": mats_m, "mats_v": mats_v, "vecs": vecs, "vecs_m": vecs_m, "vecs_v": vecs_v}


@jax.custom_vjp
def low(v):
    return lax.optimization_barrier(v.astype(jnp.bfloat16)).astype(jnp.float32)

@jax.custom_vjp
def low_back(v):
    return v

def low_keep(v):
    return (low(v), None)

def low_pass(kept, grad):
    return (grad,)

def back_keep(v):
    return (v, None)

def back_low(kept, grad):
    return (low(grad),)
low.defvjp(low_keep, low_pass)
low_back.defvjp(back_keep, back_low)
norm_epsilon = 1e-12
masked_score = -1000000000.0
beta_one = 0.9
beta_two = 0.999
adam_epsilon = 1e-08
weight_decay = 0.01

def matmul(left_side, right_side):
    return jnp.dot(left_side, right_side, precision=lax.Precision.HIGHEST, preferred_element_type=jnp.float32)

def layer_norm(resid, gain, shift):
    centred = resid - lax.optimization_barrier(jnp.mean(resid, axis=-1, keepdims=True))
    spread = lax.optimization_barrier(jnp.mean(centred * centred, axis=-1, keepdims=True))
    return centred * lax.rsqrt(spread + norm_epsilon) * gain + shift

def unpack(mat_row, vec_row):
    edge_one = 3 * D * D
    edge_two = 4 * D * D
    edge_three = edge_two + D * FF
    input_weight = mat_row[:edge_one].reshape(D, 3 * D)
    output_weight = mat_row[edge_one:edge_two].reshape(D, D)
    expand_weight = mat_row[edge_two:edge_three].reshape(D, FF)
    shrink_weight = mat_row[edge_three:].reshape(FF, D)
    pieces = []
    cursor = 0
    for piece_len in (D, D, D, D, D, FF, D, D, D):
        pieces.append(vec_row[cursor:cursor + piece_len])
        cursor = cursor + piece_len
    return (input_weight, output_weight, expand_weight, shrink_weight) + tuple(pieces)

def layer(params, inputs, same_span):
    input_weight, output_weight, expand_weight, shrink_weight, query_bias, value_bias, output_bias, first_gain, first_shift, expand_bias, shrink_bias, second_gain, second_shift = params
    row_count = inputs.shape[0]
    joint = matmul(low(inputs), input_weight)
    queries = low(low_back(joint[:, :D] + query_bias))
    key_rows = low(low_back(joint[:, D:2 * D]))
    values = low(low_back(joint[:, 2 * D:] + value_bias))
    query_heads = queries.reshape(row_count, HEADS, HEAD_DIM)
    key_heads = key_rows.reshape(row_count, HEADS, HEAD_DIM)
    value_heads = values.reshape(row_count, HEADS, HEAD_DIM)
    scores = jnp.einsum('thd,shd->hts', query_heads, key_heads, precision=lax.Precision.HIGHEST) * HEAD_DIM ** (-0.5)
    scores = low_back(scores)
    scores = jnp.where(same_span[None, :, :], scores, masked_score)
    row_max = lax.optimization_barrier(jnp.max(scores, axis=-1, keepdims=True))
    raised = jnp.exp(scores - row_max)
    portions = raised / lax.optimization_barrier(jnp.sum(raised, axis=-1, keepdims=True))
    attended = jnp.einsum('hts,shd->thd', low(portions), value_heads, precision=lax.Precision.HIGHEST)
    attended = low(low_back(attended.reshape(row_count, D)))
    branch = low_back(matmul(attended, output_weight) + output_bias)
    hidden = layer_norm(inputs + branch, first_gain, first_shift)
    before = low_back(matmul(low(hidden), expand_weight) + expand_bias)
    activated = low(jax.nn.gelu(before, approximate=False))
    feed = low_back(matmul(activated, shrink_weight) + shrink_bias)
    return layer_norm(hidden + feed, second_gain, second_shift)

def block(mats_low, vecs_low, token_rows, span_lengths):
    layer_one = unpack(mats_low[0], vecs_low[0])
    layer_two = unpack(mats_low[1], vecs_low[1])
    positions = jnp.arange(TOK_DEV, dtype=jnp.int32)
    starts = (jnp.cumsum(span_lengths) - span_lengths).astype(jnp.int32)
    span_of = lax.optimization_barrier(jnp.sum((positions[:, None] >= starts[None, :]).astype(jnp.int32), axis=1))
    same_span = span_of[:, None] == span_of[None, :]
    heads_mark = positions[None, :] == starts[:, None]
    is_cls = jnp.any(heads_mark, axis=0)
    picker = heads_mark.astype(jnp.float32)
    early_out = layer(layer_one, token_rows, same_span)
    cls_rows = matmul(picker, early_out)
    mixture = jnp.where(is_cls[:, None], early_out, token_rows)
    return (cls_rows, layer(layer_two, mixture, same_span))

def contrast_loss(cls_flat):
    key_count = cls_flat.shape[0]
    score_scale = 2.0 / math.sqrt(D)
    sent_cls = low(cls_flat)
    scores = low_back(matmul(sent_cls, sent_cls.T) * score_scale)
    row_index = jnp.arange(key_count, dtype=jnp.int32)
    scores = jnp.where(row_index[:, None] == row_index[None, :], masked_score, scores)
    partner = (row_index + NDOC) % key_count
    row_max = lax.optimization_barrier(jnp.max(scores, axis=-1, keepdims=True))
    logsum = row_max[:, 0] + jnp.log(lax.optimization_barrier(jnp.sum(jnp.exp(scores - row_max), axis=-1)))
    positive = lax.optimization_barrier(jnp.sum(jnp.where(row_index[None, :] == partner[:, None], scores, 0.0), axis=1))
    return jnp.sum(logsum - positive)

def adamw_update(weight, moment_one, moment_two, gradient, step_rate, decay_rate):
    first_new = beta_one * moment_one + (1.0 - beta_one) * gradient
    second_new = beta_two * moment_two + (1.0 - beta_two) * gradient * gradient
    first_hat = first_new / (1.0 - beta_one ** STEP)
    second_hat = second_new / (1.0 - beta_two ** STEP)
    weight_new = weight - step_rate * (first_hat / (jnp.sqrt(second_hat) + adam_epsilon) + decay_rate * weight)
    return (weight_new, first_new, second_new)

def reference(tokens, cotangent, lengths, mats, mats_m, mats_v, vecs, vecs_m, vecs_v):
    blocks = tokens.astype(jnp.float32).reshape(N_PAIR * N_DP, TOK_DEV, D)
    cot_blocks = cotangent.astype(jnp.float32).reshape(N_PAIR * N_DP, TOK_DEV, D)
    span_table = lengths.reshape(N_PAIR * N_DP, SPANS_DEV).astype(jnp.int32)
    saved_block = jax.checkpoint(block)

    def forward(mats_full, vecs_full, blocks_full):
        mats_low = low(mats_full)
        vecs_low = low(vecs_full)

        def scan_step(carried, item_pair):
            token_rows, span_lengths = item_pair
            cls_rows, late_out = saved_block(mats_low, vecs_low, token_rows, span_lengths)
            return (carried, (cls_rows, late_out))
        _, (cls_all, outs) = lax.scan(scan_step, jnp.zeros((), jnp.float32), (blocks_full, span_table))
        return (contrast_loss(cls_all.reshape(2 * NDOC, D)), outs)
    (loss_sum, outs), pull_back = jax.vjp(forward, mats, vecs, blocks)
    mats_grad, vecs_grad, block_grad = pull_back((jnp.ones((), jnp.float32), cot_blocks))
    total_sq = jnp.sum(mats_grad * mats_grad) + jnp.sum(vecs_grad * vecs_grad)
    grad_norm = jnp.sqrt(total_sq)
    clip_factor = jnp.minimum(1.0, math.sqrt(2 * (PL + QL)) / (grad_norm + 1e-06))
    new_mats, new_mats_m, new_mats_v = adamw_update(mats, mats_m, mats_v, mats_grad * clip_factor, 0.1, weight_decay)
    new_vecs, new_vecs_m, new_vecs_v = adamw_update(vecs, vecs_m, vecs_v, vecs_grad * clip_factor, 0.5, 0.0)
    head_out = outs.reshape(N_PAIR, N_DP * TOK_DEV, D).astype(jnp.bfloat16)
    token_grad = block_grad.reshape(N_PAIR, N_DP * TOK_DEV, D)
    contrastive = loss_sum / (2 * NDOC)
    return (head_out, token_grad, contrastive, grad_norm, new_mats, new_mats_m, new_mats_v, new_vecs, new_vecs_m, new_vecs_v)
```

```python
import math

import jax
import jax.numpy as jnp
from jax import lax
from jax.experimental import pallas as pl
from jax.experimental.pallas import tpu as pltpu
from jax.sharding import PartitionSpec as P

D = 768
HEADS = 12
HEAD_DIM = 64
FF = 3072
STEP = 10
PL = 7077888
QL = 9216

norm_epsilon = 1e-12
masked_score = -1000000000.0
beta_one = 0.9
beta_two = 0.999
adam_epsilon = 1e-08
weight_decay = 0.01

F32 = jnp.float32
BF16 = jnp.bfloat16
TOK = 256
GRAN = 96
GRANS = PL // D // GRAN
VMEM_BYTES = 63_000_000

V_BQ, V_BV, V_BO, V_G1, V_C1, V_B1, V_B2, V_G2, V_C2 = 0, 1, 2, 3, 4, 5, 9, 10, 11

R_E, R_DF, R_H, R_DA, R_ATT, R_DO, R_U, R_DQ, R_Q, R_DATT, R_WK, R_PU = (
    0, 8, 10, 12, 20, 22, 24, 26, 28, 30, 32, 56,
)
PAY = 80
PAY_A = 48


def nn(a, b):
    return lax.dot_general(a, b, (((1,), (0,)), ((), ())), preferred_element_type=F32)


def nt(a, b):
    return lax.dot_general(a, b, (((1,), (1,)), ((), ())), preferred_element_type=F32)


def tn(a, b):
    return lax.dot_general(a, b, (((0,), (0,)), ((), ())), preferred_element_type=F32)


def iota(shape, axis):
    return lax.broadcasted_iota(jnp.int32, shape, axis)


def erf(x):
    x = jnp.clip(x, -3.832506856900711, 3.832506856900711)
    s = x * x
    top = 0.00022905065861350646
    for c in (0.0034082910107109506, 0.050955695062380861, 0.18520832239976145, 1.128379143519084):
        top = top * s + c
    low = -1.1791602954361697e-7
    for c in (
        0.000023547966471313185,
        0.0010179625278914885,
        0.014070470171167667,
        0.11098505178285362,
        0.49746925110067538,
        1.0,
    ):
        low = low * s + c
    return x * top / low


def gelu_both(a):
    phi = 0.5 + 0.5 * erf(a * math.sqrt(0.5))
    return a * phi, phi + a * jnp.exp(-0.5 * a * a) * (1.0 / math.sqrt(2.0 * math.pi))


def norm_forward(r):
    centred = r - jnp.mean(r, axis=-1, keepdims=True)
    rstd = lax.rsqrt(jnp.mean(centred * centred, axis=-1, keepdims=True) + norm_epsilon)
    return centred * rstd, rstd


def norm_backward(dy, gain, xhat, rstd):
    dx = dy * gain
    return rstd * (
        dx - jnp.mean(dx, axis=-1, keepdims=True) - xhat * jnp.mean(dx * xhat, axis=-1, keepdims=True)
    )


def colsum(v):
    return jnp.sum(v, axis=0, keepdims=True)


def flip(v, axis, bit):
    return lax.ppermute(v, axis, [(i, i ^ bit) for i in range(lax.axis_size(axis))])


def core_flip(v):
    return flip(v, "dp", 1)


def x_flip(v):
    return flip(v, "dp", 2)


def y_flip(v):
    return flip(v, "pair", 1)


def z_up(v):
    n = lax.axis_size("dp")
    return lax.ppermute(v, "dp", [(i, (i + 4) % n) for i in range(n)])


def gather_pieces(own, split):
    out = []
    slot = own
    for k in range(4):
        cut = split[k]
        over_x = x_flip(slot)
        over_y = y_flip(slot)
        out += [slot, over_x, over_y, y_flip(over_x[:cut]), x_flip(over_y[cut:])]
        if k < 3:
            slot = z_up(slot)
    return out + [core_flip(p) for p in out]


def doubled(v, dp, pair):
    for axis, bit, here in (
        ("pair", 1, pair),
        ("dp", 1, dp & 1),
        ("dp", 2, (dp >> 1) & 1),
        ("dp", 4, (dp >> 2) & 1),
        ("dp", 8, (dp >> 3) & 1),
    ):
        r = flip(v, axis, bit)
        v = jnp.where(here == 0, jnp.concatenate([v, r], 0), jnp.concatenate([r, v], 0))
    return v


def summed(v):
    for axis, bit in (("pair", 1), ("dp", 1), ("dp", 2), ("dp", 4), ("dp", 8)):
        v = v + flip(v, axis, bit)
    return v


def add16(a, b):
    return (a.astype(F32) + b.astype(F32)).astype(BF16)


def pick(index, cases):
    return lax.select_n(index, *cases)


def reduce_pieces(mine, theirs, z):
    half = mine[0].shape[1] // 2
    first, second = [None] * 4, [None] * 4
    for t in (3, 2, 1, 0):
        r = core_flip(theirs[t])
        own_a, own_b, x_a, x_b, y_a, y_b, d_a, d_b = [
            add16(mine[t][i, s], r[i, s]) for i in range(4) for s in (slice(0, half), slice(half, None))
        ]
        got_a = y_flip(d_a)
        got_b = x_flip(d_b)
        xb = x_flip(x_b)
        ya = y_flip(y_a)
        xa = x_flip(add16(x_a, got_a))
        yb = y_flip(add16(y_b, got_b))
        first[t] = (own_a.astype(F32) + xa.astype(F32) + ya.astype(F32)).astype(BF16)
        second[t] = (own_b.astype(F32) + xb.astype(F32) + yb.astype(F32)).astype(BF16)
    done = []
    for part in (first, second):
        moving = z_up(pick((z + 3) & 3, part))
        moving = z_up(add16(pick((z + 2) & 3, part), moving))
        moving = z_up(add16(pick((z + 1) & 3, part), moving))
        done += [pick(z, part), moving]
    return done


def by_kind(granule, emit):
    joint = granule < 24
    wide = (granule >= 32) & (granule < 64)
    pl.when(joint)(lambda: emit(3))
    pl.when(wide)(lambda: emit(4))
    pl.when(jnp.logical_not(joint | wide))(lambda: emit(1))


def pack_kernel(info, flat, out0, out1):
    for gi in range(3):

        def emit(n, gi=gi):
            m = GRAN // n
            for layer, out in enumerate((out0, out1)):
                for j in range(6):
                    parts = [
                        flat[pl.ds(12 * (GRAN * gi + p) + 2 * j + layer, m, stride=12 * n), :] for p in range(n)
                    ]
                    tile = parts[0] if n == 1 else jnp.concatenate(parts, 0)
                    out[gi, :, 128 * j : 128 * (j + 1)] = tile.astype(BF16)

        by_kind(3 * info[0] + gi, emit)


def piece_places(info):
    z, x, c, y = info[1], info[2], info[3], info[4]
    places = []
    for other in (0, 1):
        for k in range(4):
            cut = SPLIT[k]
            for dx, dy, lo, hi in ((0, 0, 0, 3), (1, 0, 0, 3), (0, 1, 0, 3), (1, 1, 0, cut), (1, 1, cut, 3)):
                dev = (
                    8 * ((z + 4 - k) & 3)
                    + 4 * jnp.bitwise_xor(x, dx)
                    + 2 * jnp.bitwise_xor(c, other)
                    + jnp.bitwise_xor(y, dy)
                )
                places.append((3 * dev + lo, hi - lo))
    return places


SPLIT = (1, 2, 1, 2)


def fill(info, pieces, wbuf, sem):
    copies = [
        pltpu.make_async_copy(piece, wbuf.at[pl.ds(start, n)], sem.at[i])
        for i, (piece, (start, n)) in enumerate(zip(pieces, piece_places(info)))
    ]
    for c in copies:
        c.start()
    return copies


def split_w1(wbuf, w1):
    def step(i, carry):
        rows = wbuf[pl.ds(32 + 4 * i, 4)].astype(F32)
        for j in range(4):
            part = rows[:, 24 * j : 24 * (j + 1), :].reshape(GRAN, D).astype(BF16)
            w1[j, pl.ds(pl.multiple_of(GRAN * i, GRAN), GRAN), :] = part
        return carry

    lax.fori_loop(0, 8, step, 0)


def w_in(wbuf, j):
    return wbuf[0:24, 32 * j : 32 * (j + 1), :].reshape(D, D)


def w_out(wbuf):
    return wbuf[24:32].reshape(D, D)


def w_shrink(wbuf, j):
    return wbuf[64 + 8 * j : 72 + 8 * j].reshape(D, D)


def expander():
    r, c = iota((32, 16), 0), iota((32, 16), 1)
    return ((r < 24) & ((r & 1) == c)).astype(BF16)


def head_mask():
    r, lane = iota((32, D), 0), iota((32, D), 1)
    return (r < 24) & ((r >> 1) == (lane >> 6))


def spread(expand, mask, rows):
    return jnp.where(mask, nn(expand, rows), 0.0).astype(BF16)


def first_forward(
    info, u_ref, vec, *refs
):
    pieces = refs[:40]
    y_out, xh1_o, rs1_o, xh2_o, rs2_o, gp_o, e_o, h_o, att_o, u_o, q_o, pu_o, qk_o, p_o, wbuf, w1, sem = refs[40:]
    copies = fill(info, pieces, wbuf, sem)
    start = info[5]
    u = u_ref[...]
    r, t = iota((16, TOK), 0), iota((16, TOK), 1)
    picker = (((r == 0) & (t == 0)) | ((r == 1) & (t == start))).astype(BF16)
    cls = nn(picker, u)
    cls16 = cls.astype(BF16)
    expand, mask = expander(), head_mask()
    r, t = iota((32, TOK), 0), iota((32, TOK), 1)
    inside = (t >= start).astype(jnp.int32) == (r & 1)
    real = r < 24
    for c in copies:
        c.wait()
    split_w1(wbuf, w1)
    q = (nn(cls16, w_in(wbuf, 0)) + vec[V_BQ : V_BQ + 1, :]).astype(BF16)
    qk = nt(spread(expand, mask, q), w_in(wbuf, 1)).astype(BF16)
    scores = jnp.where(inside, nt(qk, u) * HEAD_DIM**-0.5, masked_score)
    raised = jnp.exp(scores - jnp.max(scores, axis=-1, keepdims=True))
    portions = jnp.where(real, raised / jnp.sum(raised, axis=-1, keepdims=True), 0.0)
    low = portions.astype(BF16)
    pu = nn(low, u).astype(BF16)
    weight = jnp.sum(low.astype(F32), axis=-1, keepdims=True)
    heads = nn(pu, w_in(wbuf, 2)) + weight * vec[V_BV : V_BV + 1, :]
    att = tn(expand, jnp.where(mask, heads, 0.0).astype(BF16)).astype(BF16)
    xhat, rstd = norm_forward(cls + nn(att, w_out(wbuf)) + vec[V_BO : V_BO + 1, :])
    xh1_o[...] = xhat
    rs1_o[...] = jnp.broadcast_to(rstd, (16, 128))
    h = xhat * vec[V_G1 : V_G1 + 1, :] + vec[V_C1 : V_C1 + 1, :]
    h16 = h.astype(BF16)
    f = vec[V_B2 : V_B2 + 1, :]
    for j in range(4):
        e, gp = gelu_both(nn(h16, w1[j]) + vec[V_B1 + j : V_B1 + j + 1, :])
        e = e.astype(BF16)
        e_o[j] = e
        gp_o[j] = gp
        f = f + nn(e, w_shrink(wbuf, j))
    xhat, rstd = norm_forward(h + f)
    xh2_o[...] = xhat
    rs2_o[...] = jnp.broadcast_to(rstd, (16, 128))
    y_out[...] = xhat * vec[V_G2 : V_G2 + 1, :] + vec[V_C2 : V_C2 + 1, :]
    h_o[...] = h16
    att_o[...] = att
    u_o[...] = cls16
    q_o[...] = q
    pu_o[...] = pu
    qk_o[...] = qk
    p_o[...] = portions


def first_backward(
    info, u_ref, vec, cls_all, dz, xh1, rs1, xh2, rs2, gp_i, e_i, h_i, att_i, ucls, q_i, pu_i, qk_i, p_i, *refs
):
    pieces = refs[:40]
    tg_out, pay_out, vg_out, loss_out, wbuf, w1, rows16, dcls, pay, sem = refs[40:]
    copies = fill(info, pieces, wbuf, sem)
    start = info[5]
    u = u_ref[...]
    keys = cls_all[...]
    n_keys = keys.shape[0]
    scale = 2.0 / math.sqrt(D)
    r, c = iota((n_keys, n_keys), 0), iota((n_keys, n_keys), 1)
    scores = jnp.where(r == c, masked_score, nt(keys, keys) * scale)
    top = jnp.max(scores, axis=-1, keepdims=True)
    raised = jnp.exp(scores - top)
    total = jnp.sum(raised, axis=-1, keepdims=True)
    partner = jnp.bitwise_xor(r, 2) == c
    positive = jnp.sum(jnp.where(partner, scores, 0.0), axis=-1, keepdims=True)
    terms = top + jnp.log(total) - positive
    loss_out[...] = jnp.broadcast_to(colsum(terms) * (1.0 / n_keys), (8, 128))
    pull = (raised / total - partner.astype(F32)).astype(BF16)
    dcls[...] = (nn(pull, keys) + tn(pull, keys)) * scale
    rows16[...] = jnp.zeros((16, D), F32)
    rows16[0:1, :] = dz[0:1, :] + dcls[pl.ds(2 * info[0], 1), :]
    rows16[1:2, :] = dz[pl.ds(start, 1), :] + dcls[pl.ds(2 * info[0] + 1, 1), :]
    dy = rows16[...]
    for copy in copies:
        copy.wait()
    split_w1(wbuf, w1)
    vg_out[...] = jnp.zeros((16, D), F32)
    xhat = xh2[...]
    vg_out[V_G2 : V_G2 + 1, :] = colsum(dy * xhat)
    vg_out[V_C2 : V_C2 + 1, :] = colsum(dy)
    dr2 = norm_backward(dy, vec[V_G2 : V_G2 + 1, :], xhat, rs2[:, 0:1])
    df = dr2.astype(BF16)
    pay[R_DF : R_DF + 2, :] = df.astype(F32)[0:2, :]
    vg_out[V_B2 : V_B2 + 1, :] = colsum(df.astype(F32))
    dh = dr2
    for j in range(4):
        da = (gp_i[j] * nt(df, w_shrink(wbuf, j))).astype(BF16)
        pay[R_E + 2 * j : R_E + 2 * j + 2, :] = e_i[j].astype(F32)[0:2, :]
        pay[R_DA + 2 * j : R_DA + 2 * j + 2, :] = da.astype(F32)[0:2, :]
        vg_out[V_B1 + j : V_B1 + j + 1, :] = colsum(da.astype(F32))
        dh = dh + nt(da, w1[j])
    xhat = xh1[...]
    vg_out[V_G1 : V_G1 + 1, :] = colsum(dh * xhat)
    vg_out[V_C1 : V_C1 + 1, :] = colsum(dh)
    dr1 = norm_backward(dh, vec[V_G1 : V_G1 + 1, :], xhat, rs1[:, 0:1])
    do = dr1.astype(BF16)
    vg_out[V_BO : V_BO + 1, :] = colsum(do.astype(F32))
    datt = nt(do, w_out(wbuf)).astype(BF16)
    expand, mask = expander(), head_mask()
    portions = p_i[...]
    low = portions.astype(BF16)
    each = spread(expand, mask, datt)
    dvk = nt(each, w_in(wbuf, 2)).astype(BF16)
    constant = jnp.sum(each.astype(F32) * vec[V_BV : V_BV + 1, :], axis=-1, keepdims=True)
    dp = nt(dvk, u) + constant
    ds = (portions * (dp - jnp.sum(dp * portions, axis=-1, keepdims=True))).astype(BF16)
    dsu = nn(ds, u)
    weight = jnp.sum(low.astype(F32), axis=-1, keepdims=True)
    vg_out[V_BV : V_BV + 1, :] = colsum(each.astype(F32) * weight)
    part = jnp.where(mask, nn(dsu.astype(BF16), w_in(wbuf, 1)) * HEAD_DIM**-0.5, 0.0).astype(BF16)
    dq = tn(expand, part).astype(BF16)
    vg_out[V_BQ : V_BQ + 1, :] = colsum(dq.astype(F32))
    rows16[...] = dr1 + nt(dq, w_in(wbuf, 0))
    du = tn(ds, qk_i[...]) * HEAD_DIM**-0.5 + tn(low, dvk)
    is_cls = (iota((TOK, 1), 0) == 0) | (iota((TOK, 1), 0) == start)
    tg_out[...] = du + jnp.where(is_cls, 0.0, dz[...])
    tg_out[0:1, :] = tg_out[0:1, :] + rows16[0:1, :]
    tg_out[pl.ds(start, 1), :] = tg_out[pl.ds(start, 1), :] + rows16[1:2, :]
    for row, rows in ((R_H, h_i), (R_ATT, att_i), (R_U, ucls), (R_Q, q_i)):
        pay[row : row + 2, :] = rows[...].astype(F32)[0:2, :]
    for row, rows in ((R_DO, do), (R_DQ, dq), (R_DATT, datt)):
        pay[row : row + 2, :] = rows.astype(F32)[0:2, :]
    pay[R_WK : R_WK + 24, :] = dsu[0:24, :] * HEAD_DIM**-0.5
    pay[R_PU : R_PU + 24, :] = pu_i[...].astype(F32)[0:24, :]
    pay_out[...] = pay[...].astype(BF16)


def second_block(info, u_ref, cot_ref, y_ref, vec, *refs):
    pieces = refs[:40]
    head_out, dz_out, vg_out = refs[40:43]
    outs = refs[43:51]
    (wbuf, w1, gbuf, zf, zb, qs, ks, vs, pm, att, xh1, hb, ht, gp, es, das, xh2, acc, stage, dqs, dks, dvs, sem, osem) = refs[51:]
    copies = fill(info, pieces, wbuf, sem)
    start = info[5]
    zf[...] = u_ref[...].astype(F32)
    zf[0:1, :] = y_ref[0:1, :]
    zf[pl.ds(start, 1), :] = y_ref[1:2, :]
    z16 = zf[...].astype(BF16)
    zb[...] = z16
    for c in copies:
        c.wait()
    split_w1(wbuf, w1)
    qs[...] = (nn(z16, w_in(wbuf, 0)) + vec[V_BQ : V_BQ + 1, :]).astype(BF16)
    ks[...] = nn(z16, w_in(wbuf, 1)).astype(BF16)
    vs[...] = (nn(z16, w_in(wbuf, 2)) + vec[V_BV : V_BV + 1, :]).astype(BF16)
    low_lane = iota((TOK, 128), 1) < HEAD_DIM
    same = (iota((TOK, TOK), 0) >= start) == (iota((TOK, TOK), 1) >= start)

    def lanes(p):
        return pl.ds(pl.multiple_of(128 * p, 128), 128)

    def attend(p, carry):
        qp, kp, vp = qs[:, lanes(p)], ks[:, lanes(p)], vs[:, lanes(p)]
        res = []
        for hh in range(2):
            qm = jnp.where(low_lane == (hh == 0), qp, jnp.zeros_like(qp))
            s = jnp.where(same, nt(qm, kp) * HEAD_DIM**-0.5, masked_score)
            raised = jnp.exp(s - jnp.max(s, axis=-1, keepdims=True))
            portions = raised / jnp.sum(raised, axis=-1, keepdims=True)
            pm[2 * p + hh] = portions
            res.append(nn(portions.astype(BF16), vp))
        att[:, lanes(p)] = jnp.where(low_lane, res[0], res[1]).astype(BF16)
        return carry

    lax.fori_loop(0, 6, attend, 0)
    xhat, rstd1 = norm_forward(zf[...] + (nn(att[...], w_out(wbuf)) + vec[V_BO : V_BO + 1, :]))
    xh1[...] = xhat
    h = xhat * vec[V_G1 : V_G1 + 1, :] + vec[V_C1 : V_C1 + 1, :]
    hb[...] = h.astype(BF16)
    ht[...] = h.T.astype(BF16)
    acc[...] = h + vec[V_B2 : V_B2 + 1, :]
    for j in range(4):
        e, slope = gelu_both(nn(hb[...], w1[j]) + vec[V_B1 + j : V_B1 + j + 1, :])
        gp[j] = slope
        e = e.astype(BF16)
        es[j] = e
        acc[...] += nn(e, w_shrink(wbuf, j))
    xhat, rstd2 = norm_forward(acc[...])
    xh2[...] = xhat
    head_out[...] = (xhat * vec[V_G2 : V_G2 + 1, :] + vec[V_C2 : V_C2 + 1, :]).astype(BF16)

    vg_out[...] = jnp.zeros((16, D), F32)
    dy = cot_ref[...].astype(F32)
    vg_out[V_G2 : V_G2 + 1, :] = colsum(dy * xh2[...])
    vg_out[V_C2 : V_C2 + 1, :] = colsum(dy)
    dr = norm_backward(dy, vec[V_G2 : V_G2 + 1, :], xh2[...], rstd2)
    acc[...] = dr
    df = dr.astype(BF16)
    dqs[...] = df
    vg_out[V_B2 : V_B2 + 1, :] = colsum(df.astype(F32))
    for j in range(4):
        df = dqs[...]
        gbuf[64 + 8 * j : 72 + 8 * j] = tn(es[j], df).astype(BF16).reshape(8, GRAN, D)
        da = (gp[j] * nt(df, w_shrink(wbuf, j))).astype(BF16)
        das[j] = da
        vg_out[V_B1 + j : V_B1 + j + 1, :] = colsum(da.astype(F32))
        acc[...] += nt(da, w1[j])

    def expand_grad(i, carry):
        rows = ht[pl.ds(pl.multiple_of(192 * i, 192), 192), :]
        for j in range(4):
            stage[:, 24 * j : 24 * (j + 1), :] = nn(rows, das[j]).reshape(8, 24, D)
        gbuf[pl.ds(32 + 8 * i, 8)] = stage[...].astype(BF16)
        return carry

    lax.fori_loop(0, 4, expand_grad, 0)
    dh = acc[...]
    vg_out[V_G1 : V_G1 + 1, :] = colsum(dh * xh1[...])
    vg_out[V_C1 : V_C1 + 1, :] = colsum(dh)
    dr = norm_backward(dh, vec[V_G1 : V_G1 + 1, :], xh1[...], rstd1)
    acc[...] = dr
    do = dr.astype(BF16)
    vg_out[V_BO : V_BO + 1, :] = colsum(do.astype(F32))
    gbuf[24:32] = tn(att[...], do).astype(BF16).reshape(8, GRAN, D)
    att[...] = nt(do, w_out(wbuf)).astype(BF16)

    def attend_back(p, carry):
        qp, kp, vp, dp_ = qs[:, lanes(p)], ks[:, lanes(p)], vs[:, lanes(p)], att[:, lanes(p)]
        dq, dk, dv = [], [], []
        for hh in range(2):
            portions = pm[2 * p + hh]
            dam = jnp.where(low_lane == (hh == 0), dp_, jnp.zeros_like(dp_))
            dp = nt(dam, vp)
            dv.append(tn(portions.astype(BF16), dp_))
            ds = (portions * (dp - jnp.sum(dp * portions, axis=-1, keepdims=True))).astype(BF16)
            dq.append(nn(ds, kp))
            dk.append(tn(ds, qp))
        dqs[:, lanes(p)] = (jnp.where(low_lane, dq[0], dq[1]) * HEAD_DIM**-0.5).astype(BF16)
        dks[:, lanes(p)] = (jnp.where(low_lane, dk[0], dk[1]) * HEAD_DIM**-0.5).astype(BF16)
        dvs[:, lanes(p)] = jnp.where(low_lane, dv[0], dv[1]).astype(BF16)
        return carry

    lax.fori_loop(0, 6, attend_back, 0)
    vg_out[V_BQ : V_BQ + 1, :] = colsum(dqs[...].astype(F32))
    vg_out[V_BV : V_BV + 1, :] = colsum(dvs[...].astype(F32))
    for j, part in enumerate((dqs, dks, dvs)):
        gbuf[0:24, 32 * j : 32 * (j + 1), :] = tn(zb[...], part[...]).astype(BF16).reshape(24, 32, D)
        acc[...] += nt(part[...], w_in(wbuf, j))
    dz_out[...] = acc[...]
    x, c, y = info[2], info[3], info[4]
    sends = []
    for t in (3, 2, 1, 0):
        for other in (1, 0):
            for rel in range(4):
                dev = (
                    8 * t
                    + 4 * jnp.bitwise_xor(x, rel & 1)
                    + 2 * jnp.bitwise_xor(c, other)
                    + jnp.bitwise_xor(y, rel >> 1)
                )
                i = 4 * other + t
                copy = pltpu.make_async_copy(gbuf.at[pl.ds(3 * dev, 3)], outs[i].at[rel], osem.at[4 * i + rel])
                copy.start()
                sends.append(copy)
    for copy in sends:
        copy.wait()


def owner_grad(info, *refs):
    pieces = refs[:40]
    out, pbuf, pf, sem = refs[40:]
    copies = []
    n = 0
    for other in range(2):
        for k in range(4):
            for slot, lo, hi in ((0, 0, PAY), (1, 0, PAY), (2, 0, PAY), (3, 0, PAY_A), (3, PAY_A, PAY)):
                dst = pbuf.at[16 * other + 4 * k + slot, pl.ds(lo, hi - lo)]
                copies.append(pltpu.make_async_copy(pieces[n], dst, sem.at[n]))
                n += 1
    for c in copies:
        c.start()
    for c in copies:
        c.wait()

    def widen(i, carry):
        for j in range(6):
            pf[j, pl.ds(pl.multiple_of(PAY * i, PAY), PAY), :] = pbuf[i, :, 128 * j : 128 * (j + 1)].astype(F32)
        return carry

    lax.fori_loop(0, 32, widen, 0)

    def rows(first):
        return jnp.concatenate(
            [
                jnp.concatenate(
                    [pf[j, pl.ds(first + s, 32, stride=PAY), :] for j in range(6)], axis=1
                )
                for s in range(2)
            ],
            axis=0,
        ).astype(BF16)

    def chosen(count, offset, source):
        one_hot = (iota((count, D), 1) == iota((count, D), 0) + offset).astype(BF16)
        return nt(one_hot, source).astype(BF16)

    def put(gi, n, p, value):
        m = GRAN // n
        for j in range(6):
            out[pl.ds(6 * (GRAN * gi + p) + j, m, stride=6 * n), :] = value[:, 128 * j : 128 * (j + 1)]

    for gi in range(3):
        g = 3 * info[0] + gi

        @pl.when(g < 24)
        def _(gi=gi, g=g):
            off = 32 * g
            put(gi, 3, 0, nn(chosen(32, off, rows(R_U)), rows(R_DQ)))
            lane = iota((64, D), 1) >> 6
            for p, left, right in ((1, R_WK, R_Q), (2, R_PU, R_DATT)):
                base = rows(right)
                total = jnp.zeros((32, D), F32)
                for h in range(HEADS):
                    masked = jnp.where(lane == h, base, jnp.zeros_like(base))
                    total = total + nn(chosen(32, off, rows(left + 2 * h)), masked)
                put(gi, 3, p, total)

        @pl.when((g >= 24) & (g < 32))
        def _(gi=gi, g=g):
            put(gi, 1, 0, nn(chosen(GRAN, GRAN * (g - 24), rows(R_ATT)), rows(R_DO)))

        @pl.when((g >= 32) & (g < 64))
        def _(gi=gi, g=g):
            left = chosen(24, 24 * (g - 32), rows(R_H))
            for p in range(4):
                put(gi, 4, p, nn(left, rows(R_DA + 2 * p)))

        @pl.when(g >= 64)
        def _(gi=gi, g=g):
            part = (g - 64) >> 3
            put(gi, 1, 0, nn(chosen(GRAN, GRAN * ((g - 64) & 7), rows(R_E + 2 * part)), rows(R_DF)))


def join_grads(info, g0, a1, a2, b1, b2, out, square, buf):
    g = g0[...]
    out[pl.ds(0, 1728, stride=2), :] = g
    buf[0:144, :] = a1[...].astype(F32) + a2[...].astype(F32)
    buf[144:288, :] = b1[...].astype(F32) + b2[...].astype(F32)
    total = buf[...]
    sq = jnp.sum((g * g).reshape(216, 8, 128), axis=0)
    for j in range(6):
        v = total[:, 128 * j : 128 * (j + 1)]
        sq = sq + jnp.sum((v * v).reshape(36, 8, 128), axis=0)
    square[...] = sq
    for gi in range(3):

        def emit(n, gi=gi):
            m = GRAN // n
            for p in range(n):
                for j in range(6):
                    out[pl.ds(12 * (GRAN * gi + p) + 2 * j + 1, m, stride=12 * n), :] = buf[
                        GRAN * gi + m * p : GRAN * gi + m * (p + 1), 128 * j : 128 * (j + 1)
                    ]

        by_kind(3 * info[0] + gi, emit)


def adamw_kernel(coef, w, m, v, g, w_out_, m_out, v_out):
    new = adamw_update(w[...], m[...], v[...], g[...] * coef[0], 0.1, weight_decay)
    w_out_[...], m_out[...], v_out[...] = new


def adamw_update(weight, moment_one, moment_two, gradient, step_rate, decay_rate):
    first_new = beta_one * moment_one + (1.0 - beta_one) * gradient
    second_new = beta_two * moment_two + (1.0 - beta_two) * gradient * gradient
    first_hat = first_new / (1.0 - beta_one**STEP)
    second_hat = second_new / (1.0 - beta_two**STEP)
    weight_new = weight - step_rate * (first_hat / (jnp.sqrt(second_hat) + adam_epsilon) + decay_rate * weight)
    return (weight_new, first_new, second_new)


SMEM = pl.BlockSpec(memory_space=pltpu.SMEM)
VMEM = pl.BlockSpec(memory_space=pltpu.VMEM)
ANY = pl.BlockSpec(memory_space=pl.ANY)


def struct(*shape, dtype=F32):
    return jax.ShapeDtypeStruct(shape, dtype)


def call(kernel, name, ins, in_specs, outs, out_specs, scratch=(), flops=0, moved=0):
    return pl.pallas_call(
        kernel,
        out_shape=outs,
        in_specs=in_specs,
        out_specs=out_specs,
        scratch_shapes=list(scratch),
        name=name,
        compiler_params=pltpu.CompilerParams(vmem_limit_bytes=VMEM_BYTES),
        cost_estimate=pl.CostEstimate(flops=flops, bytes_accessed=moved, transcendentals=0),
    )(*ins)


def flat_view(a):
    return a.reshape(2, -1, 128).transpose(1, 0, 2).reshape(-1, 128)


def flat_back(a):
    return a.reshape(-1, 2, 128).transpose(1, 0, 2).reshape(2, -1)


def body(tokens, cotangent, lengths, mats, mats_m, mats_v, vecs, vecs_m, vecs_v):
    dp, pair = lax.axis_index("dp"), lax.axis_index("pair")
    device = 2 * dp + pair
    z = dp >> 2
    info = jnp.stack(
        [device, z, (dp >> 1) & 1, dp & 1, pair, lengths[0, 0, 0], jnp.int32(0), jnp.int32(0)]
    ).astype(jnp.int32)
    u = tokens[0]
    cot = cotangent[0]
    shard = struct(3, GRAN, D, dtype=BF16)
    flat = flat_view(mats)
    own0, own1 = call(pack_kernel, "pack", (info, flat), [SMEM, VMEM], (shard, shard), (VMEM, VMEM))
    pieces0 = gather_pieces(own0, SPLIT)
    every_vec = doubled(vecs.astype(BF16).reshape(1, -1), dp, pair)
    every_vec = every_vec.reshape(32, 2, -1).transpose(1, 0, 2).reshape(2, 12, D).astype(F32)
    every_vec = jnp.pad(every_vec, ((0, 0), (0, 4), (0, 0)))
    vec0, vec1 = every_vec[0], every_vec[1]
    row = struct(16, D)
    row16 = struct(16, D, dtype=BF16)
    saved_shapes = (
        row, struct(16, 128), row, struct(16, 128), struct(4, 16, D), struct(4, 16, D, dtype=BF16),
        row16, row16, row16, row16, struct(32, D, dtype=BF16), struct(32, D, dtype=BF16), struct(32, TOK),
    )
    weights = [
        pltpu.VMEM((GRANS, GRAN, D), BF16),
        pltpu.VMEM((4, D, D), BF16),
    ]
    y_cls, *saved = call(
        first_forward,
        "first_forward",
        (info, u, vec0, *pieces0),
        [SMEM, VMEM, VMEM] + [ANY] * 40,
        (row, *saved_shapes),
        (VMEM,) * 14,
        weights + [pltpu.SemaphoreType.DMA((40,))],
        flops=2 * 32 * PL,
        moved=2 * PL,
    )
    every_cls = doubled(y_cls[0:2].astype(BF16), dp, pair)
    pieces1 = gather_pieces(own1, SPLIT)
    part = struct(4, 3, GRAN, D, dtype=BF16)
    mid16 = pltpu.VMEM((TOK, D), BF16)
    mid = pltpu.VMEM((TOK, D), F32)
    head_out, dz, vg1, *terms = call(
        second_block,
        "second_block",
        (info, u, cot, y_cls, vec1, *pieces1),
        [SMEM, VMEM, VMEM, VMEM, VMEM] + [ANY] * 40,
        (struct(TOK, D, dtype=BF16), struct(TOK, D), row) + (part,) * 8,
        (VMEM, VMEM, VMEM) + (ANY,) * 8,
        weights
        + [
            pltpu.VMEM((GRANS, GRAN, D), BF16),
            mid, mid16, mid16, mid16, mid16,
            pltpu.VMEM((HEADS, TOK, TOK), F32),
            mid16, mid, mid16,
            pltpu.VMEM((D, TOK), BF16),
            pltpu.VMEM((4, TOK, D), F32),
            pltpu.VMEM((4, TOK, D), BF16),
            pltpu.VMEM((4, TOK, D), BF16),
            mid, mid,
            pltpu.VMEM((8, GRAN, D), F32),
            mid16, mid16, mid16,
            pltpu.SemaphoreType.DMA((40,)),
            pltpu.SemaphoreType.DMA((32,)),
        ],
        flops=6 * TOK * PL,
        moved=4 * PL,
    )
    terms = [t.reshape(4, 288, D) for t in terms]
    a1, a2, b1, b2 = reduce_pieces(terms[:4], terms[4:], z)
    token_grad, payload, vg0, loss = call(
        first_backward,
        "first_backward",
        (info, u, vec0, every_cls, dz, *saved, *pieces0),
        [SMEM] + [VMEM] * 17 + [ANY] * 40,
        (struct(TOK, D), struct(PAY, D, dtype=BF16), row, struct(8, 128)),
        (VMEM,) * 4,
        weights
        + [
            pltpu.VMEM((16, D), F32),
            pltpu.VMEM((64, D), F32),
            pltpu.VMEM((PAY, D), F32),
            pltpu.SemaphoreType.DMA((40,)),
        ],
        flops=2 * 32 * PL,
        moved=2 * PL,
    )
    flat0 = call(
        owner_grad,
        "owner_grad",
        (info, *gather_pieces(payload, (PAY_A,) * 4)),
        [SMEM] + [ANY] * 40,
        struct(1728, 128),
        VMEM,
        [
            pltpu.VMEM((32, PAY, D), BF16),
            pltpu.VMEM((6, 32 * PAY, 128), F32),
            pltpu.SemaphoreType.DMA((40,)),
        ],
        flops=2 * 768 * 768 * 768,
        moved=2 * 32 * PAY * D,
    )
    vec_sum = summed(jnp.concatenate([vg0[:12], vg1[:12]], 0)).reshape(2, QL)
    grad_vecs = lax.dynamic_slice(vec_sum, (0, device * vecs.shape[1]), vecs.shape)
    grads, square = call(
        join_grads,
        "join_grads",
        (info, flat0, a1, a2, b1, b2),
        [SMEM] + [VMEM] * 5,
        (struct(3456, 128), struct(8, 128)),
        (VMEM, VMEM),
        [pltpu.VMEM((288, D), F32)],
    )
    square_sum = jnp.sum(square) + jnp.sum(grad_vecs * grad_vecs)
    total_sq = summed(jnp.broadcast_to(square_sum, (8, 128)))[0, 0]
    grad_norm = jnp.sqrt(total_sq)
    clip_factor = jnp.minimum(1.0, math.sqrt(2 * (PL + QL)) / (grad_norm + 1e-06))
    block = pl.BlockSpec((432, 128), lambda i: (i, 0))
    new = pl.pallas_call(
        adamw_kernel,
        grid=(8,),
        in_specs=[SMEM] + [block] * 4,
        out_specs=(block,) * 3,
        out_shape=(struct(3456, 128),) * 3,
        name="adamw",
    )(clip_factor.reshape(1), flat, flat_view(mats_m), flat_view(mats_v), grads)
    new_mats, new_mats_m, new_mats_v = [flat_back(a) for a in new]
    new_vecs, new_vecs_m, new_vecs_v = adamw_update(vecs, vecs_m, vecs_v, grad_vecs * clip_factor, 0.5, 0.0)
    return (
        head_out[None],
        token_grad[None],
        loss[0, 0],
        grad_norm,
        new_mats,
        new_mats_m,
        new_mats_v,
        new_vecs,
        new_vecs_m,
        new_vecs_v,
    )


def matmul(left_side, right_side):
    return jnp.dot(left_side, right_side, preferred_element_type=jnp.float32)


def inner_rows(left_side, right_side):
    return lax.dot_general(
        left_side, right_side, (((0,), (0,)), ((), ())), preferred_element_type=jnp.float32
    )


def outer_cols(left_side, right_side):
    return lax.dot_general(
        left_side, right_side, (((1,), (1,)), ((), ())), preferred_element_type=jnp.float32
    )


def exact_dot(left_side, right_side):
    return jnp.dot(
        left_side, right_side, precision=lax.Precision.HIGHEST, preferred_element_type=jnp.float32
    )


def layer_norm(resid, gain, shift):
    centred = resid - jnp.mean(resid, axis=-1, keepdims=True)
    spread = jnp.mean(centred * centred, axis=-1, keepdims=True)
    return centred * lax.rsqrt(spread + norm_epsilon) * gain + shift


def gelu_exact(before):
    return jax.nn.gelu(before, approximate=False)


def unpack(mat_row, vec_row):
    edge_one = 3 * D * D
    edge_two = 4 * D * D
    edge_three = edge_two + D * FF
    input_weight = mat_row[:edge_one].reshape(D, 3 * D)
    output_weight = mat_row[edge_one:edge_two].reshape(D, D)
    expand_weight = mat_row[edge_two:edge_three].reshape(D, FF)
    shrink_weight = mat_row[edge_three:].reshape(FF, D)
    vector = vec_row.astype(jnp.float32)
    pieces = []
    cursor = 0
    for piece_len in (D, D, D, D, D, FF, D, D, D):
        pieces.append(vector[cursor : cursor + piece_len])
        cursor = cursor + piece_len
    return (input_weight, output_weight, expand_weight, shrink_weight) + tuple(pieces)


def head_scores(queries, key_rows, same_span):
    row_count = queries.shape[0]
    query_heads = queries.reshape(row_count, HEADS, HEAD_DIM)
    key_heads = key_rows.reshape(row_count, HEADS, HEAD_DIM)
    scores = jnp.einsum(
        "thd,shd->hts", query_heads, key_heads, preferred_element_type=jnp.float32
    ) * HEAD_DIM ** (-0.5)
    return jnp.where(same_span[None, :, :], scores, masked_score)


def layer_forward(params, inputs, same_span):
    (
        input_weight,
        output_weight,
        expand_weight,
        shrink_weight,
        query_bias,
        value_bias,
        output_bias,
        first_gain,
        first_shift,
        expand_bias,
        shrink_bias,
        second_gain,
        second_shift,
    ) = params
    row_count = inputs.shape[0]
    low_input = inputs.astype(jnp.bfloat16)
    joint = matmul(low_input, input_weight)
    queries = (joint[:, :D] + query_bias).astype(jnp.bfloat16)
    key_rows = joint[:, D : 2 * D].astype(jnp.bfloat16)
    values = (joint[:, 2 * D :] + value_bias).astype(jnp.bfloat16)
    scores = head_scores(queries, key_rows, same_span)
    row_max = jnp.max(scores, axis=-1, keepdims=True)
    raised = jnp.exp(scores - row_max)
    summed = jnp.sum(raised, axis=-1, keepdims=True)
    portions = raised / summed
    logsum = row_max + jnp.log(summed)
    value_heads = values.reshape(row_count, HEADS, HEAD_DIM)
    attended = jnp.einsum(
        "hts,shd->thd",
        portions.astype(jnp.bfloat16),
        value_heads,
        preferred_element_type=jnp.float32,
    )
    attended = attended.reshape(row_count, D).astype(jnp.bfloat16)
    resid_one = inputs + (matmul(attended, output_weight) + output_bias)
    hidden = layer_norm(resid_one, first_gain, first_shift)
    low_hidden = hidden.astype(jnp.bfloat16)
    before = matmul(low_hidden, expand_weight) + expand_bias
    activated = gelu_exact(before).astype(jnp.bfloat16)
    resid_two = hidden + (matmul(activated, shrink_weight) + shrink_bias)
    output = layer_norm(resid_two, second_gain, second_shift)
    kept = (
        low_input,
        queries,
        key_rows,
        values,
        logsum,
        attended,
        resid_one,
        low_hidden,
        before,
        activated,
        resid_two,
    )
    return (output, kept)


def layer_backward(params, kept, grad_out, same_span):
    (
        input_weight,
        output_weight,
        expand_weight,
        shrink_weight,
        query_bias,
        value_bias,
        output_bias,
        first_gain,
        first_shift,
        expand_bias,
        shrink_bias,
        second_gain,
        second_shift,
    ) = params
    (
        low_input,
        queries,
        key_rows,
        values,
        logsum,
        attended,
        resid_one,
        low_hidden,
        before,
        activated,
        resid_two,
    ) = kept
    row_count = low_input.shape[0]
    _, norm_pull_two = jax.vjp(layer_norm, resid_two, second_gain, second_shift)
    d_resid_two, d_second_gain, d_second_shift = norm_pull_two(grad_out)
    d_feed = d_resid_two.astype(jnp.bfloat16)
    d_shrink = inner_rows(activated, d_feed)
    d_shrink_bias = jnp.sum(d_feed.astype(jnp.float32), axis=0)
    _, gelu_pull = jax.vjp(gelu_exact, before)
    d_before = gelu_pull(outer_cols(d_feed, shrink_weight))[0].astype(jnp.bfloat16)
    d_expand = inner_rows(low_hidden, d_before)
    d_expand_bias = jnp.sum(d_before.astype(jnp.float32), axis=0)
    d_hidden = d_resid_two + outer_cols(d_before, expand_weight)
    _, norm_pull_one = jax.vjp(layer_norm, resid_one, first_gain, first_shift)
    d_resid_one, d_first_gain, d_first_shift = norm_pull_one(d_hidden)
    d_branch = d_resid_one.astype(jnp.bfloat16)
    d_output = inner_rows(attended, d_branch)
    d_output_bias = jnp.sum(d_branch.astype(jnp.float32), axis=0)
    d_attended = outer_cols(d_branch, output_weight).astype(jnp.bfloat16)
    portions = jnp.exp(head_scores(queries, key_rows, same_span) - logsum)
    query_heads = queries.reshape(row_count, HEADS, HEAD_DIM)
    key_heads = key_rows.reshape(row_count, HEADS, HEAD_DIM)
    value_heads = values.reshape(row_count, HEADS, HEAD_DIM)
    d_att_heads = d_attended.reshape(row_count, HEADS, HEAD_DIM)
    d_portions = jnp.einsum(
        "thd,shd->hts", d_att_heads, value_heads, preferred_element_type=jnp.float32
    )
    d_values = jnp.einsum(
        "hts,thd->shd",
        portions.astype(jnp.bfloat16),
        d_att_heads,
        preferred_element_type=jnp.float32,
    )
    d_values = d_values.reshape(row_count, D).astype(jnp.bfloat16)
    d_scores = portions * (d_portions - jnp.sum(d_portions * portions, axis=-1, keepdims=True))
    d_scores = d_scores.astype(jnp.bfloat16)
    score_scale = HEAD_DIM ** (-0.5)
    d_queries = (
        jnp.einsum("hts,shd->thd", d_scores, key_heads, preferred_element_type=jnp.float32)
        * score_scale
    )
    d_queries = d_queries.reshape(row_count, D).astype(jnp.bfloat16)
    d_keys = (
        jnp.einsum("hts,thd->shd", d_scores, query_heads, preferred_element_type=jnp.float32)
        * score_scale
    )
    d_keys = d_keys.reshape(row_count, D).astype(jnp.bfloat16)
    d_joint = jnp.concatenate([d_queries, d_keys, d_values], axis=1)
    d_input_weight = inner_rows(low_input, d_joint)
    d_query_bias = jnp.sum(d_queries.astype(jnp.float32), axis=0)
    d_value_bias = jnp.sum(d_values.astype(jnp.float32), axis=0)
    d_inputs = d_resid_one + outer_cols(d_joint, input_weight)
    mat_grad = jnp.concatenate(
        [
            d_input_weight.reshape(-1),
            d_output.reshape(-1),
            d_expand.reshape(-1),
            d_shrink.reshape(-1),
        ]
    )
    vec_grad = jnp.concatenate(
        [
            d_query_bias,
            d_value_bias,
            d_output_bias,
            d_first_gain,
            d_first_shift,
            d_expand_bias,
            d_shrink_bias,
            d_second_gain,
            d_second_shift,
        ]
    )
    return (d_inputs, mat_grad, vec_grad)


def contrast_rows(anchors, key_table, anchor_index, span_count, score_scale):
    key_count = key_table.shape[0]
    key_index = jnp.arange(key_count, dtype=jnp.int32)
    scores = outer_cols(anchors, key_table) * score_scale
    scores = jnp.where(anchor_index[:, None] == key_index[None, :], masked_score, scores)
    partner = (
        jnp.bitwise_xor(anchor_index // span_count, 1) * span_count + anchor_index % span_count
    )
    row_max = jnp.max(scores, axis=-1, keepdims=True)
    raised = jnp.exp(scores - row_max)
    summed = jnp.sum(raised, axis=-1, keepdims=True)
    logsum = row_max[:, 0] + jnp.log(summed[:, 0])
    target = key_index[None, :] == partner[:, None]
    positive = jnp.sum(jnp.where(target, scores, 0.0), axis=1)
    grads_low = (raised / summed - target.astype(jnp.float32)).astype(jnp.bfloat16)
    return (grads_low, logsum - positive)


def general_body(tokens, cotangent, lengths, mats, mats_m, mats_v, vecs, vecs_m, vecs_v):
    full_mats, full_vecs = (
        lax.all_gather(mats.astype(jnp.bfloat16), ("dp", "pair"), axis=1, tiled=True),
        lax.all_gather(vecs.astype(jnp.bfloat16), ("dp", "pair"), axis=1, tiled=True),
    )
    layer_one = unpack(full_mats[0], full_vecs[0])
    layer_two = unpack(full_mats[1], full_vecs[1])
    inputs = tokens[0].astype(jnp.float32)
    row_count = inputs.shape[0]
    span_lengths = lengths[0, 0]
    span_count = span_lengths.shape[0]
    positions = jnp.arange(row_count, dtype=jnp.int32)
    order = jnp.arange(span_count)
    starts = jnp.sum(jnp.where(order[None, :] < order[:, None], span_lengths[None, :], 0), axis=1)
    span_of = jnp.sum((positions[:, None] >= starts[None, :]).astype(jnp.int32), axis=1)
    same_span = span_of[:, None] == span_of[None, :]
    heads_mark = positions[None, :] == starts[:, None]
    is_cls = jnp.any(heads_mark, axis=0)[:, None]
    picker = heads_mark.astype(jnp.float32)
    doc_groups = lax.axis_size("dp")
    early_out, kept_one = layer_forward(layer_one, inputs, same_span)
    cls_rows = exact_dot(picker, early_out)
    mixture = jnp.where(is_cls, early_out, inputs)
    late_out, kept_two = layer_forward(layer_two, mixture, same_span)
    sent_cls = cls_rows.astype(jnp.bfloat16)
    every_cls = lax.all_gather(sent_cls, ("dp", "pair"), axis=0, tiled=True)
    key_count = every_cls.shape[0]
    score_scale = 2.0 / math.sqrt(D)
    offset = lax.axis_index(("dp", "pair")) * span_count
    own_index = offset + jnp.arange(span_count, dtype=jnp.int32)
    grads_low, loss_terms = contrast_rows(sent_cls, every_cls, own_index, span_count, score_scale)
    anchor_part = matmul(grads_low, every_cls) * score_scale
    key_part = lax.psum_scatter(
        inner_rows(grads_low, sent_cls) * score_scale,
        ("dp", "pair"),
        scatter_dimension=0,
        tiled=True,
    )
    cls_grad = anchor_part + key_part
    grad_late = cotangent[0].astype(jnp.float32)
    d_mixture, late_mats, late_vecs = layer_backward(layer_two, kept_two, grad_late, same_span)
    grad_early = jnp.where(is_cls, d_mixture, 0.0) + exact_dot(picker.T, cls_grad)
    d_inputs, early_mats, early_vecs = layer_backward(layer_one, kept_one, grad_early, same_span)
    token_grad = d_inputs + jnp.where(is_cls, 0.0, d_mixture)
    all_pieces = (
        lax.all_to_all(
            early_mats.reshape(doc_groups, -1).astype(jnp.bfloat16),
            "dp",
            split_axis=0,
            concat_axis=0,
            tiled=True,
        ).astype(jnp.float32),
        lax.all_to_all(
            late_mats.reshape(doc_groups, -1).astype(jnp.bfloat16),
            "dp",
            split_axis=0,
            concat_axis=0,
            tiled=True,
        ).astype(jnp.float32),
        lax.all_to_all(
            early_vecs.reshape(doc_groups, -1).astype(jnp.bfloat16),
            "dp",
            split_axis=0,
            concat_axis=0,
            tiled=True,
        ).astype(jnp.float32),
        lax.all_to_all(
            late_vecs.reshape(doc_groups, -1).astype(jnp.bfloat16),
            "dp",
            split_axis=0,
            concat_axis=0,
            tiled=True,
        ).astype(jnp.float32),
    )
    early_mats_part, late_mats_part, early_vecs_part, late_vecs_part = (
        lax.psum_scatter(
            jnp.sum(all_pieces[0], axis=0).astype(jnp.bfloat16),
            "pair",
            scatter_dimension=0,
            tiled=True,
        ).astype(jnp.float32),
        lax.psum_scatter(
            jnp.sum(all_pieces[1], axis=0).astype(jnp.bfloat16),
            "pair",
            scatter_dimension=0,
            tiled=True,
        ).astype(jnp.float32),
        lax.psum_scatter(
            jnp.sum(all_pieces[2], axis=0).astype(jnp.bfloat16),
            "pair",
            scatter_dimension=0,
            tiled=True,
        ).astype(jnp.float32),
        lax.psum_scatter(
            jnp.sum(all_pieces[3], axis=0).astype(jnp.bfloat16),
            "pair",
            scatter_dimension=0,
            tiled=True,
        ).astype(jnp.float32),
    )
    grad_mats = jnp.stack([early_mats_part, late_mats_part])
    grad_vecs = jnp.stack([early_vecs_part, late_vecs_part])
    square_sum = jnp.sum(grad_mats * grad_mats) + jnp.sum(grad_vecs * grad_vecs)
    total_sq, loss_sum = lax.psum((square_sum, jnp.sum(loss_terms)), ("dp", "pair"))
    grad_norm = jnp.sqrt(total_sq)
    clip_factor = jnp.minimum(1.0, math.sqrt(2 * (PL + QL)) / (grad_norm + 1e-06))
    new_mats, new_mats_m, new_mats_v = adamw_update(
        mats, mats_m, mats_v, grad_mats * clip_factor, 0.1, weight_decay
    )
    new_vecs, new_vecs_m, new_vecs_v = adamw_update(
        vecs, vecs_m, vecs_v, grad_vecs * clip_factor, 0.5, 0.0
    )
    contrastive = loss_sum / key_count
    return (
        late_out.astype(jnp.bfloat16)[None],
        token_grad[None],
        contrastive,
        grad_norm,
        new_mats,
        new_mats_m,
        new_mats_v,
        new_vecs,
        new_vecs_m,
        new_vecs_v,
    )


def solution(mesh):
    flat = P(None, ("dp", "pair"))
    rows = P("pair", "dp", None)
    here = dict(mesh.shape) == {"dp": 16, "pair": 2}
    return jax.shard_map(
        body if here else general_body,
        mesh=mesh,
        in_specs=(rows, rows, rows) + (flat,) * 6,
        out_specs=(rows, rows, P(), P()) + (flat,) * 6,
        check_vma=False,
    )
```

```python
import math

import jax
import jax.numpy as jnp
from jax import lax
from jax.experimental import pallas as pl
from jax.experimental.pallas import tpu as pltpu
from jax.sharding import PartitionSpec as P

D = 768
HEADS = 12
HEAD_DIM = 64
FF = 3072
STEP = 10
PL = 7077888
QL = 9216

norm_epsilon = 1e-12
masked_score = -1000000000.0
beta_one = 0.9
beta_two = 0.999
adam_epsilon = 1e-08
weight_decay = 0.01

F32 = jnp.float32
BF16 = jnp.bfloat16
TOK = 256
GRAN = 96
GRANS = PL // D // GRAN
VMEM_BYTES = 63_000_000

V_BQ, V_BV, V_BO, V_G1, V_C1, V_B1, V_B2, V_G2, V_C2 = 0, 1, 2, 3, 4, 5, 9, 10, 11

R_E, R_DF, R_H, R_DA, R_ATT, R_DO, R_U, R_DQ, R_Q, R_DATT, R_WK, R_PU = (
    0, 8, 10, 12, 20, 22, 24, 26, 28, 30, 32, 56,
)
PAY = 80


def nn(a, b):
    return lax.dot_general(a, b, (((1,), (0,)), ((), ())), preferred_element_type=F32)


def nt(a, b):
    return lax.dot_general(a, b, (((1,), (1,)), ((), ())), preferred_element_type=F32)


def tn(a, b):
    return lax.dot_general(a, b, (((0,), (0,)), ((), ())), preferred_element_type=F32)


def iota(shape, axis):
    return lax.broadcasted_iota(jnp.int32, shape, axis)


def erf(x):
    x = jnp.clip(x, -3.832506856900711, 3.832506856900711)
    s = x * x
    top = 0.00022905065861350646
    for c in (0.0034082910107109506, 0.050955695062380861, 0.18520832239976145, 1.128379143519084):
        top = top * s + c
    low = -1.1791602954361697e-7
    for c in (
        0.000023547966471313185,
        0.0010179625278914885,
        0.014070470171167667,
        0.11098505178285362,
        0.49746925110067538,
        1.0,
    ):
        low = low * s + c
    return x * top / low


def gelu_both(a):
    phi = 0.5 + 0.5 * erf(a * math.sqrt(0.5))
    return a * phi, phi + a * jnp.exp(-0.5 * a * a) * (1.0 / math.sqrt(2.0 * math.pi))


def norm_forward(r):
    centred = r - jnp.mean(r, axis=-1, keepdims=True)
    rstd = lax.rsqrt(jnp.mean(centred * centred, axis=-1, keepdims=True) + norm_epsilon)
    return centred * rstd, rstd


def norm_backward(dy, gain, xhat, rstd):
    dx = dy * gain
    return rstd * (
        dx - jnp.mean(dx, axis=-1, keepdims=True) - xhat * jnp.mean(dx * xhat, axis=-1, keepdims=True)
    )


def colsum(v):
    return jnp.sum(v, axis=0, keepdims=True)


def flip(v, axis, bit):
    return lax.ppermute(v, axis, [(i, i ^ bit) for i in range(lax.axis_size(axis))])


def core_flip(v):
    return flip(v, "dp", 1)


def x_flip(v):
    return flip(v, "dp", 2)


def y_flip(v):
    return flip(v, "pair", 1)


def z_up(v):
    n = lax.axis_size("dp")
    return lax.ppermute(v, "dp", [(i, (i + 4) % n) for i in range(n)])


def z_turn(v, places):
    n = lax.axis_size("dp")
    return lax.ppermute(v, "dp", [(i, (i + 4 * places) % n) for i in range(n)])


def xor_flip(v, pair_bit, dp_bits):
    if not pair_bit:
        return flip(v, "dp", dp_bits)
    n = lax.axis_size("dp")
    return lax.ppermute(v, ("dp", "pair"), [(i, i ^ (2 * dp_bits + 1)) for i in range(2 * n)])


def fence(values):
    return list(lax.optimization_barrier(tuple(values)))


SMALL_STEPS = (((1, 0), (0, 1), (1, 1)), ((0, 2), (0, 4), (0, 6)), ((0, 8),))


def gather_step(v, step, device):
    got = [v] + [xor_flip(v, *bits) for bits in SMALL_STEPS[step]]
    here = (device >> (2 * step)) & (len(got) - 1)
    return lambda: jnp.concatenate([pick(here ^ p, got) for p in range(len(got))], 0)


def sum_step(v, step):
    return v + (flip(v, "pair", 1) if step == 0 else flip(v, "dp", 1 << (step - 1)))


def sum_quick(v):
    for bits in SMALL_STEPS:
        got = [v] + [xor_flip(v, *b) for b in bits]
        v = got[0] + got[1] if len(got) == 2 else (got[0] + got[1]) + (got[2] + got[3])
    return v


def pick(index, cases):
    return lax.select_n(index, *cases)


GATHER_ROUNDS = (
    ("x0", "y0", "s1"),
    ("d0", "e0", "x1", "y1", "s2"),
    ("d1", "e1", "x2", "y2", "s3"),
    ("d2", "e2", "x3", "y3"),
    ("d3", "e3"),
)


SEND_VEC, SEND_ONE, SEND = 288, 304, 592


def gather_blocks(own):
    have = {"s0": own}
    across = ["s0"]
    for r, tasks in enumerate(GATHER_ROUNDS):
        sources = {}
        for name in tasks:
            kind, k = name[0], int(name[1])
            sources[name] = {"s": f"s{k - 1}", "x": f"s{k}", "y": f"s{k}", "d": f"x{k}", "e": f"y{k}"}[kind]
        names = list(dict.fromkeys([*sources.values(), *across]))
        if r:
            have.update(zip(names, fence([have[i] for i in names])))
        for name, source in sources.items():
            move = {
                "s": z_up, "x": x_flip, "y": y_flip, "d": lambda v: y_flip(v[:SEND_ONE]), "e": lambda v: x_flip(v[SEND_ONE:])
            }[name[0]]
            have[name] = move(have[source])
        if 0 < r < 4:
            names = [*across, *tasks[:2]]
            have.update(zip(names, fence([have[i] for i in names])))
        for i in across:
            have["c" + i] = core_flip(have[i])
        across = list(tasks)
    for i in across:
        have["c" + i] = core_flip(have[i])
    return [[have[c + kind + str(k)] for c in ("", "c") for k in range(4) for kind in kinds] for kinds in ("sxyd", "sxye")]


def add16(a, b):
    return (a.astype(F32) + b.astype(F32)).astype(BF16)


GROUPS = ((3, 2), (1, 0))
GROUP_ROWS = 2304
SX, SY, QX, QY, OWN = 0, 576, 1152, 1440, 1728


def by_kind(granule, emit):
    joint = granule < 24
    wide = (granule >= 32) & (granule < 64)
    pl.when(joint)(lambda: emit(3))
    pl.when(wide)(lambda: emit(4))
    pl.when(jnp.logical_not(joint | wide))(lambda: emit(1))


def pack_kernel(info, flat, vecs, out):
    out[SEND_VEC:SEND_ONE, :] = jnp.zeros((SEND_ONE - SEND_VEC, D), BF16)
    both = vecs[...]
    out[SEND_VEC:SEND_ONE, 0:288] = jnp.concatenate([both, jnp.zeros((14, 288), F32)], 0).astype(BF16)
    for gi in range(3):

        def emit(n, gi=gi):
            m = GRAN // n
            for layer in range(2):
                for j in range(6):
                    parts = [
                        flat[pl.ds(12 * (GRAN * gi + p) + 2 * j + layer, m, stride=12 * n), :] for p in range(n)
                    ]
                    tile = parts[0] if n == 1 else jnp.concatenate(parts, 0)
                    at = SEND_ONE * layer + GRAN * gi
                    out[at : at + GRAN, 128 * j : 128 * (j + 1)] = tile.astype(BF16)

        by_kind(3 * info[0] + gi, emit)


def fill(info, pieces, diagonals, block, wbuf, vbuf, sem):
    z, x, c, y = info[1], info[2], info[3], info[4]
    copies = []
    for other in (0, 1):
        for k in range(4):
            for kind in range(4):
                i = 16 * other + 4 * k + kind
                dev = (
                    8 * ((z + 4 - k) & 3)
                    + 4 * jnp.bitwise_xor(x, kind & 1)
                    + 2 * jnp.bitwise_xor(c, other)
                    + jnp.bitwise_xor(y, kind >> 1)
                )
                source = pieces[i].at[pl.ds(SEND_ONE if block and kind < 3 else 0, 288)]
                copies.append(pltpu.make_async_copy(source, wbuf.at[pl.ds(pl.multiple_of(288 * dev, 16), 288)], sem.at[i]))
                source = (pieces if kind < 3 else diagonals)[i].at[pl.ds(SEND_VEC, 16)]
                copies.append(pltpu.make_async_copy(source, vbuf.at[dev], sem.at[32 + i]))
    for copy in copies:
        copy.start()
    return copies


def order_vec(vbuf, block, vec):
    every = vbuf[:, 0:2, :].astype(F32)
    for q in range(QL // GRAN):
        to, lo = GRAN * (q % 8), GRAN * (q % 3)
        vec[q // 8 : q // 8 + 1, to : to + GRAN] = every[q // 3, block : block + 1, lo : lo + GRAN]


def split_w1(wbuf, w1):
    def step(i, carry):
        rows = wbuf[pl.ds(32 + 4 * i, 4)].astype(F32)
        for j in range(4):
            part = rows[:, 24 * j : 24 * (j + 1), :].reshape(GRAN, D).astype(BF16)
            w1[j, pl.ds(pl.multiple_of(GRAN * i, GRAN), GRAN), :] = part
        return carry

    lax.fori_loop(0, 8, step, 0)


def w_in(wbuf, j):
    return wbuf[0:24, 32 * j : 32 * (j + 1), :].reshape(D, D)


def w_out(wbuf):
    return wbuf[24:32].reshape(D, D)


def w_shrink(wbuf, j):
    return wbuf[64 + 8 * j : 72 + 8 * j].reshape(D, D)


def expander():
    r, c = iota((32, 16), 0), iota((32, 16), 1)
    return ((r < 24) & ((r & 1) == c)).astype(BF16)


def head_mask():
    r, lane = iota((32, D), 0), iota((32, D), 1)
    return (r < 24) & ((r >> 1) == (lane >> 6))


def spread(expand, mask, rows):
    return jnp.where(mask, nn(expand, rows), 0.0).astype(BF16)


def first_forward(
    info, u_ref, *refs
):
    pieces = diagonals = refs[:32]
    y_out, xh1_o, rs1_o, xh2_o, rs2_o, gp_o, e_o, h_o, att_o, u_o, q_o, pu_o, qk_o, p_o, vec, vbuf, wflat, w1, sem = refs[32:]
    copies = fill(info, pieces, diagonals, 0, wflat, vbuf, sem)
    wbuf = wflat.reshape(GRANS, GRAN, D)
    start = info[5]
    u = u_ref[...]
    r, t = iota((16, TOK), 0), iota((16, TOK), 1)
    picker = (((r == 0) & (t == 0)) | ((r == 1) & (t == start))).astype(BF16)
    cls = nn(picker, u)
    cls16 = cls.astype(BF16)
    expand, mask = expander(), head_mask()
    r, t = iota((32, TOK), 0), iota((32, TOK), 1)
    inside = (t >= start).astype(jnp.int32) == (r & 1)
    real = r < 24
    for c in copies:
        c.wait()
    order_vec(vbuf, 0, vec)
    split_w1(wbuf, w1)
    q = (nn(cls16, w_in(wbuf, 0)) + vec[V_BQ : V_BQ + 1, :]).astype(BF16)
    qk = nt(spread(expand, mask, q), w_in(wbuf, 1)).astype(BF16)
    scores = jnp.where(inside, nt(qk, u) * HEAD_DIM**-0.5, masked_score)
    raised = jnp.exp(scores - jnp.max(scores, axis=-1, keepdims=True))
    portions = jnp.where(real, raised / jnp.sum(raised, axis=-1, keepdims=True), 0.0)
    low = portions.astype(BF16)
    pu = nn(low, u).astype(BF16)
    weight = jnp.sum(low.astype(F32), axis=-1, keepdims=True)
    heads = nn(pu, w_in(wbuf, 2)) + weight * vec[V_BV : V_BV + 1, :]
    att = tn(expand, jnp.where(mask, heads, 0.0).astype(BF16)).astype(BF16)
    xhat, rstd = norm_forward(cls + nn(att, w_out(wbuf)) + vec[V_BO : V_BO + 1, :])
    xh1_o[...] = xhat
    rs1_o[...] = jnp.broadcast_to(rstd, (16, 128))
    h = xhat * vec[V_G1 : V_G1 + 1, :] + vec[V_C1 : V_C1 + 1, :]
    h16 = h.astype(BF16)
    f = vec[V_B2 : V_B2 + 1, :]
    for j in range(4):
        e, gp = gelu_both(nn(h16, w1[j]) + vec[V_B1 + j : V_B1 + j + 1, :])
        e = e.astype(BF16)
        e_o[j] = e
        gp_o[j] = gp
        f = f + nn(e, w_shrink(wbuf, j))
    xhat, rstd = norm_forward(h + f)
    xh2_o[...] = xhat
    rs2_o[...] = jnp.broadcast_to(rstd, (16, 128))
    y_out[...] = xhat * vec[V_G2 : V_G2 + 1, :] + vec[V_C2 : V_C2 + 1, :]
    h_o[...] = h16
    att_o[...] = att
    u_o[...] = cls16
    q_o[...] = q
    pu_o[...] = pu
    qk_o[...] = qk
    p_o[...] = portions


def first_backward(
    info, u_ref, cls_all, dz, xh1, rs1, xh2, rs2, gp_i, e_i, h_i, att_i, ucls, q_i, pu_i, qk_i, p_i, *refs
):
    pieces = diagonals = refs[:32]
    tg_out, pay_out, vg_out, loss_out, vec, vbuf, wflat, w1, rows16, dcls, pay, sem = refs[32:]
    copies = fill(info, pieces, diagonals, 0, wflat, vbuf, sem)
    wbuf = wflat.reshape(GRANS, GRAN, D)
    start = info[5]
    u = u_ref[...]
    keys = cls_all[...]
    n_keys = keys.shape[0]
    scale = 2.0 / math.sqrt(D)
    r, c = iota((n_keys, n_keys), 0), iota((n_keys, n_keys), 1)
    scores = jnp.where(r == c, masked_score, nt(keys, keys) * scale)
    top = jnp.max(scores, axis=-1, keepdims=True)
    raised = jnp.exp(scores - top)
    total = jnp.sum(raised, axis=-1, keepdims=True)
    partner = jnp.bitwise_xor(r, 2) == c
    positive = jnp.sum(jnp.where(partner, scores, 0.0), axis=-1, keepdims=True)
    terms = top + jnp.log(total) - positive
    loss_out[...] = jnp.broadcast_to(colsum(terms) * (1.0 / n_keys), (8, 128))
    pull = (raised / total - partner.astype(F32)).astype(BF16)
    dcls[...] = (nn(pull, keys) + tn(pull, keys)) * scale
    rows16[...] = jnp.zeros((16, D), F32)
    rows16[0:1, :] = dz[0:1, :] + dcls[pl.ds(2 * info[0], 1), :]
    rows16[1:2, :] = dz[pl.ds(start, 1), :] + dcls[pl.ds(2 * info[0] + 1, 1), :]
    dy = rows16[...]
    for copy in copies:
        copy.wait()
    order_vec(vbuf, 0, vec)
    split_w1(wbuf, w1)
    vg_out[...] = jnp.zeros((16, D), F32)
    xhat = xh2[...]
    vg_out[V_G2 : V_G2 + 1, :] = colsum(dy * xhat)
    vg_out[V_C2 : V_C2 + 1, :] = colsum(dy)
    dr2 = norm_backward(dy, vec[V_G2 : V_G2 + 1, :], xhat, rs2[:, 0:1])
    df = dr2.astype(BF16)
    pay[R_DF : R_DF + 2, :] = df.astype(F32)[0:2, :]
    vg_out[V_B2 : V_B2 + 1, :] = colsum(df.astype(F32))
    dh = dr2
    for j in range(4):
        da = (gp_i[j] * nt(df, w_shrink(wbuf, j))).astype(BF16)
        pay[R_E + 2 * j : R_E + 2 * j + 2, :] = e_i[j].astype(F32)[0:2, :]
        pay[R_DA + 2 * j : R_DA + 2 * j + 2, :] = da.astype(F32)[0:2, :]
        vg_out[V_B1 + j : V_B1 + j + 1, :] = colsum(da.astype(F32))
        dh = dh + nt(da, w1[j])
    xhat = xh1[...]
    vg_out[V_G1 : V_G1 + 1, :] = colsum(dh * xhat)
    vg_out[V_C1 : V_C1 + 1, :] = colsum(dh)
    dr1 = norm_backward(dh, vec[V_G1 : V_G1 + 1, :], xhat, rs1[:, 0:1])
    do = dr1.astype(BF16)
    vg_out[V_BO : V_BO + 1, :] = colsum(do.astype(F32))
    datt = nt(do, w_out(wbuf)).astype(BF16)
    expand, mask = expander(), head_mask()
    portions = p_i[...]
    low = portions.astype(BF16)
    each = spread(expand, mask, datt)
    dvk = nt(each, w_in(wbuf, 2)).astype(BF16)
    constant = jnp.sum(each.astype(F32) * vec[V_BV : V_BV + 1, :], axis=-1, keepdims=True)
    dp = nt(dvk, u) + constant
    ds = (portions * (dp - jnp.sum(dp * portions, axis=-1, keepdims=True))).astype(BF16)
    dsu = nn(ds, u)
    weight = jnp.sum(low.astype(F32), axis=-1, keepdims=True)
    vg_out[V_BV : V_BV + 1, :] = colsum(each.astype(F32) * weight)
    part = jnp.where(mask, nn(dsu.astype(BF16), w_in(wbuf, 1)) * HEAD_DIM**-0.5, 0.0).astype(BF16)
    dq = tn(expand, part).astype(BF16)
    vg_out[V_BQ : V_BQ + 1, :] = colsum(dq.astype(F32))
    rows16[...] = dr1 + nt(dq, w_in(wbuf, 0))
    du = tn(ds, qk_i[...]) * HEAD_DIM**-0.5 + tn(low, dvk)
    is_cls = (iota((TOK, 1), 0) == 0) | (iota((TOK, 1), 0) == start)
    tg_out[...] = du + jnp.where(is_cls, 0.0, dz[...])
    tg_out[0:1, :] = tg_out[0:1, :] + rows16[0:1, :]
    tg_out[pl.ds(start, 1), :] = tg_out[pl.ds(start, 1), :] + rows16[1:2, :]
    for row, rows in ((R_H, h_i), (R_ATT, att_i), (R_U, ucls), (R_Q, q_i)):
        pay[row : row + 2, :] = rows[...].astype(F32)[0:2, :]
    for row, rows in ((R_DO, do), (R_DQ, dq), (R_DATT, datt)):
        pay[row : row + 2, :] = rows.astype(F32)[0:2, :]
    pay[R_WK : R_WK + 24, :] = dsu[0:24, :] * HEAD_DIM**-0.5
    pay[R_PU : R_PU + 24, :] = pu_i[...].astype(F32)[0:24, :]
    pay_out[...] = pay[...].astype(BF16)


def second_block(info, u_ref, cot_ref, y_ref, *refs):
    pieces = refs[:32]
    diagonals = {4 * i + 3: refs[32 + i] for i in range(8)}
    head_out, dz_out, vg_out = refs[40:43]
    outs = refs[43:47]
    (vec, vbuf, wflat, w1, grads, zf, zb, qs, ks, vs, pm, att, xh1, hb, ht, gp, es, das, xh2, acc, stage, dqs, dks, dvs, sem, osem) = refs[47:]
    copies = fill(info, pieces, diagonals, 1, wflat, vbuf, sem)
    wbuf = wflat.reshape(GRANS, GRAN, D)
    gbuf = grads.reshape(GRANS, GRAN, D)
    start = info[5]
    zf[...] = u_ref[...].astype(F32)
    zf[0:1, :] = y_ref[0:1, :]
    zf[pl.ds(start, 1), :] = y_ref[1:2, :]
    z16 = zf[...].astype(BF16)
    zb[...] = z16
    for c in copies:
        c.wait()
    order_vec(vbuf, 1, vec)
    split_w1(wbuf, w1)
    qs[...] = (nn(z16, w_in(wbuf, 0)) + vec[V_BQ : V_BQ + 1, :]).astype(BF16)
    ks[...] = nn(z16, w_in(wbuf, 1)).astype(BF16)
    vs[...] = (nn(z16, w_in(wbuf, 2)) + vec[V_BV : V_BV + 1, :]).astype(BF16)
    low_lane = iota((TOK, 128), 1) < HEAD_DIM
    same = (iota((TOK, TOK), 0) >= start) == (iota((TOK, TOK), 1) >= start)

    def lanes(p):
        return pl.ds(pl.multiple_of(128 * p, 128), 128)

    def attend(p, carry):
        qp, kp, vp = qs[:, lanes(p)], ks[:, lanes(p)], vs[:, lanes(p)]
        res = []
        for hh in range(2):
            qm = jnp.where(low_lane == (hh == 0), qp, jnp.zeros_like(qp))
            s = jnp.where(same, nt(qm, kp) * HEAD_DIM**-0.5, masked_score)
            raised = jnp.exp(s - jnp.max(s, axis=-1, keepdims=True))
            portions = raised / jnp.sum(raised, axis=-1, keepdims=True)
            pm[2 * p + hh] = portions
            res.append(nn(portions.astype(BF16), vp))
        att[:, lanes(p)] = jnp.where(low_lane, res[0], res[1]).astype(BF16)
        return carry

    lax.fori_loop(0, 6, attend, 0)
    xhat, rstd1 = norm_forward(zf[...] + (nn(att[...], w_out(wbuf)) + vec[V_BO : V_BO + 1, :]))
    xh1[...] = xhat
    h = xhat * vec[V_G1 : V_G1 + 1, :] + vec[V_C1 : V_C1 + 1, :]
    hb[...] = h.astype(BF16)
    ht[...] = h.T.astype(BF16)
    acc[...] = h + vec[V_B2 : V_B2 + 1, :]
    for j in range(4):
        e, slope = gelu_both(nn(hb[...], w1[j]) + vec[V_B1 + j : V_B1 + j + 1, :])
        gp[j] = slope
        e = e.astype(BF16)
        es[j] = e
        acc[...] += nn(e, w_shrink(wbuf, j))
    xhat, rstd2 = norm_forward(acc[...])
    xh2[...] = xhat
    head_out[...] = (xhat * vec[V_G2 : V_G2 + 1, :] + vec[V_C2 : V_C2 + 1, :]).astype(BF16)

    vg_out[...] = jnp.zeros((16, D), F32)
    dy = cot_ref[...].astype(F32)
    vg_out[V_G2 : V_G2 + 1, :] = colsum(dy * xh2[...])
    vg_out[V_C2 : V_C2 + 1, :] = colsum(dy)
    dr = norm_backward(dy, vec[V_G2 : V_G2 + 1, :], xh2[...], rstd2)
    acc[...] = dr
    df = dr.astype(BF16)
    dqs[...] = df
    vg_out[V_B2 : V_B2 + 1, :] = colsum(df.astype(F32))
    for j in range(4):
        df = dqs[...]
        gbuf[64 + 8 * j : 72 + 8 * j] = tn(es[j], df).astype(BF16).reshape(8, GRAN, D)
        da = (gp[j] * nt(df, w_shrink(wbuf, j))).astype(BF16)
        das[j] = da
        vg_out[V_B1 + j : V_B1 + j + 1, :] = colsum(da.astype(F32))
        acc[...] += nt(da, w1[j])

    def expand_grad(i, carry):
        rows = ht[pl.ds(pl.multiple_of(192 * i, 192), 192), :]
        for j in range(4):
            stage[:, 24 * j : 24 * (j + 1), :] = nn(rows, das[j]).reshape(8, 24, D)
        gbuf[pl.ds(32 + 8 * i, 8)] = stage[...].astype(BF16)
        return carry

    lax.fori_loop(0, 4, expand_grad, 0)
    dh = acc[...]
    vg_out[V_G1 : V_G1 + 1, :] = colsum(dh * xh1[...])
    vg_out[V_C1 : V_C1 + 1, :] = colsum(dh)
    dr = norm_backward(dh, vec[V_G1 : V_G1 + 1, :], xh1[...], rstd1)
    acc[...] = dr
    do = dr.astype(BF16)
    vg_out[V_BO : V_BO + 1, :] = colsum(do.astype(F32))
    gbuf[24:32] = tn(att[...], do).astype(BF16).reshape(8, GRAN, D)
    att[...] = nt(do, w_out(wbuf)).astype(BF16)

    def attend_back(p, carry):
        qp, kp, vp, dp_ = qs[:, lanes(p)], ks[:, lanes(p)], vs[:, lanes(p)], att[:, lanes(p)]
        dq, dk, dv = [], [], []
        for hh in range(2):
            portions = pm[2 * p + hh]
            dam = jnp.where(low_lane == (hh == 0), dp_, jnp.zeros_like(dp_))
            dp = nt(dam, vp)
            dv.append(tn(portions.astype(BF16), dp_))
            ds = (portions * (dp - jnp.sum(dp * portions, axis=-1, keepdims=True))).astype(BF16)
            dq.append(nn(ds, kp))
            dk.append(tn(ds, qp))
        dqs[:, lanes(p)] = (jnp.where(low_lane, dq[0], dq[1]) * HEAD_DIM**-0.5).astype(BF16)
        dks[:, lanes(p)] = (jnp.where(low_lane, dk[0], dk[1]) * HEAD_DIM**-0.5).astype(BF16)
        dvs[:, lanes(p)] = jnp.where(low_lane, dv[0], dv[1]).astype(BF16)
        return carry

    lax.fori_loop(0, 6, attend_back, 0)
    vg_out[V_BQ : V_BQ + 1, :] = colsum(dqs[...].astype(F32))
    vg_out[V_BV : V_BV + 1, :] = colsum(dvs[...].astype(F32))
    for j, part in enumerate((dqs, dks, dvs)):
        gbuf[0:24, 32 * j : 32 * (j + 1), :] = tn(zb[...], part[...]).astype(BF16).reshape(24, 32, D)
        acc[...] += nt(part[...], w_in(wbuf, j))
    dz_out[...] = acc[...]
    x, c, y = info[2], info[3], info[4]
    sends = []
    for other in (1, 0):
        for group, places in enumerate(GROUPS):
            out = outs[2 * other + group]
            for i, t in enumerate(places):
                for rel, pieces_of in ((3, ((SY + 144 * i, 0), (SX + 144 * i, 144))),
                                       (1, ((QX + 144 * i, 0), (SX + 288 + 144 * i, 144))),
                                       (2, ((SY + 288 + 144 * i, 0), (QY + 144 * i, 144))),
                                       (0, ((OWN + 288 * i, 0),))):
                    dev = (
                        8 * t
                        + 4 * jnp.bitwise_xor(x, rel & 1)
                        + 2 * jnp.bitwise_xor(c, other)
                        + jnp.bitwise_xor(y, rel >> 1)
                    )
                    rows = 288 if rel == 0 else 144
                    for to, lo in pieces_of:
                        source = grads.at[pl.ds(pl.multiple_of(288 * dev + lo, 16), rows)]
                        sends.append(pltpu.make_async_copy(source, out.at[pl.ds(to, rows)], osem.at[len(sends)]))
                        sends[-1].start()
    for copy in sends:
        copy.wait()


def total_kernel(own, over_x, over_y, last_x, last_y, first, second):
    for i, out in enumerate((first, second)):
        part = slice(144 * i, 144 * (i + 1))
        for half, (one, two) in enumerate(((last_x, over_y), (over_x, last_y))):
            mine = own[288 * i + 144 * half : 288 * i + 144 * (half + 1), :].astype(F32)
            out[144 * half : 144 * (half + 1), :] = (
                mine + one[part, :].astype(F32) + two[part, :].astype(F32)
            ).astype(BF16)


def owner_grad(info, *refs):
    pieces = refs[:10]
    out, pbuf, pf, sem = refs[10:]
    copies = []
    at = 0
    for i, piece in enumerate(pieces):
        copies.append(pltpu.make_async_copy(piece, pbuf.at[pl.ds(at, piece.shape[0])], sem.at[i]))
        at += piece.shape[0]
    for c in copies:
        c.start()
    for c in copies:
        c.wait()

    def widen(i, carry):
        at = pl.ds(pl.multiple_of(PAY * i, PAY), PAY)
        for j in range(6):
            pf[j, at, :] = pbuf[at, 128 * j : 128 * (j + 1)].astype(F32)
        return carry

    lax.fori_loop(0, 32, widen, 0)

    def rows(first):
        return jnp.concatenate(
            [
                jnp.concatenate(
                    [pf[j, pl.ds(first + s, 32, stride=PAY), :] for j in range(6)], axis=1
                )
                for s in range(2)
            ],
            axis=0,
        ).astype(BF16)

    def chosen(count, offset, source):
        one_hot = (iota((count, D), 1) == iota((count, D), 0) + offset).astype(BF16)
        return nt(one_hot, source).astype(BF16)

    def put(gi, n, p, value):
        m = GRAN // n
        for j in range(6):
            out[pl.ds(6 * (GRAN * gi + p) + j, m, stride=6 * n), :] = value[:, 128 * j : 128 * (j + 1)]

    for gi in range(3):
        g = 3 * info[0] + gi

        @pl.when(g < 24)
        def _(gi=gi, g=g):
            off = 32 * g
            put(gi, 3, 0, nn(chosen(32, off, rows(R_U)), rows(R_DQ)))
            lane = iota((64, D), 1) >> 6
            for p, left, right in ((1, R_WK, R_Q), (2, R_PU, R_DATT)):
                base = rows(right)
                total = jnp.zeros((32, D), F32)
                for h in range(HEADS):
                    masked = jnp.where(lane == h, base, jnp.zeros_like(base))
                    total = total + nn(chosen(32, off, rows(left + 2 * h)), masked)
                put(gi, 3, p, total)

        @pl.when((g >= 24) & (g < 32))
        def _(gi=gi, g=g):
            put(gi, 1, 0, nn(chosen(GRAN, GRAN * (g - 24), rows(R_ATT)), rows(R_DO)))

        @pl.when((g >= 32) & (g < 64))
        def _(gi=gi, g=g):
            left = chosen(24, 24 * (g - 32), rows(R_H))
            for p in range(4):
                put(gi, 4, p, nn(left, rows(R_DA + 2 * p)))

        @pl.when(g >= 64)
        def _(gi=gi, g=g):
            part = (g - 64) >> 3
            put(gi, 1, 0, nn(chosen(GRAN, GRAN * ((g - 64) & 7), rows(R_E + 2 * part)), rows(R_DF)))


def join_grads(info, g0, a, b, gv, out, square, buf):
    g = g0[...]
    out[pl.ds(0, 1728, stride=2), :] = g
    buf[...] = a[...].astype(F32) + b[...].astype(F32)
    total = buf[...]
    sq = jnp.sum((g * g).reshape(216, 8, 128), axis=0)
    for j in range(6):
        v = total[:, 128 * j : 128 * (j + 1)]
        sq = sq + jnp.sum((v * v).reshape(36, 8, 128), axis=0)
    whole = jnp.sum(colsum(sq), axis=1, keepdims=True)
    whole = whole + jnp.sum(colsum(gv[...] * gv[...]), axis=1, keepdims=True)
    square[...] = jnp.broadcast_to(whole, (8, 128))
    for gi in range(3):

        def emit(n, gi=gi):
            m = GRAN // n
            for p in range(n):
                for j in range(6):
                    out[pl.ds(12 * (GRAN * gi + p) + 2 * j + 1, m, stride=12 * n), :] = buf[
                        GRAN * gi + m * p : GRAN * gi + m * (p + 1), 128 * j : 128 * (j + 1)
                    ]

        by_kind(3 * info[0] + gi, emit)


def adamw_kernel(sq, w, m, v, g, vw, vm, vv, vg, w_new, m_new, v_new, vw_new, vm_new, vv_new, norm_out):
    norm = jnp.sqrt(sq[...])
    norm_out[...] = norm
    coef = jnp.minimum(1.0, math.sqrt(2 * (PL + QL)) / (norm[0:1, 0:1] + 1e-06))
    w_new[...], m_new[...], v_new[...] = adamw_update(w[...], m[...], v[...], g[...] * coef, 0.1, weight_decay)
    vw_new[...], vm_new[...], vv_new[...] = adamw_update(vw[...], vm[...], vv[...], vg[...] * coef, 0.5, 0.0)


def adamw_update(weight, moment_one, moment_two, gradient, step_rate, decay_rate):
    first_new = beta_one * moment_one + (1.0 - beta_one) * gradient
    second_new = beta_two * moment_two + (1.0 - beta_two) * gradient * gradient
    first_hat = first_new / (1.0 - beta_one**STEP)
    second_hat = second_new / (1.0 - beta_two**STEP)
    weight_new = weight - step_rate * (first_hat / (jnp.sqrt(second_hat) + adam_epsilon) + decay_rate * weight)
    return (weight_new, first_new, second_new)


SMEM = pl.BlockSpec(memory_space=pltpu.SMEM)
VMEM = pl.BlockSpec(memory_space=pltpu.VMEM)
ANY = pl.BlockSpec(memory_space=pl.ANY)


def struct(*shape, dtype=F32):
    return jax.ShapeDtypeStruct(shape, dtype)


def call(kernel, name, ins, in_specs, outs, out_specs, scratch=(), flops=0, moved=0):
    return pl.pallas_call(
        kernel,
        out_shape=outs,
        in_specs=in_specs,
        out_specs=out_specs,
        scratch_shapes=list(scratch),
        name=name,
        compiler_params=pltpu.CompilerParams(vmem_limit_bytes=VMEM_BYTES),
        cost_estimate=pl.CostEstimate(flops=flops, bytes_accessed=moved, transcendentals=0),
    )(*ins)


def flat_view(a):
    return a.reshape(2, -1, 128).transpose(1, 0, 2).reshape(-1, 128)


def flat_back(a):
    return a.reshape(-1, 2, 128).transpose(1, 0, 2).reshape(2, -1)


def body(tokens, cotangent, lengths, mats, mats_m, mats_v, vecs, vecs_m, vecs_v):
    dp, pair = lax.axis_index("dp"), lax.axis_index("pair")
    device = 2 * dp + pair
    z = dp >> 2
    info = jnp.stack(
        [device, z, (dp >> 1) & 1, dp & 1, pair, lengths[0, 0, 0], jnp.int32(0), jnp.int32(0)]
    ).astype(jnp.int32)
    u = tokens[0]
    cot = cotangent[0]
    flat = flat_view(mats)
    own = call(pack_kernel, "pack", (info, flat, vecs), [SMEM, VMEM, VMEM], struct(SEND, D, dtype=BF16), VMEM)
    pieces0, pieces1 = gather_blocks(own)
    row = struct(16, D)
    row16 = struct(16, D, dtype=BF16)
    saved_shapes = (
        row, struct(16, 128), row, struct(16, 128), struct(4, 16, D), struct(4, 16, D, dtype=BF16),
        row16, row16, row16, row16, struct(32, D, dtype=BF16), struct(32, D, dtype=BF16), struct(32, TOK),
    )
    weights = [
        pltpu.VMEM((16, D), F32),
        pltpu.VMEM((32, 16, D), BF16),
        pltpu.VMEM((GRANS * GRAN, D), BF16),
        pltpu.VMEM((4, D, D), BF16),
    ]
    y_cls, *saved = call(
        first_forward,
        "first_forward",
        (info, u, *pieces0),
        [SMEM, VMEM] + [ANY] * 32,
        (row, *saved_shapes),
        (VMEM,) * 14,
        weights + [pltpu.SemaphoreType.DMA((64,))],
        flops=2 * 32 * PL,
        moved=2 * PL,
    )
    part = struct(GROUP_ROWS, D, dtype=BF16)
    mid16 = pltpu.VMEM((TOK, D), BF16)
    mid = pltpu.VMEM((TOK, D), F32)
    head_out, dz, vg1, *terms = call(
        second_block,
        "second_block",
        (info, u, cot, y_cls, *pieces1, *pieces0[3::4]),
        [SMEM, VMEM, VMEM, VMEM] + [ANY] * 40,
        (struct(TOK, D, dtype=BF16), struct(TOK, D), row) + (part,) * 4,
        (VMEM, VMEM, VMEM) + (ANY,) * 4,
        weights
        + [
            pltpu.VMEM((GRANS * GRAN, D), BF16),
            mid, mid16, mid16, mid16, mid16,
            pltpu.VMEM((HEADS, TOK, TOK), F32),
            mid16, mid, mid16,
            pltpu.VMEM((D, TOK), BF16),
            pltpu.VMEM((4, TOK, D), F32),
            pltpu.VMEM((4, TOK, D), BF16),
            pltpu.VMEM((4, TOK, D), BF16),
            mid, mid,
            pltpu.VMEM((8, GRAN, D), F32),
            mid16, mid16, mid16,
            pltpu.SemaphoreType.DMA((64,)),
            pltpu.SemaphoreType.DMA((56,)),
        ],
        flops=6 * TOK * PL,
        moved=4 * PL,
    )
    mine, theirs = terms[:2], terms[2:]

    def settle(group, came):
        return [
            add16(mine[group][lo:hi], came[lo:hi])
            for lo, hi in ((SX, SY), (SY, QX), (QX, QY), (QY, OWN), (OWN, GROUP_ROWS))
        ]

    def plane_total(own, over_x, over_y, last_x, last_y):
        whole, half = pl.BlockSpec((576, D), lambda i: (0, 0)), pl.BlockSpec((288, D), lambda i: (0, 0))
        second = pl.BlockSpec((288, D), lambda i: (1, 0))
        return pl.pallas_call(
            total_kernel,
            grid=(1,),
            in_specs=[whole, second, second, half, half],
            out_specs=[half, half],
            out_shape=[struct(288, D, dtype=BF16)] * 2,
            name="total",
        )(own, over_x, over_y, last_x, last_y)

    theirs[0], theirs[1], cls = fence([*theirs, y_cls[0:2].astype(BF16)])
    came_a, came_b = core_flip(theirs[0]), core_flip(theirs[1])
    cls = gather_step(cls, 0, device)()
    sx, sy, qx_a, qy_a, own_a = settle(0, came_a)
    sx, sy, cls = fence([sx, sy, cls])
    over_xa, over_ya = x_flip(sx), y_flip(sy)
    cls = gather_step(cls, 1, device)()
    sx, sy, qx_b, qy_b, own_b = fence(settle(1, came_b))
    qx_a, qy_a, sx, sy, cls = fence([add16(qx_a, over_ya[:288]), add16(qy_a, over_xa[:288]), sx, sy, cls])
    last_xa, last_ya = x_flip(qx_a), y_flip(qy_a)
    over_xb, over_yb = x_flip(sx), y_flip(sy)
    every_cls = gather_step(cls, 2, device)()
    token_grad, payload, vg0, loss = call(
        first_backward,
        "first_backward",
        (info, u, every_cls, dz, *saved, *pieces0),
        [SMEM] + [VMEM] * 16 + [ANY] * 32,
        (struct(TOK, D), struct(PAY, D, dtype=BF16), row, struct(8, 128)),
        (VMEM,) * 4,
        weights
        + [
            pltpu.VMEM((16, D), F32),
            pltpu.VMEM((64, D), F32),
            pltpu.VMEM((PAY, D), F32),
            pltpu.SemaphoreType.DMA((64,)),
        ],
        flops=2 * 32 * PL,
        moved=2 * PL,
    )
    a3, a2 = plane_total(own_a, over_xa, over_ya, last_xa, last_ya)
    qx_b, qy_b, pay = fence([add16(qx_b, over_yb[:288]), add16(qy_b, over_xb[:288]), payload])
    last_xb, last_yb = x_flip(qx_b), y_flip(qy_b)
    slots = jnp.concatenate([pay, z_turn(pay, 1), z_turn(pay, 3), z_turn(pay, 2)], 0)
    a1, a0 = plane_total(own_b, over_xb, over_yb, last_xb, last_yb)
    at_z = [a0, a1, a2, a3]
    moving, slots, vec_sum = fence([pick((z + 3) & 3, at_z), slots, jnp.concatenate([vg0[:12], vg1[:12]], 0)])
    moving = z_up(moving)
    over_x, over_y = x_flip(slots), y_flip(slots)
    rows = [slots, over_x, over_y]
    vec_sum = sum_step(vec_sum, 0)
    vec_sum = sum_step(vec_sum, 1)
    moving, *rows, vec_sum = fence([add16(pick((z + 2) & 3, at_z), moving), *rows, vec_sum])
    moving = z_up(moving)
    half = rows[0].shape[0] // 2
    rows += [y_flip(rows[1][:half]), x_flip(rows[2][half:])]
    rows += [core_flip(v) for v in rows]
    vec_sum = sum_step(vec_sum, 2)
    vec_sum = sum_step(vec_sum, 3)
    moving, vec_sum = fence([add16(pick((z + 1) & 3, at_z), moving), vec_sum])
    moving = z_up(moving)
    vec_sum = sum_step(vec_sum, 4).reshape(2, QL)
    flat0 = call(
        owner_grad,
        "owner_grad",
        (info, *rows),
        [SMEM] + [ANY] * 10,
        struct(1728, 128),
        VMEM,
        [
            pltpu.VMEM((32 * PAY, D), BF16),
            pltpu.VMEM((6, 32 * PAY, 128), F32),
            pltpu.SemaphoreType.DMA((10,)),
        ],
        flops=2 * 768 * 768 * 768,
        moved=2 * 32 * PAY * D,
    )
    grad_vecs = lax.dynamic_slice(vec_sum, (0, device * vecs.shape[1]), vecs.shape)
    grads, square = call(
        join_grads,
        "join_grads",
        (info, flat0, pick(z, at_z), moving, grad_vecs),
        [SMEM] + [VMEM] * 4,
        (struct(3456, 128), struct(8, 128)),
        (VMEM, VMEM),
        [pltpu.VMEM((288, D), F32)],
    )
    block = pl.BlockSpec((864, 128), lambda i: (i, 0))
    small = pl.BlockSpec(vecs.shape, lambda i: (0, 0))
    tile = pl.BlockSpec((8, 128), lambda i: (0, 0))
    *new, new_vecs, new_vecs_m, new_vecs_v, norm = pl.pallas_call(
        adamw_kernel,
        grid=(4,),
        in_specs=[tile] + [block] * 4 + [small] * 4,
        out_specs=(block,) * 3 + (small,) * 3 + (tile,),
        out_shape=(struct(3456, 128),) * 3 + (struct(*vecs.shape),) * 3 + (struct(8, 128),),
        name="adamw",
    )(sum_quick(square), flat, flat_view(mats_m), flat_view(mats_v), grads, vecs, vecs_m, vecs_v, grad_vecs)
    new_mats, new_mats_m, new_mats_v = [flat_back(a) for a in new]
    return (
        head_out[None],
        token_grad[None],
        loss[0, 0],
        norm[0, 0],
        new_mats,
        new_mats_m,
        new_mats_v,
        new_vecs,
        new_vecs_m,
        new_vecs_v,
    )


def matmul(left_side, right_side):
    return jnp.dot(left_side, right_side, preferred_element_type=jnp.float32)


def inner_rows(left_side, right_side):
    return lax.dot_general(
        left_side, right_side, (((0,), (0,)), ((), ())), preferred_element_type=jnp.float32
    )


def outer_cols(left_side, right_side):
    return lax.dot_general(
        left_side, right_side, (((1,), (1,)), ((), ())), preferred_element_type=jnp.float32
    )


def exact_dot(left_side, right_side):
    return jnp.dot(
        left_side, right_side, precision=lax.Precision.HIGHEST, preferred_element_type=jnp.float32
    )


def layer_norm(resid, gain, shift):
    centred = resid - jnp.mean(resid, axis=-1, keepdims=True)
    spread = jnp.mean(centred * centred, axis=-1, keepdims=True)
    return centred * lax.rsqrt(spread + norm_epsilon) * gain + shift


def gelu_exact(before):
    return jax.nn.gelu(before, approximate=False)


def unpack(mat_row, vec_row):
    edge_one = 3 * D * D
    edge_two = 4 * D * D
    edge_three = edge_two + D * FF
    input_weight = mat_row[:edge_one].reshape(D, 3 * D)
    output_weight = mat_row[edge_one:edge_two].reshape(D, D)
    expand_weight = mat_row[edge_two:edge_three].reshape(D, FF)
    shrink_weight = mat_row[edge_three:].reshape(FF, D)
    vector = vec_row.astype(jnp.float32)
    pieces = []
    cursor = 0
    for piece_len in (D, D, D, D, D, FF, D, D, D):
        pieces.append(vector[cursor : cursor + piece_len])
        cursor = cursor + piece_len
    return (input_weight, output_weight, expand_weight, shrink_weight) + tuple(pieces)


def head_scores(queries, key_rows, same_span):
    row_count = queries.shape[0]
    query_heads = queries.reshape(row_count, HEADS, HEAD_DIM)
    key_heads = key_rows.reshape(row_count, HEADS, HEAD_DIM)
    scores = jnp.einsum(
        "thd,shd->hts", query_heads, key_heads, preferred_element_type=jnp.float32
    ) * HEAD_DIM ** (-0.5)
    return jnp.where(same_span[None, :, :], scores, masked_score)


def layer_forward(params, inputs, same_span):
    (
        input_weight,
        output_weight,
        expand_weight,
        shrink_weight,
        query_bias,
        value_bias,
        output_bias,
        first_gain,
        first_shift,
        expand_bias,
        shrink_bias,
        second_gain,
        second_shift,
    ) = params
    row_count = inputs.shape[0]
    low_input = inputs.astype(jnp.bfloat16)
    joint = matmul(low_input, input_weight)
    queries = (joint[:, :D] + query_bias).astype(jnp.bfloat16)
    key_rows = joint[:, D : 2 * D].astype(jnp.bfloat16)
    values = (joint[:, 2 * D :] + value_bias).astype(jnp.bfloat16)
    scores = head_scores(queries, key_rows, same_span)
    row_max = jnp.max(scores, axis=-1, keepdims=True)
    raised = jnp.exp(scores - row_max)
    summed = jnp.sum(raised, axis=-1, keepdims=True)
    portions = raised / summed
    logsum = row_max + jnp.log(summed)
    value_heads = values.reshape(row_count, HEADS, HEAD_DIM)
    attended = jnp.einsum(
        "hts,shd->thd",
        portions.astype(jnp.bfloat16),
        value_heads,
        preferred_element_type=jnp.float32,
    )
    attended = attended.reshape(row_count, D).astype(jnp.bfloat16)
    resid_one = inputs + (matmul(attended, output_weight) + output_bias)
    hidden = layer_norm(resid_one, first_gain, first_shift)
    low_hidden = hidden.astype(jnp.bfloat16)
    before = matmul(low_hidden, expand_weight) + expand_bias
    activated = gelu_exact(before).astype(jnp.bfloat16)
    resid_two = hidden + (matmul(activated, shrink_weight) + shrink_bias)
    output = layer_norm(resid_two, second_gain, second_shift)
    kept = (
        low_input,
        queries,
        key_rows,
        values,
        logsum,
        attended,
        resid_one,
        low_hidden,
        before,
        activated,
        resid_two,
    )
    return (output, kept)


def layer_backward(params, kept, grad_out, same_span):
    (
        input_weight,
        output_weight,
        expand_weight,
        shrink_weight,
        query_bias,
        value_bias,
        output_bias,
        first_gain,
        first_shift,
        expand_bias,
        shrink_bias,
        second_gain,
        second_shift,
    ) = params
    (
        low_input,
        queries,
        key_rows,
        values,
        logsum,
        attended,
        resid_one,
        low_hidden,
        before,
        activated,
        resid_two,
    ) = kept
    row_count = low_input.shape[0]
    _, norm_pull_two = jax.vjp(layer_norm, resid_two, second_gain, second_shift)
    d_resid_two, d_second_gain, d_second_shift = norm_pull_two(grad_out)
    d_feed = d_resid_two.astype(jnp.bfloat16)
    d_shrink = inner_rows(activated, d_feed)
    d_shrink_bias = jnp.sum(d_feed.astype(jnp.float32), axis=0)
    _, gelu_pull = jax.vjp(gelu_exact, before)
    d_before = gelu_pull(outer_cols(d_feed, shrink_weight))[0].astype(jnp.bfloat16)
    d_expand = inner_rows(low_hidden, d_before)
    d_expand_bias = jnp.sum(d_before.astype(jnp.float32), axis=0)
    d_hidden = d_resid_two + outer_cols(d_before, expand_weight)
    _, norm_pull_one = jax.vjp(layer_norm, resid_one, first_gain, first_shift)
    d_resid_one, d_first_gain, d_first_shift = norm_pull_one(d_hidden)
    d_branch = d_resid_one.astype(jnp.bfloat16)
    d_output = inner_rows(attended, d_branch)
    d_output_bias = jnp.sum(d_branch.astype(jnp.float32), axis=0)
    d_attended = outer_cols(d_branch, output_weight).astype(jnp.bfloat16)
    portions = jnp.exp(head_scores(queries, key_rows, same_span) - logsum)
    query_heads = queries.reshape(row_count, HEADS, HEAD_DIM)
    key_heads = key_rows.reshape(row_count, HEADS, HEAD_DIM)
    value_heads = values.reshape(row_count, HEADS, HEAD_DIM)
    d_att_heads = d_attended.reshape(row_count, HEADS, HEAD_DIM)
    d_portions = jnp.einsum(
        "thd,shd->hts", d_att_heads, value_heads, preferred_element_type=jnp.float32
    )
    d_values = jnp.einsum(
        "hts,thd->shd",
        portions.astype(jnp.bfloat16),
        d_att_heads,
        preferred_element_type=jnp.float32,
    )
    d_values = d_values.reshape(row_count, D).astype(jnp.bfloat16)
    d_scores = portions * (d_portions - jnp.sum(d_portions * portions, axis=-1, keepdims=True))
    d_scores = d_scores.astype(jnp.bfloat16)
    score_scale = HEAD_DIM ** (-0.5)
    d_queries = (
        jnp.einsum("hts,shd->thd", d_scores, key_heads, preferred_element_type=jnp.float32)
        * score_scale
    )
    d_queries = d_queries.reshape(row_count, D).astype(jnp.bfloat16)
    d_keys = (
        jnp.einsum("hts,thd->shd", d_scores, query_heads, preferred_element_type=jnp.float32)
        * score_scale
    )
    d_keys = d_keys.reshape(row_count, D).astype(jnp.bfloat16)
    d_joint = jnp.concatenate([d_queries, d_keys, d_values], axis=1)
    d_input_weight = inner_rows(low_input, d_joint)
    d_query_bias = jnp.sum(d_queries.astype(jnp.float32), axis=0)
    d_value_bias = jnp.sum(d_values.astype(jnp.float32), axis=0)
    d_inputs = d_resid_one + outer_cols(d_joint, input_weight)
    mat_grad = jnp.concatenate(
        [
            d_input_weight.reshape(-1),
            d_output.reshape(-1),
            d_expand.reshape(-1),
            d_shrink.reshape(-1),
        ]
    )
    vec_grad = jnp.concatenate(
        [
            d_query_bias,
            d_value_bias,
            d_output_bias,
            d_first_gain,
            d_first_shift,
            d_expand_bias,
            d_shrink_bias,
            d_second_gain,
            d_second_shift,
        ]
    )
    return (d_inputs, mat_grad, vec_grad)


def contrast_rows(anchors, key_table, anchor_index, span_count, score_scale):
    key_count = key_table.shape[0]
    key_index = jnp.arange(key_count, dtype=jnp.int32)
    scores = outer_cols(anchors, key_table) * score_scale
    scores = jnp.where(anchor_index[:, None] == key_index[None, :], masked_score, scores)
    partner = (
        jnp.bitwise_xor(anchor_index // span_count, 1) * span_count + anchor_index % span_count
    )
    row_max = jnp.max(scores, axis=-1, keepdims=True)
    raised = jnp.exp(scores - row_max)
    summed = jnp.sum(raised, axis=-1, keepdims=True)
    logsum = row_max[:, 0] + jnp.log(summed[:, 0])
    target = key_index[None, :] == partner[:, None]
    positive = jnp.sum(jnp.where(target, scores, 0.0), axis=1)
    grads_low = (raised / summed - target.astype(jnp.float32)).astype(jnp.bfloat16)
    return (grads_low, logsum - positive)


def general_body(tokens, cotangent, lengths, mats, mats_m, mats_v, vecs, vecs_m, vecs_v):
    full_mats, full_vecs = (
        lax.all_gather(mats.astype(jnp.bfloat16), ("dp", "pair"), axis=1, tiled=True),
        lax.all_gather(vecs.astype(jnp.bfloat16), ("dp", "pair"), axis=1, tiled=True),
    )
    layer_one = unpack(full_mats[0], full_vecs[0])
    layer_two = unpack(full_mats[1], full_vecs[1])
    inputs = tokens[0].astype(jnp.float32)
    row_count = inputs.shape[0]
    span_lengths = lengths[0, 0]
    span_count = span_lengths.shape[0]
    positions = jnp.arange(row_count, dtype=jnp.int32)
    order = jnp.arange(span_count)
    starts = jnp.sum(jnp.where(order[None, :] < order[:, None], span_lengths[None, :], 0), axis=1)
    span_of = jnp.sum((positions[:, None] >= starts[None, :]).astype(jnp.int32), axis=1)
    same_span = span_of[:, None] == span_of[None, :]
    heads_mark = positions[None, :] == starts[:, None]
    is_cls = jnp.any(heads_mark, axis=0)[:, None]
    picker = heads_mark.astype(jnp.float32)
    doc_groups = lax.axis_size("dp")
    early_out, kept_one = layer_forward(layer_one, inputs, same_span)
    cls_rows = exact_dot(picker, early_out)
    mixture = jnp.where(is_cls, early_out, inputs)
    late_out, kept_two = layer_forward(layer_two, mixture, same_span)
    sent_cls = cls_rows.astype(jnp.bfloat16)
    every_cls = lax.all_gather(sent_cls, ("dp", "pair"), axis=0, tiled=True)
    key_count = every_cls.shape[0]
    score_scale = 2.0 / math.sqrt(D)
    offset = lax.axis_index(("dp", "pair")) * span_count
    own_index = offset + jnp.arange(span_count, dtype=jnp.int32)
    grads_low, loss_terms = contrast_rows(sent_cls, every_cls, own_index, span_count, score_scale)
    anchor_part = matmul(grads_low, every_cls) * score_scale
    key_part = lax.psum_scatter(
        inner_rows(grads_low, sent_cls) * score_scale,
        ("dp", "pair"),
        scatter_dimension=0,
        tiled=True,
    )
    cls_grad = anchor_part + key_part
    grad_late = cotangent[0].astype(jnp.float32)
    d_mixture, late_mats, late_vecs = layer_backward(layer_two, kept_two, grad_late, same_span)
    grad_early = jnp.where(is_cls, d_mixture, 0.0) + exact_dot(picker.T, cls_grad)
    d_inputs, early_mats, early_vecs = layer_backward(layer_one, kept_one, grad_early, same_span)
    token_grad = d_inputs + jnp.where(is_cls, 0.0, d_mixture)
    all_pieces = (
        lax.all_to_all(
            early_mats.reshape(doc_groups, -1).astype(jnp.bfloat16),
            "dp",
            split_axis=0,
            concat_axis=0,
            tiled=True,
        ).astype(jnp.float32),
        lax.all_to_all(
            late_mats.reshape(doc_groups, -1).astype(jnp.bfloat16),
            "dp",
            split_axis=0,
            concat_axis=0,
            tiled=True,
        ).astype(jnp.float32),
        lax.all_to_all(
            early_vecs.reshape(doc_groups, -1).astype(jnp.bfloat16),
            "dp",
            split_axis=0,
            concat_axis=0,
            tiled=True,
        ).astype(jnp.float32),
        lax.all_to_all(
            late_vecs.reshape(doc_groups, -1).astype(jnp.bfloat16),
            "dp",
            split_axis=0,
            concat_axis=0,
            tiled=True,
        ).astype(jnp.float32),
    )
    early_mats_part, late_mats_part, early_vecs_part, late_vecs_part = (
        lax.psum_scatter(
            jnp.sum(all_pieces[0], axis=0).astype(jnp.bfloat16),
            "pair",
            scatter_dimension=0,
            tiled=True,
        ).astype(jnp.float32),
        lax.psum_scatter(
            jnp.sum(all_pieces[1], axis=0).astype(jnp.bfloat16),
            "pair",
            scatter_dimension=0,
            tiled=True,
        ).astype(jnp.float32),
        lax.psum_scatter(
            jnp.sum(all_pieces[2], axis=0).astype(jnp.bfloat16),
            "pair",
            scatter_dimension=0,
            tiled=True,
        ).astype(jnp.float32),
        lax.psum_scatter(
            jnp.sum(all_pieces[3], axis=0).astype(jnp.bfloat16),
            "pair",
            scatter_dimension=0,
            tiled=True,
        ).astype(jnp.float32),
    )
    grad_mats = jnp.stack([early_mats_part, late_mats_part])
    grad_vecs = jnp.stack([early_vecs_part, late_vecs_part])
    square_sum = jnp.sum(grad_mats * grad_mats) + jnp.sum(grad_vecs * grad_vecs)
    total_sq, loss_sum = lax.psum((square_sum, jnp.sum(loss_terms)), ("dp", "pair"))
    grad_norm = jnp.sqrt(total_sq)
    clip_factor = jnp.minimum(1.0, math.sqrt(2 * (PL + QL)) / (grad_norm + 1e-06))
    new_mats, new_mats_m, new_mats_v = adamw_update(
        mats, mats_m, mats_v, grad_mats * clip_factor, 0.1, weight_decay
    )
    new_vecs, new_vecs_m, new_vecs_v = adamw_update(
        vecs, vecs_m, vecs_v, grad_vecs * clip_factor, 0.5, 0.0
    )
    contrastive = loss_sum / key_count
    return (
        late_out.astype(jnp.bfloat16)[None],
        token_grad[None],
        contrastive,
        grad_norm,
        new_mats,
        new_mats_m,
        new_mats_v,
        new_vecs,
        new_vecs_m,
        new_vecs_v,
    )


def solution(mesh):
    flat = P(None, ("dp", "pair"))
    rows = P("pair", "dp", None)
    here = dict(mesh.shape) == {"dp": 16, "pair": 2}
    return jax.shard_map(
        body if here else general_body,
        mesh=mesh,
        in_specs=(rows, rows, rows) + (flat,) * 6,
        out_specs=(rows, rows, P(), P()) + (flat,) * 6,
        check_vma=False,
    )
```

```python
import math

import jax
import jax.numpy as jnp
from jax import lax
from jax.experimental import pallas as pl
from jax.experimental.pallas import tpu as pltpu
from jax.sharding import PartitionSpec as P

D = 768
HEADS = 12
HEAD_DIM = 64
FF = 3072
STEP = 10
PL = 7077888
QL = 9216

norm_epsilon = 1e-12
masked_score = -1000000000.0
beta_one = 0.9
beta_two = 0.999
adam_epsilon = 1e-08
weight_decay = 0.01

F32 = jnp.float32
BF16 = jnp.bfloat16
TOK = 256
GRAN = 96
GRANS = PL // D // GRAN
VMEM_BYTES = 63_000_000

V_BQ, V_BV, V_BO, V_G1, V_C1, V_B1, V_B2, V_G2, V_C2 = 0, 1, 2, 3, 4, 5, 9, 10, 11

R_E, R_DF, R_H, R_DA, R_ATT, R_DO, R_U, R_DQ, R_Q, R_DATT, R_WK, R_PU, R_VEC = (
    0, 8, 10, 12, 20, 22, 24, 26, 28, 30, 32, 56, 80,
)
PAY = 96


def nn(a, b):
    return lax.dot_general(a, b, (((1,), (0,)), ((), ())), preferred_element_type=F32)


def nt(a, b):
    return lax.dot_general(a, b, (((1,), (1,)), ((), ())), preferred_element_type=F32)


def tn(a, b):
    return lax.dot_general(a, b, (((0,), (0,)), ((), ())), preferred_element_type=F32)


def iota(shape, axis):
    return lax.broadcasted_iota(jnp.int32, shape, axis)


def erf(x):
    x = jnp.clip(x, -3.832506856900711, 3.832506856900711)
    s = x * x
    top = 0.00022905065861350646
    for c in (0.0034082910107109506, 0.050955695062380861, 0.18520832239976145, 1.128379143519084):
        top = top * s + c
    low = -1.1791602954361697e-7
    for c in (
        0.000023547966471313185,
        0.0010179625278914885,
        0.014070470171167667,
        0.11098505178285362,
        0.49746925110067538,
        1.0,
    ):
        low = low * s + c
    return x * top / low


def gelu_both(a):
    phi = 0.5 + 0.5 * erf(a * math.sqrt(0.5))
    return a * phi, phi + a * jnp.exp(-0.5 * a * a) * (1.0 / math.sqrt(2.0 * math.pi))


def norm_forward(r):
    centred = r - jnp.mean(r, axis=-1, keepdims=True)
    rstd = lax.rsqrt(jnp.mean(centred * centred, axis=-1, keepdims=True) + norm_epsilon)
    return centred * rstd, rstd


def norm_backward(dy, gain, xhat, rstd):
    dx = dy * gain
    return rstd * (
        dx - jnp.mean(dx, axis=-1, keepdims=True) - xhat * jnp.mean(dx * xhat, axis=-1, keepdims=True)
    )


def colsum(v):
    return jnp.sum(v, axis=0, keepdims=True)


def flip(v, axis, bit):
    return lax.ppermute(v, axis, [(i, i ^ bit) for i in range(lax.axis_size(axis))])


def core_flip(v):
    return flip(v, "dp", 1)


def x_flip(v):
    return flip(v, "dp", 2)


def y_flip(v):
    return flip(v, "pair", 1)


def z_up(v):
    n = lax.axis_size("dp")
    return lax.ppermute(v, "dp", [(i, (i + 4) % n) for i in range(n)])


def z_turn(v, places):
    n = lax.axis_size("dp")
    return lax.ppermute(v, "dp", [(i, (i + 4 * places) % n) for i in range(n)])


def xor_flip(v, pair_bit, dp_bits):
    if not pair_bit:
        return flip(v, "dp", dp_bits)
    n = lax.axis_size("dp")
    return lax.ppermute(v, ("dp", "pair"), [(i, i ^ (2 * dp_bits + 1)) for i in range(2 * n)])


def fence(values):
    return list(lax.optimization_barrier(tuple(values)))


SMALL_STEPS = (((1, 0), (0, 1), (1, 1)), ((0, 2), (0, 4), (0, 6)), ((0, 8),))


def gather_step(v, step, device):
    got = [v] + [xor_flip(v, *bits) for bits in SMALL_STEPS[step]]
    here = (device >> (2 * step)) & (len(got) - 1)
    return lambda: jnp.concatenate([pick(here ^ p, got) for p in range(len(got))], 0)


def sum_quick(v):
    for bits in SMALL_STEPS:
        got = [v] + [xor_flip(v, *b) for b in bits]
        v = got[0] + got[1] if len(got) == 2 else (got[0] + got[1]) + (got[2] + got[3])
    return v


def pick(index, cases):
    return lax.select_n(index, *cases)


GATHER_ROUNDS = (
    ("x0", "y0", "s1"),
    ("d0", "e0", "x1", "y1", "s2"),
    ("d1", "e1", "x2", "y2", "s3"),
    ("d2", "e2", "x3", "y3"),
    ("d3", "e3"),
)


SEND_VEC, SEND_ONE, SEND = 288, 304, 592


def gather_blocks(own):
    have = {"s0": own}
    across = ["s0"]
    for r, tasks in enumerate(GATHER_ROUNDS):
        sources = {}
        for name in tasks:
            kind, k = name[0], int(name[1])
            sources[name] = {"s": f"s{k - 1}", "x": f"s{k}", "y": f"s{k}", "d": f"x{k}", "e": f"y{k}"}[kind]
        names = list(dict.fromkeys([*sources.values(), *across]))
        if r:
            have.update(zip(names, fence([have[i] for i in names])))
        for name, source in sources.items():
            move = {
                "s": z_up, "x": x_flip, "y": y_flip, "d": lambda v: y_flip(v[:SEND_ONE]), "e": lambda v: x_flip(v[SEND_ONE:])
            }[name[0]]
            have[name] = move(have[source])
        if 0 < r < 4:
            names = [*across, *tasks[:2]]
            have.update(zip(names, fence([have[i] for i in names])))
        for i in across:
            have["c" + i] = core_flip(have[i])
        across = list(tasks)
    for i in across:
        have["c" + i] = core_flip(have[i])
    return [[have[c + kind + str(k)] for c in ("", "c") for k in range(4) for kind in kinds] for kinds in ("sxyd", "sxye")]


def add16(a, b):
    return (a.astype(F32) + b.astype(F32)).astype(BF16)


GROUPS = ((3, 2), (1, 0))
GROUP_ROWS = 2304
HALF = 1152
SX, SY, QX, QY, OWN = 0, 576, 1152, 1440, 1728


def by_kind(granule, emit):
    joint = granule < 24
    wide = (granule >= 32) & (granule < 64)
    pl.when(joint)(lambda: emit(3))
    pl.when(wide)(lambda: emit(4))
    pl.when(jnp.logical_not(joint | wide))(lambda: emit(1))


def pack_kernel(info, flat, vecs, out):
    out[SEND_VEC:SEND_ONE, :] = jnp.zeros((SEND_ONE - SEND_VEC, D), BF16)
    both = vecs[...]
    out[SEND_VEC:SEND_ONE, 0:288] = jnp.concatenate([both, jnp.zeros((14, 288), F32)], 0).astype(BF16)
    for gi in range(3):

        def emit(n, gi=gi):
            m = GRAN // n
            for layer in range(2):
                for j in range(6):
                    parts = [
                        flat[pl.ds(12 * (GRAN * gi + p) + 2 * j + layer, m, stride=12 * n), :] for p in range(n)
                    ]
                    tile = parts[0] if n == 1 else jnp.concatenate(parts, 0)
                    at = SEND_ONE * layer + GRAN * gi
                    out[at : at + GRAN, 128 * j : 128 * (j + 1)] = tile.astype(BF16)

        by_kind(3 * info[0] + gi, emit)


def owner(info, plane, kind, other):
    return (
        8 * plane
        + 4 * jnp.bitwise_xor(info[2], kind & 1)
        + 2 * jnp.bitwise_xor(info[3], other)
        + jnp.bitwise_xor(info[4], kind >> 1)
    )


def fill(info, pieces, diagonals, block, wbuf, vbuf, sem):
    vecs = []
    for other in (0, 1):
        for k in range(4):
            for kind in range(4):
                i = 16 * other + 4 * k + kind
                source = (pieces if kind < 3 else diagonals)[i].at[pl.ds(SEND_VEC, 16)]
                dev = owner(info, (info[1] + 4 - k) & 3, kind, other)
                vecs.append(pltpu.make_async_copy(source, vbuf.at[dev], sem.at[32 + i]))
    for copy in vecs:
        copy.start()

    def copies(plane, k):
        made = []
        for other in (0, 1):
            for kind in range(4):
                source = pieces[16 * other + 4 * k + kind].at[pl.ds(SEND_ONE if block and kind < 3 else 0, 288)]
                rows = pl.ds(pl.multiple_of(288 * owner(info, plane, kind, other), 16), 288)
                made.append(pltpu.make_async_copy(source, wbuf.at[rows], sem.at[8 * plane + 2 * kind + other]))
        return made

    for plane in range(4):
        for k in range(4):

            @pl.when(((info[1] + 4 - plane) & 3) == k)
            def _(plane=plane, k=k):
                for copy in copies(plane, k):
                    copy.start()

    def wait_vecs():
        for copy in vecs:
            copy.wait()

    def wait(plane):
        for copy in copies(plane, 0):
            copy.wait()

    return wait_vecs, wait


def order_vec(vbuf, block, vec):
    every = vbuf[:, 0:2, :].astype(F32)
    for q in range(QL // GRAN):
        to, lo = GRAN * (q % 8), GRAN * (q % 3)
        vec[q // 8 : q // 8 + 1, to : to + GRAN] = every[q // 3, block : block + 1, lo : lo + GRAN]


def split_w1(wbuf, w1):
    def step(i, carry):
        rows = wbuf[pl.ds(32 + 4 * i, 4)].astype(F32)
        for j in range(4):
            part = rows[:, 24 * j : 24 * (j + 1), :].reshape(GRAN, D).astype(BF16)
            w1[j, pl.ds(pl.multiple_of(GRAN * i, GRAN), GRAN), :] = part
        return carry

    lax.fori_loop(0, 8, step, 0)


def w_in(wbuf, j):
    return wbuf[0:24, 32 * j : 32 * (j + 1), :].reshape(D, D)


def w_out(wbuf):
    return wbuf[24:32].reshape(D, D)


def w_shrink(wbuf, j):
    return wbuf[64 + 8 * j : 72 + 8 * j].reshape(D, D)


def expander():
    r, c = iota((32, 16), 0), iota((32, 16), 1)
    return ((r < 24) & ((r & 1) == c)).astype(BF16)


def head_mask():
    r, lane = iota((32, D), 0), iota((32, D), 1)
    return (r < 24) & ((r >> 1) == (lane >> 6))


def spread(expand, mask, rows):
    return jnp.where(mask, nn(expand, rows), 0.0).astype(BF16)


def first_forward(
    info, u_ref, *refs
):
    pieces = diagonals = refs[:32]
    y_out, xh1_o, rs1_o, xh2_o, rs2_o, gp_o, e_o, h_o, att_o, u_o, q_o, pu_o, qk_o, p_o, vec, vbuf, wflat, w1, sem = refs[32:]
    wait_vecs, wait = fill(info, pieces, diagonals, 0, wflat, vbuf, sem)
    wbuf = wflat.reshape(GRANS, GRAN, D)
    start = info[5]
    u = u_ref[...]
    r, t = iota((16, TOK), 0), iota((16, TOK), 1)
    picker = (((r == 0) & (t == 0)) | ((r == 1) & (t == start))).astype(BF16)
    cls = nn(picker, u)
    cls16 = cls.astype(BF16)
    expand, mask = expander(), head_mask()
    r, t = iota((32, TOK), 0), iota((32, TOK), 1)
    inside = (t >= start).astype(jnp.int32) == (r & 1)
    real = r < 24
    wait_vecs()
    order_vec(vbuf, 0, vec)
    wait(0)
    q = (nn(cls16, w_in(wbuf, 0)) + vec[V_BQ : V_BQ + 1, :]).astype(BF16)
    qk = nt(spread(expand, mask, q), w_in(wbuf, 1)).astype(BF16)
    scores = jnp.where(inside, nt(qk, u) * HEAD_DIM**-0.5, masked_score)
    raised = jnp.exp(scores - jnp.max(scores, axis=-1, keepdims=True))
    portions = jnp.where(real, raised / jnp.sum(raised, axis=-1, keepdims=True), 0.0)
    low = portions.astype(BF16)
    pu = nn(low, u).astype(BF16)
    weight = jnp.sum(low.astype(F32), axis=-1, keepdims=True)
    heads = nn(pu, w_in(wbuf, 2)) + weight * vec[V_BV : V_BV + 1, :]
    att = tn(expand, jnp.where(mask, heads, 0.0).astype(BF16)).astype(BF16)
    wait(1)
    xhat, rstd = norm_forward(cls + nn(att, w_out(wbuf)) + vec[V_BO : V_BO + 1, :])
    xh1_o[...] = xhat
    rs1_o[...] = jnp.broadcast_to(rstd, (16, 128))
    h = xhat * vec[V_G1 : V_G1 + 1, :] + vec[V_C1 : V_C1 + 1, :]
    h16 = h.astype(BF16)
    f = vec[V_B2 : V_B2 + 1, :]
    wait(2)
    split_w1(wbuf, w1)
    wait(3)
    for j in range(4):
        e, gp = gelu_both(nn(h16, w1[j]) + vec[V_B1 + j : V_B1 + j + 1, :])
        e = e.astype(BF16)
        e_o[j] = e
        gp_o[j] = gp
        f = f + nn(e, w_shrink(wbuf, j))
    xhat, rstd = norm_forward(h + f)
    xh2_o[...] = xhat
    rs2_o[...] = jnp.broadcast_to(rstd, (16, 128))
    y_out[...] = xhat * vec[V_G2 : V_G2 + 1, :] + vec[V_C2 : V_C2 + 1, :]
    h_o[...] = h16
    att_o[...] = att
    u_o[...] = cls16
    q_o[...] = q
    pu_o[...] = pu
    qk_o[...] = qk
    p_o[...] = portions


def first_backward(
    info, u_ref, cls_all, dz, vg1, xh1, rs1, xh2, rs2, gp_i, e_i, h_i, att_i, ucls, q_i, pu_i, qk_i, p_i, *refs
):
    pieces = diagonals = refs[:32]
    tg_out, pay_out, loss_out, vec, vbuf, wflat, w1, rows16, dcls, pay, sem = refs[32:]
    wait_vecs, wait = fill(info, pieces, diagonals, 0, wflat, vbuf, sem)
    wbuf = wflat.reshape(GRANS, GRAN, D)
    start = info[5]
    u = u_ref[...]
    keys = cls_all[...]
    n_keys = keys.shape[0]
    scale = 2.0 / math.sqrt(D)
    r, c = iota((n_keys, n_keys), 0), iota((n_keys, n_keys), 1)
    scores = jnp.where(r == c, masked_score, nt(keys, keys) * scale)
    top = jnp.max(scores, axis=-1, keepdims=True)
    raised = jnp.exp(scores - top)
    total = jnp.sum(raised, axis=-1, keepdims=True)
    partner = jnp.bitwise_xor(r, 2) == c
    positive = jnp.sum(jnp.where(partner, scores, 0.0), axis=-1, keepdims=True)
    terms = top + jnp.log(total) - positive
    loss_out[...] = jnp.broadcast_to(colsum(terms) * (1.0 / n_keys), (8, 128))
    pull = (raised / total - partner.astype(F32)).astype(BF16)
    dcls[...] = (nn(pull, keys) + tn(pull, keys)) * scale
    rows16[...] = jnp.zeros((16, D), F32)
    rows16[0:1, :] = dz[0:1, :] + dcls[pl.ds(2 * info[0], 1), :]
    rows16[1:2, :] = dz[pl.ds(start, 1), :] + dcls[pl.ds(2 * info[0] + 1, 1), :]
    dy = rows16[...]
    wait_vecs()
    order_vec(vbuf, 0, vec)
    for plane in range(4):
        wait(plane)
    split_w1(wbuf, w1)
    xhat = xh2[...]
    pay[R_VEC + 14 : R_VEC + 15, :] = colsum(dy * xhat)
    pay[R_VEC + 15 : R_VEC + 16, :] = colsum(dy)
    dr2 = norm_backward(dy, vec[V_G2 : V_G2 + 1, :], xhat, rs2[:, 0:1])
    df = dr2.astype(BF16)
    pay[R_DF : R_DF + 2, :] = df.astype(F32)[0:2, :]
    dh = dr2
    for j in range(4):
        da = (gp_i[j] * nt(df, w_shrink(wbuf, j))).astype(BF16)
        pay[R_E + 2 * j : R_E + 2 * j + 2, :] = e_i[j].astype(F32)[0:2, :]
        pay[R_DA + 2 * j : R_DA + 2 * j + 2, :] = da.astype(F32)[0:2, :]
        dh = dh + nt(da, w1[j])
    xhat = xh1[...]
    pay[R_VEC + 12 : R_VEC + 13, :] = colsum(dh * xhat)
    pay[R_VEC + 13 : R_VEC + 14, :] = colsum(dh)
    dr1 = norm_backward(dh, vec[V_G1 : V_G1 + 1, :], xhat, rs1[:, 0:1])
    do = dr1.astype(BF16)
    datt = nt(do, w_out(wbuf)).astype(BF16)
    expand, mask = expander(), head_mask()
    portions = p_i[...]
    low = portions.astype(BF16)
    each = spread(expand, mask, datt)
    dvk = nt(each, w_in(wbuf, 2)).astype(BF16)
    constant = jnp.sum(each.astype(F32) * vec[V_BV : V_BV + 1, :], axis=-1, keepdims=True)
    dp = nt(dvk, u) + constant
    ds = (portions * (dp - jnp.sum(dp * portions, axis=-1, keepdims=True))).astype(BF16)
    dsu = nn(ds, u)
    part = jnp.where(mask, nn(dsu.astype(BF16), w_in(wbuf, 1)) * HEAD_DIM**-0.5, 0.0).astype(BF16)
    dq = tn(expand, part).astype(BF16)
    rows16[...] = dr1 + nt(dq, w_in(wbuf, 0))
    du = tn(ds, qk_i[...]) * HEAD_DIM**-0.5 + tn(low, dvk)
    is_cls = (iota((TOK, 1), 0) == 0) | (iota((TOK, 1), 0) == start)
    tg_out[...] = du + jnp.where(is_cls, 0.0, dz[...])
    tg_out[0:1, :] = tg_out[0:1, :] + rows16[0:1, :]
    tg_out[pl.ds(start, 1), :] = tg_out[pl.ds(start, 1), :] + rows16[1:2, :]
    for row, rows in ((R_H, h_i), (R_ATT, att_i), (R_U, ucls), (R_Q, q_i)):
        pay[row : row + 2, :] = rows[...].astype(F32)[0:2, :]
    for row, rows in ((R_DO, do), (R_DQ, dq), (R_DATT, datt)):
        pay[row : row + 2, :] = rows.astype(F32)[0:2, :]
    pay[R_WK : R_WK + 24, :] = dsu[0:24, :] * HEAD_DIM**-0.5
    pay[R_PU : R_PU + 24, :] = pu_i[...].astype(F32)[0:24, :]
    pay[R_VEC : R_VEC + 12, :] = vg1[0:12, :]
    pay_out[...] = pay[...].astype(BF16)


def lanes(p):
    return pl.ds(pl.multiple_of(128 * p, 128), 128)


def send_groups(info, grads, planes, outs, sem):
    sends = []
    for other in (1, 0):
        for i, t in enumerate(planes):
            for kind, parts in ((3, ((SY + 144 * i, 0), (SX + 144 * i, 144))),
                                (1, ((QX + 144 * i, 0), (SX + 288 + 144 * i, 144))),
                                (2, ((SY + 288 + 144 * i, 0), (QY + 144 * i, 144))),
                                (0, ((OWN + 288 * i, 0),))):
                dev = owner(info, t, kind, other)
                rows = 288 if kind == 0 else 144
                for to, lo in parts:
                    source = grads.at[pl.ds(pl.multiple_of(288 * dev + lo, 16), rows)]
                    sends.append(pltpu.make_async_copy(source, outs[1 - other][to // HALF].at[pl.ds(to % HALF, rows)], sem.at[len(sends)]))
                    sends[-1].start()
    return sends


def second_block(info, u_ref, cot_ref, y_ref, *refs):
    pieces = refs[:32]
    diagonals = {4 * i + 3: refs[32 + i] for i in range(8)}
    head_out, dr_out, vg_out, zb, qs, ks, vs, att = refs[40:48]
    pm_out, w1_grad, theirs1, theirs2, mine1, mine2 = refs[48:54]
    (vec, vbuf, wflat, w1, grads, zf, pm, xh1, hb, ht, gp, es, das, xh2, acc, stage, dfs, sem, osem) = refs[54:]
    wait_vecs, wait = fill(info, pieces, diagonals, 1, wflat, vbuf, sem)
    wbuf = wflat.reshape(GRANS, GRAN, D)
    gbuf = grads.reshape(GRANS, GRAN, D)
    start = info[5]
    zf[...] = u_ref[...].astype(F32)
    zf[0:1, :] = y_ref[0:1, :]
    zf[pl.ds(start, 1), :] = y_ref[1:2, :]
    z16 = zf[...].astype(BF16)
    zb[...] = z16
    wait_vecs()
    order_vec(vbuf, 1, vec)
    wait(0)
    qs[...] = (nn(z16, w_in(wbuf, 0)) + vec[V_BQ : V_BQ + 1, :]).astype(BF16)
    ks[...] = nn(z16, w_in(wbuf, 1)).astype(BF16)
    vs[...] = (nn(z16, w_in(wbuf, 2)) + vec[V_BV : V_BV + 1, :]).astype(BF16)
    low_lane = iota((TOK, 128), 1) < HEAD_DIM
    same = (iota((TOK, TOK), 0) >= start) == (iota((TOK, TOK), 1) >= start)

    def attend(p, carry):
        qp, kp, vp = qs[:, lanes(p)], ks[:, lanes(p)], vs[:, lanes(p)]
        res = []
        for hh in range(2):
            qm = jnp.where(low_lane == (hh == 0), qp, jnp.zeros_like(qp))
            s = jnp.where(same, nt(qm, kp) * HEAD_DIM**-0.5, masked_score)
            raised = jnp.exp(s - jnp.max(s, axis=-1, keepdims=True))
            portions = raised / jnp.sum(raised, axis=-1, keepdims=True)
            pm[2 * p + hh] = portions
            res.append(nn(portions.astype(BF16), vp))
        att[:, lanes(p)] = jnp.where(low_lane, res[0], res[1]).astype(BF16)
        return carry

    lax.fori_loop(0, 6, attend, 0)
    saved = [pltpu.make_async_copy(pm, pm_out, osem.at[28])]
    saved[0].start()
    wait(1)
    xhat, rstd1 = norm_forward(zf[...] + (nn(att[...], w_out(wbuf)) + vec[V_BO : V_BO + 1, :]))
    xh1[...] = xhat
    h = xhat * vec[V_G1 : V_G1 + 1, :] + vec[V_C1 : V_C1 + 1, :]
    hb[...] = h.astype(BF16)
    ht[...] = h.T.astype(BF16)
    acc[...] = h + vec[V_B2 : V_B2 + 1, :]
    wait(2)
    split_w1(wbuf, w1)
    wait(3)
    for j in range(4):
        e, slope = gelu_both(nn(hb[...], w1[j]) + vec[V_B1 + j : V_B1 + j + 1, :])
        gp[j] = slope
        e = e.astype(BF16)
        es[j] = e
        acc[...] += nn(e, w_shrink(wbuf, j))
    xhat, rstd2 = norm_forward(acc[...])
    xh2[...] = xhat
    head_out[...] = (xhat * vec[V_G2 : V_G2 + 1, :] + vec[V_C2 : V_C2 + 1, :]).astype(BF16)

    vg_out[...] = jnp.zeros((16, D), F32)
    dy = cot_ref[...].astype(F32)
    vg_out[V_G2 : V_G2 + 1, :] = colsum(dy * xh2[...])
    vg_out[V_C2 : V_C2 + 1, :] = colsum(dy)
    dr = norm_backward(dy, vec[V_G2 : V_G2 + 1, :], xh2[...], rstd2)
    acc[...] = dr
    df = dr.astype(BF16)
    dfs[...] = df
    vg_out[V_B2 : V_B2 + 1, :] = colsum(df.astype(F32))
    for j in range(4):
        df = dfs[...]
        gbuf[64 + 8 * j : 72 + 8 * j] = tn(es[j], df).astype(BF16).reshape(8, GRAN, D)
        da = (gp[j] * nt(df, w_shrink(wbuf, j))).astype(BF16)
        das[j] = da
        vg_out[V_B1 + j : V_B1 + j + 1, :] = colsum(da.astype(F32))
        acc[...] += nt(da, w1[j])

    def expand_grad(i, carry):
        rows = ht[pl.ds(pl.multiple_of(192 * i, 192), 192), :]
        for j in range(4):
            stage[:, 24 * j : 24 * (j + 1), :] = nn(rows, das[j]).reshape(8, 24, D)
        gbuf[pl.ds(32 + 8 * i, 8)] = stage[...].astype(BF16)
        return carry

    lax.fori_loop(0, 4, expand_grad, 0)
    saved.append(pltpu.make_async_copy(grads.at[pl.ds(3072, 1536)], w1_grad, osem.at[29]))
    saved[1].start()
    saved += send_groups(info, grads, GROUPS[0], ((theirs1, theirs2), (mine1, mine2)), osem)
    dh = acc[...]
    vg_out[V_G1 : V_G1 + 1, :] = colsum(dh * xh1[...])
    vg_out[V_C1 : V_C1 + 1, :] = colsum(dh)
    dr_out[...] = norm_backward(dh, vec[V_G1 : V_G1 + 1, :], xh1[...], rstd1)
    for copy in saved:
        copy.wait()


def second_attention(info, dr, vg_in, zb, qs, ks, vs, att, *refs):
    pieces = refs[:32]
    pm_in, w1_grad, dz_out, vg_out, theirs1, theirs2, mine1, mine2, wflat, grads, pm, datt, dqs, dks, dvs, sem = refs[32:]
    wbuf = wflat.reshape(GRANS // 2, GRAN, D)
    gbuf = grads.reshape(GRANS // 2, GRAN, D)
    waits = []
    for other in (0, 1):
        for k in range(4):
            for kind in range(4):
                i = 16 * other + 4 * k + kind
                dev = owner(info, (info[1] + 4 - k) & 3, kind, other)
                source = pieces[i].at[pl.ds(SEND_ONE if kind < 3 else 0, 288)]
                rows = pl.ds(pl.multiple_of(288 * jnp.minimum(dev, 15), 16), 288)
                copy = pltpu.make_async_copy(source, wflat.at[rows], sem.at[i])
                used = dev < 11
                pl.when(used)(copy.start)
                waits.append((used, copy))
    saved = [
        pltpu.make_async_copy(pm_in, pm, sem.at[32]),
        pltpu.make_async_copy(w1_grad, grads.at[pl.ds(3072, 1536)], sem.at[33]),
    ]
    for copy in saved:
        copy.start()
    vg_out[...] = vg_in[...]
    do = dr[...].astype(BF16)
    vg_out[V_BO : V_BO + 1, :] = colsum(do.astype(F32))
    gbuf[24:32] = tn(att[...], do).astype(BF16).reshape(8, GRAN, D)
    for used, copy in waits:
        pl.when(used)(copy.wait)
    datt[...] = nt(do, w_out(wbuf)).astype(BF16)
    saved[0].wait()
    low_lane = iota((TOK, 128), 1) < HEAD_DIM

    def attend_back(p, carry):
        qp, kp, vp, dp_ = qs[:, lanes(p)], ks[:, lanes(p)], vs[:, lanes(p)], datt[:, lanes(p)]
        dq, dk, dv = [], [], []
        for hh in range(2):
            portions = pm[2 * p + hh]
            dam = jnp.where(low_lane == (hh == 0), dp_, jnp.zeros_like(dp_))
            dp = nt(dam, vp)
            dv.append(tn(portions.astype(BF16), dp_))
            ds = (portions * (dp - jnp.sum(dp * portions, axis=-1, keepdims=True))).astype(BF16)
            dq.append(nn(ds, kp))
            dk.append(tn(ds, qp))
        dqs[:, lanes(p)] = (jnp.where(low_lane, dq[0], dq[1]) * HEAD_DIM**-0.5).astype(BF16)
        dks[:, lanes(p)] = (jnp.where(low_lane, dk[0], dk[1]) * HEAD_DIM**-0.5).astype(BF16)
        dvs[:, lanes(p)] = jnp.where(low_lane, dv[0], dv[1]).astype(BF16)
        return carry

    lax.fori_loop(0, 6, attend_back, 0)
    vg_out[V_BQ : V_BQ + 1, :] = colsum(dqs[...].astype(F32))
    vg_out[V_BV : V_BV + 1, :] = colsum(dvs[...].astype(F32))
    dz = dr[...]
    for j, part in enumerate((dqs, dks, dvs)):
        gbuf[0:24, 32 * j : 32 * (j + 1), :] = tn(zb[...], part[...]).astype(BF16).reshape(24, 32, D)
    saved[1].wait()
    sends = send_groups(info, grads, GROUPS[1], ((theirs1, theirs2), (mine1, mine2)), sem)
    for j, part in enumerate((dqs, dks, dvs)):
        dz = dz + nt(part[...], w_in(wbuf, j))
    dz_out[...] = dz
    for copy in sends:
        copy.wait()


def total_kernel(own, over_x, over_y, last_x, last_y, first, second):
    for i, out in enumerate((first, second)):
        part = slice(144 * i, 144 * (i + 1))
        for half, (one, two) in enumerate(((last_x, over_y), (over_x, last_y))):
            mine = own[288 * i + 144 * half : 288 * i + 144 * (half + 1), :].astype(F32)
            out[144 * half : 144 * (half + 1), :] = (
                mine + one[part, :].astype(F32) + two[part, :].astype(F32)
            ).astype(BF16)


def owner_grad(info, *refs):
    pieces = refs[:10]
    out, vec_out, pbuf, abuf, qbuf, sem = refs[10:]
    copies = []
    at = 0
    for i, piece in enumerate(pieces):
        copies.append(pltpu.make_async_copy(piece, pbuf.at[pl.ds(at, piece.shape[0])], sem.at[i]))
        at += piece.shape[0]
    for c in copies:
        c.start()
    for c in copies:
        c.wait()
    n_rows = 32 * PAY
    each = pbuf.reshape(32, PAY, D)
    r, c = iota((PAY, n_rows), 0), iota((PAY, n_rows), 1)
    place = c - PAY * ((c * 43691) >> 22)
    tot = nn((place == r).astype(BF16), pbuf[...])
    for row, first in [(V_BQ, R_DQ), (V_BV, R_DATT), (V_BO, R_DO), (V_B2, R_DF)] + [
        (V_B1 + j, R_DA + 2 * j) for j in range(4)
    ]:
        vec_out[row : row + 1, :] = tot[first : first + 1, :] + tot[first + 1 : first + 2, :]
    vec_out[V_G1 : V_C1 + 1, :] = tot[R_VEC + 12 : R_VEC + 14, :]
    vec_out[V_G2 : V_C2 + 1, :] = tot[R_VEC + 14 : R_VEC + 16, :]
    vec_out[12:24, :] = tot[R_VEC : R_VEC + 12, :]

    def pick_rows(*firsts):
        r, c = iota((64, n_rows), 0), iota((64, n_rows), 1)
        base = PAY * (r >> 1) + (r & 1)
        select = jnp.concatenate([(c == base + first).astype(BF16) for first in firsts], 0)
        got = nn(select, pbuf[...]).astype(BF16)
        return [got[64 * i : 64 * (i + 1), :] for i in range(len(firsts))]

    def chosen(count, offset, source):
        one_hot = (iota((count, D), 1) == iota((count, D), 0) + offset).astype(BF16)
        return nt(one_hot, source).astype(BF16)

    def put(gi, n, p, value):
        m = GRAN // n
        for j in range(6):
            out[pl.ds(6 * (GRAN * gi + p) + j, m, stride=6 * n), :] = value[:, 128 * j : 128 * (j + 1)]

    @pl.when(info[0] < 8)
    def _():
        off = GRAN * info[0]
        ucls, dq, q, datt = pick_rows(R_U, R_DQ, R_Q, R_DATT)
        parts = [nn(chosen(GRAN, off, ucls), dq)]
        r, c = iota((D, 64), 0), iota((D, 64), 1)
        inside = r - 24 * (c >> 1)
        expand = ((inside >= 0) & (inside < 24) & ((r & 1) == (c & 1))).astype(BF16)
        r = iota((D, D), 0)
        mine = (r - 24 * ((r * 2731) >> 16)) >> 1 == iota((D, D), 1) >> 6
        for right, lo, skip in ((q, 32, 0), (datt, 48, 8)):
            qbuf[...] = jnp.where(mine, nn(expand, right), 0.0).astype(BF16)

            def compact(i, carry, lo=lo, skip=skip):
                rows = each[pl.ds(8 * i, 8), lo : lo + 32, :].astype(F32)
                abuf[pl.ds(pl.multiple_of(192 * i, 192), 192), :] = (
                    rows[:, skip : skip + 24, :].reshape(192, D).astype(BF16)
                )
                return carry

            lax.fori_loop(0, 4, compact, 0)
            parts.append(nn(chosen(GRAN, off, abuf[...]), qbuf[...]))
        for gi in range(3):
            for p in range(3):
                put(gi, 3, p, parts[p][32 * gi : 32 * (gi + 1), :])

    for gi in range(3):
        g = 3 * info[0] + gi

        @pl.when((g >= 24) & (g < 32))
        def _(gi=gi, g=g):
            left, right = pick_rows(R_ATT, R_DO)
            put(gi, 1, 0, nn(chosen(GRAN, GRAN * (g - 24), left), right))

        @pl.when((g >= 32) & (g < 64))
        def _(gi=gi, g=g):
            left, *rights = pick_rows(R_H, *[R_DA + 2 * p for p in range(4)])
            left = chosen(32, 24 * (g - 32), left)
            for p in range(4):
                put(gi, 4, p, nn(left, rights[p])[0:24, :])

        @pl.when(g >= 64)
        def _(gi=gi, g=g):
            left, right = pick_rows(R_E + 2 * ((g - 64) >> 3), R_DF)
            put(gi, 1, 0, nn(chosen(GRAN, GRAN * ((g - 64) & 7), left), right))


def join_grads(info, g0, a, b, gv, out, square, buf):
    g = g0[...]
    out[pl.ds(0, 1728, stride=2), :] = g
    buf[...] = a[...].astype(F32) + b[...].astype(F32)
    total = buf[...]
    sq = jnp.sum((g * g).reshape(216, 8, 128), axis=0)
    for j in range(6):
        v = total[:, 128 * j : 128 * (j + 1)]
        sq = sq + jnp.sum((v * v).reshape(36, 8, 128), axis=0)
    whole = jnp.sum(colsum(sq), axis=1, keepdims=True)
    whole = whole + jnp.sum(colsum(gv[...] * gv[...]), axis=1, keepdims=True)
    square[...] = jnp.broadcast_to(whole, (8, 128))
    for gi in range(3):

        def emit(n, gi=gi):
            m = GRAN // n
            for p in range(n):
                for j in range(6):
                    out[pl.ds(12 * (GRAN * gi + p) + 2 * j + 1, m, stride=12 * n), :] = buf[
                        GRAN * gi + m * p : GRAN * gi + m * (p + 1), 128 * j : 128 * (j + 1)
                    ]

        by_kind(3 * info[0] + gi, emit)


def adamw_kernel(sq, w, m, v, g, vw, vm, vv, vg, w_new, m_new, v_new, vw_new, vm_new, vv_new, norm_out):
    norm = jnp.sqrt(sq[...])
    norm_out[0, 0] = norm[0, 0]
    coef = jnp.minimum(1.0, math.sqrt(2 * (PL + QL)) / (norm[0:1, 0:1] + 1e-06))
    w_new[...], m_new[...], v_new[...] = adamw_update(w[...], m[...], v[...], g[...] * coef, 0.1, weight_decay)
    vw_new[...], vm_new[...], vv_new[...] = adamw_update(vw[...], vm[...], vv[...], vg[...] * coef, 0.5, 0.0)


def adamw_update(weight, moment_one, moment_two, gradient, step_rate, decay_rate):
    first_new = beta_one * moment_one + (1.0 - beta_one) * gradient
    second_new = beta_two * moment_two + (1.0 - beta_two) * gradient * gradient
    first_hat = first_new / (1.0 - beta_one**STEP)
    second_hat = second_new / (1.0 - beta_two**STEP)
    weight_new = weight - step_rate * (first_hat / (jnp.sqrt(second_hat) + adam_epsilon) + decay_rate * weight)
    return (weight_new, first_new, second_new)


def order_kernel(info, a3, a2, own, over_x, over_y, last_x, last_y, o1, o2, o3, o0, acc):
    acc[3], acc[2] = a3[...], a2[...]
    total_kernel(own, over_x, over_y, last_x, last_y, acc.at[1], acc.at[0])
    for k, out in enumerate((o1, o2, o3, o0)):
        out[...] = acc[(info[1] + 3 - k) & 3]


SMEM = pl.BlockSpec(memory_space=pltpu.SMEM)
VMEM = pl.BlockSpec(memory_space=pltpu.VMEM)
ANY = pl.BlockSpec(memory_space=pl.ANY)


def struct(*shape, dtype=F32):
    return jax.ShapeDtypeStruct(shape, dtype)


def call(kernel, name, ins, in_specs, outs, out_specs, scratch=(), flops=0, moved=0):
    return pl.pallas_call(
        kernel,
        out_shape=outs,
        in_specs=in_specs,
        out_specs=out_specs,
        scratch_shapes=list(scratch),
        name=name,
        compiler_params=pltpu.CompilerParams(vmem_limit_bytes=VMEM_BYTES),
        cost_estimate=pl.CostEstimate(flops=flops, bytes_accessed=moved, transcendentals=0),
    )(*ins)


def flat_view(a):
    return a.reshape(2, -1, 128).transpose(1, 0, 2).reshape(-1, 128)


def flat_back(a):
    return a.reshape(-1, 2, 128).transpose(1, 0, 2).reshape(2, -1)


def body(tokens, cotangent, lengths, mats, mats_m, mats_v, vecs, vecs_m, vecs_v):
    dp, pair = lax.axis_index("dp"), lax.axis_index("pair")
    device = 2 * dp + pair
    z = dp >> 2
    info = jnp.stack(
        [device, z, (dp >> 1) & 1, dp & 1, pair, lengths[0, 0, 0], jnp.int32(0), jnp.int32(0)]
    ).astype(jnp.int32)
    u = tokens[0]
    cot = cotangent[0]
    flat = flat_view(mats)
    own = call(pack_kernel, "pack", (info, flat, vecs), [SMEM, VMEM, VMEM], struct(SEND, D, dtype=BF16), VMEM)
    pieces0, pieces1 = gather_blocks(own)
    row = struct(16, D)
    row16 = struct(16, D, dtype=BF16)
    saved_shapes = (
        row, struct(16, 128), row, struct(16, 128), struct(4, 16, D), struct(4, 16, D, dtype=BF16),
        row16, row16, row16, row16, struct(32, D, dtype=BF16), struct(32, D, dtype=BF16), struct(32, TOK),
    )
    weights = [
        pltpu.VMEM((16, D), F32),
        pltpu.VMEM((32, 16, D), BF16),
        pltpu.VMEM((GRANS * GRAN, D), BF16),
        pltpu.VMEM((4, D, D), BF16),
    ]
    y_cls, *saved = call(
        first_forward,
        "first_forward",
        (info, u, *pieces0),
        [SMEM, VMEM] + [ANY] * 32,
        (row, *saved_shapes),
        (VMEM,) * 14,
        weights + [pltpu.SemaphoreType.DMA((64,))],
        flops=2 * 32 * PL,
        moved=2 * PL,
    )
    part = struct(HALF, D, dtype=BF16)
    mid16 = pltpu.VMEM((TOK, D), BF16)
    mid = pltpu.VMEM((TOK, D), F32)
    low = struct(TOK, D, dtype=BF16)
    head_out, dr, vg1, zb, qs, ks, vs, att, pm, w1_grad, theirs_a1, theirs_a2, mine_a1, mine_a2 = call(
        second_block,
        "second_block",
        (info, u, cot, y_cls, *pieces1, *pieces0[3::4]),
        [SMEM, VMEM, VMEM, VMEM] + [ANY] * 40,
        (low, struct(TOK, D), row, low, low, low, low, low, struct(HEADS, TOK, TOK), struct(1536, D, dtype=BF16)) + (part,) * 4,
        (VMEM,) * 8 + (ANY,) * 6,
        weights
        + [
            pltpu.VMEM((GRANS * GRAN, D), BF16),
            mid,
            pltpu.VMEM((HEADS, TOK, TOK), F32),
            mid, mid16,
            pltpu.VMEM((D, TOK), BF16),
            pltpu.VMEM((4, TOK, D), F32),
            pltpu.VMEM((4, TOK, D), BF16),
            pltpu.VMEM((4, TOK, D), BF16),
            mid, mid,
            pltpu.VMEM((8, GRAN, D), F32),
            mid16,
            pltpu.SemaphoreType.DMA((64,)),
            pltpu.SemaphoreType.DMA((30,)),
        ],
        flops=4 * TOK * PL,
        moved=4 * PL,
    )

    def first_part(mine, came):
        return [add16(mine[lo:hi], came[lo:hi]) for lo, hi in ((SX, SY), (SY, QX))]

    def second_part(mine, came):
        return [
            add16(mine[lo - HALF : hi - HALF], came[lo - HALF : hi - HALF])
            for lo, hi in ((QX, QY), (QY, OWN), (OWN, GROUP_ROWS))
        ]

    def plane_total(own, over_x, over_y, last_x, last_y):
        whole, half = pl.BlockSpec((576, D), lambda i: (0, 0)), pl.BlockSpec((288, D), lambda i: (0, 0))
        second = pl.BlockSpec((288, D), lambda i: (1, 0))
        return pl.pallas_call(
            total_kernel,
            grid=(1,),
            in_specs=[whole, second, second, half, half],
            out_specs=[half, half],
            out_shape=[struct(288, D, dtype=BF16)] * 2,
            name="total",
        )(own, over_x, over_y, last_x, last_y)

    cls = gather_step(y_cls[0:2].astype(BF16), 0, device)()
    theirs_a1, theirs_a2, cls = fence([theirs_a1, theirs_a2, cls])
    came_a1, came_a2 = core_flip(theirs_a1), core_flip(theirs_a2)
    cls = gather_step(cls, 1, device)()
    sx, sy, cls, dr = fence([*first_part(mine_a1, came_a1), cls, dr])
    over_xa, over_ya = x_flip(sx), y_flip(sy)
    qx_a, qy_a, own_a = second_part(mine_a2, came_a2)
    dz, vg1, theirs_b1, theirs_b2, mine_b1, mine_b2 = call(
        second_attention,
        "second_attention",
        (info, dr, vg1, zb, qs, ks, vs, att, *pieces1, pm, w1_grad),
        [SMEM] + [VMEM] * 7 + [ANY] * 34,
        (struct(TOK, D), row) + (part,) * 4,
        (VMEM, VMEM) + (ANY,) * 4,
        [
            pltpu.VMEM((GRANS * GRAN // 2, D), BF16),
            pltpu.VMEM((GRANS * GRAN // 2, D), BF16),
            pltpu.VMEM((HEADS, TOK, TOK), F32),
            mid16, mid16, mid16, mid16,
            pltpu.SemaphoreType.DMA((34,)),
        ],
        flops=2 * TOK * PL,
        moved=2 * PL,
    )
    qx_a, qy_a, theirs_b1, theirs_b2, cls = fence(
        [add16(qx_a, over_ya[:288]), add16(qy_a, over_xa[:288]), theirs_b1, theirs_b2, cls]
    )
    last_xa, last_ya = x_flip(qx_a), y_flip(qy_a)
    came_b1, came_b2 = core_flip(theirs_b1), core_flip(theirs_b2)
    every_cls = gather_step(cls, 2, device)()
    sx, sy, dz = fence([*first_part(mine_b1, came_b1), dz])
    over_xb, over_yb = x_flip(sx), y_flip(sy)
    qx_b, qy_b, own_b = second_part(mine_b2, came_b2)
    token_grad, payload, loss = call(
        first_backward,
        "first_backward",
        (info, u, every_cls, dz, vg1, *saved, *pieces0),
        [SMEM] + [VMEM] * 17 + [ANY] * 32,
        (struct(TOK, D), struct(PAY, D, dtype=BF16), struct(8, 128)),
        (VMEM,) * 3,
        weights
        + [
            pltpu.VMEM((16, D), F32),
            pltpu.VMEM((64, D), F32),
            pltpu.VMEM((PAY, D), F32),
            pltpu.SemaphoreType.DMA((64,)),
        ],
        flops=2 * 32 * PL,
        moved=2 * PL,
    )
    qx_b, qy_b, pay, last_xa, last_ya = fence(
        [add16(qx_b, over_yb[:288]), add16(qy_b, over_xb[:288]), payload, last_xa, last_ya]
    )
    last_xb, last_yb = x_flip(qx_b), y_flip(qy_b)
    a3, a2 = plane_total(own_a, over_xa, over_ya, last_xa, last_ya)
    slots = jnp.concatenate([pay, z_turn(pay, 1), z_turn(pay, 3), z_turn(pay, 2)], 0)
    whole, half = pl.BlockSpec((576, D), lambda i: (0, 0)), pl.BlockSpec((288, D), lambda i: (0, 0))
    second = pl.BlockSpec((288, D), lambda i: (1, 0))
    in_turn = pl.pallas_call(
        order_kernel,
        grid=(1,),
        in_specs=[SMEM, half, half, whole, second, second, half, half],
        out_specs=[half] * 4,
        out_shape=[struct(288, D, dtype=BF16)] * 4,
        scratch_shapes=[pltpu.VMEM((4, 288, D), BF16)],
        name="order",
    )(info, a3, a2, own_b, over_xb, over_yb, last_xb, last_yb)
    moving, slots = fence([in_turn[0], slots])
    moving = z_up(moving)
    over_x, over_y = x_flip(slots), y_flip(slots)
    rows = [slots, over_x, over_y]
    moving, *rows = fence([add16(in_turn[1], moving), *rows])
    moving = z_up(moving)
    half = rows[0].shape[0] // 2
    rows += [y_flip(rows[1][:half]), x_flip(rows[2][half:])]
    rows += [core_flip(v) for v in rows]
    [moving] = fence([add16(in_turn[2], moving)])
    moving = z_up(moving)
    flat0, vec_sum = call(
        owner_grad,
        "owner_grad",
        (info, *rows),
        [SMEM] + [ANY] * 10,
        (struct(1728, 128), struct(24, D)),
        (VMEM, VMEM),
        [
            pltpu.VMEM((32 * PAY, D), BF16),
            pltpu.VMEM((D, D), BF16),
            pltpu.VMEM((D, D), BF16),
            pltpu.SemaphoreType.DMA((10,)),
        ],
        flops=2 * 768 * 768 * 768,
        moved=2 * 32 * PAY * D,
    )
    grad_vecs = lax.dynamic_slice(vec_sum.reshape(2, QL), (0, device * vecs.shape[1]), vecs.shape)
    grads, square = call(
        join_grads,
        "join_grads",
        (info, flat0, in_turn[3], moving, grad_vecs),
        [SMEM] + [VMEM] * 4,
        (struct(3456, 128), struct(8, 128)),
        (VMEM, VMEM),
        [pltpu.VMEM((288, D), F32)],
    )
    block = pl.BlockSpec((864, 128), lambda i: (i, 0))
    small = pl.BlockSpec(vecs.shape, lambda i: (0, 0))
    tile = pl.BlockSpec((8, 128), lambda i: (0, 0))
    *new, new_vecs, new_vecs_m, new_vecs_v, norm = pl.pallas_call(
        adamw_kernel,
        grid=(4,),
        in_specs=[tile] + [block] * 4 + [small] * 4,
        out_specs=(block,) * 3 + (small,) * 3 + (SMEM,),
        out_shape=(struct(3456, 128),) * 3 + (struct(*vecs.shape),) * 3 + (struct(1, 1),),
        name="adamw",
    )(sum_quick(square), flat, flat_view(mats_m), flat_view(mats_v), grads, vecs, vecs_m, vecs_v, grad_vecs)
    new_mats, new_mats_m, new_mats_v = [flat_back(a) for a in new]
    return (
        head_out[None],
        token_grad[None],
        loss[0, 0],
        norm.reshape(()),
        new_mats,
        new_mats_m,
        new_mats_v,
        new_vecs,
        new_vecs_m,
        new_vecs_v,
    )


def matmul(left_side, right_side):
    return jnp.dot(left_side, right_side, preferred_element_type=jnp.float32)


def inner_rows(left_side, right_side):
    return lax.dot_general(
        left_side, right_side, (((0,), (0,)), ((), ())), preferred_element_type=jnp.float32
    )


def outer_cols(left_side, right_side):
    return lax.dot_general(
        left_side, right_side, (((1,), (1,)), ((), ())), preferred_element_type=jnp.float32
    )


def exact_dot(left_side, right_side):
    return jnp.dot(
        left_side, right_side, precision=lax.Precision.HIGHEST, preferred_element_type=jnp.float32
    )


def layer_norm(resid, gain, shift):
    centred = resid - jnp.mean(resid, axis=-1, keepdims=True)
    spread = jnp.mean(centred * centred, axis=-1, keepdims=True)
    return centred * lax.rsqrt(spread + norm_epsilon) * gain + shift


def gelu_exact(before):
    return jax.nn.gelu(before, approximate=False)


def unpack(mat_row, vec_row):
    edge_one = 3 * D * D
    edge_two = 4 * D * D
    edge_three = edge_two + D * FF
    input_weight = mat_row[:edge_one].reshape(D, 3 * D)
    output_weight = mat_row[edge_one:edge_two].reshape(D, D)
    expand_weight = mat_row[edge_two:edge_three].reshape(D, FF)
    shrink_weight = mat_row[edge_three:].reshape(FF, D)
    vector = vec_row.astype(jnp.float32)
    pieces = []
    cursor = 0
    for piece_len in (D, D, D, D, D, FF, D, D, D):
        pieces.append(vector[cursor : cursor + piece_len])
        cursor = cursor + piece_len
    return (input_weight, output_weight, expand_weight, shrink_weight) + tuple(pieces)


def head_scores(queries, key_rows, same_span):
    row_count = queries.shape[0]
    query_heads = queries.reshape(row_count, HEADS, HEAD_DIM)
    key_heads = key_rows.reshape(row_count, HEADS, HEAD_DIM)
    scores = jnp.einsum(
        "thd,shd->hts", query_heads, key_heads, preferred_element_type=jnp.float32
    ) * HEAD_DIM ** (-0.5)
    return jnp.where(same_span[None, :, :], scores, masked_score)


def layer_forward(params, inputs, same_span):
    (
        input_weight,
        output_weight,
        expand_weight,
        shrink_weight,
        query_bias,
        value_bias,
        output_bias,
        first_gain,
        first_shift,
        expand_bias,
        shrink_bias,
        second_gain,
        second_shift,
    ) = params
    row_count = inputs.shape[0]
    low_input = inputs.astype(jnp.bfloat16)
    joint = matmul(low_input, input_weight)
    queries = (joint[:, :D] + query_bias).astype(jnp.bfloat16)
    key_rows = joint[:, D : 2 * D].astype(jnp.bfloat16)
    values = (joint[:, 2 * D :] + value_bias).astype(jnp.bfloat16)
    scores = head_scores(queries, key_rows, same_span)
    row_max = jnp.max(scores, axis=-1, keepdims=True)
    raised = jnp.exp(scores - row_max)
    summed = jnp.sum(raised, axis=-1, keepdims=True)
    portions = raised / summed
    logsum = row_max + jnp.log(summed)
    value_heads = values.reshape(row_count, HEADS, HEAD_DIM)
    attended = jnp.einsum(
        "hts,shd->thd",
        portions.astype(jnp.bfloat16),
        value_heads,
        preferred_element_type=jnp.float32,
    )
    attended = attended.reshape(row_count, D).astype(jnp.bfloat16)
    resid_one = inputs + (matmul(attended, output_weight) + output_bias)
    hidden = layer_norm(resid_one, first_gain, first_shift)
    low_hidden = hidden.astype(jnp.bfloat16)
    before = matmul(low_hidden, expand_weight) + expand_bias
    activated = gelu_exact(before).astype(jnp.bfloat16)
    resid_two = hidden + (matmul(activated, shrink_weight) + shrink_bias)
    output = layer_norm(resid_two, second_gain, second_shift)
    kept = (
        low_input,
        queries,
        key_rows,
        values,
        logsum,
        attended,
        resid_one,
        low_hidden,
        before,
        activated,
        resid_two,
    )
    return (output, kept)


def layer_backward(params, kept, grad_out, same_span):
    (
        input_weight,
        output_weight,
        expand_weight,
        shrink_weight,
        query_bias,
        value_bias,
        output_bias,
        first_gain,
        first_shift,
        expand_bias,
        shrink_bias,
        second_gain,
        second_shift,
    ) = params
    (
        low_input,
        queries,
        key_rows,
        values,
        logsum,
        attended,
        resid_one,
        low_hidden,
        before,
        activated,
        resid_two,
    ) = kept
    row_count = low_input.shape[0]
    _, norm_pull_two = jax.vjp(layer_norm, resid_two, second_gain, second_shift)
    d_resid_two, d_second_gain, d_second_shift = norm_pull_two(grad_out)
    d_feed = d_resid_two.astype(jnp.bfloat16)
    d_shrink = inner_rows(activated, d_feed)
    d_shrink_bias = jnp.sum(d_feed.astype(jnp.float32), axis=0)
    _, gelu_pull = jax.vjp(gelu_exact, before)
    d_before = gelu_pull(outer_cols(d_feed, shrink_weight))[0].astype(jnp.bfloat16)
    d_expand = inner_rows(low_hidden, d_before)
    d_expand_bias = jnp.sum(d_before.astype(jnp.float32), axis=0)
    d_hidden = d_resid_two + outer_cols(d_before, expand_weight)
    _, norm_pull_one = jax.vjp(layer_norm, resid_one, first_gain, first_shift)
    d_resid_one, d_first_gain, d_first_shift = norm_pull_one(d_hidden)
    d_branch = d_resid_one.astype(jnp.bfloat16)
    d_output = inner_rows(attended, d_branch)
    d_output_bias = jnp.sum(d_branch.astype(jnp.float32), axis=0)
    d_attended = outer_cols(d_branch, output_weight).astype(jnp.bfloat16)
    portions = jnp.exp(head_scores(queries, key_rows, same_span) - logsum)
    query_heads = queries.reshape(row_count, HEADS, HEAD_DIM)
    key_heads = key_rows.reshape(row_count, HEADS, HEAD_DIM)
    value_heads = values.reshape(row_count, HEADS, HEAD_DIM)
    d_att_heads = d_attended.reshape(row_count, HEADS, HEAD_DIM)
    d_portions = jnp.einsum(
        "thd,shd->hts", d_att_heads, value_heads, preferred_element_type=jnp.float32
    )
    d_values = jnp.einsum(
        "hts,thd->shd",
        portions.astype(jnp.bfloat16),
        d_att_heads,
        preferred_element_type=jnp.float32,
    )
    d_values = d_values.reshape(row_count, D).astype(jnp.bfloat16)
    d_scores = portions * (d_portions - jnp.sum(d_portions * portions, axis=-1, keepdims=True))
    d_scores = d_scores.astype(jnp.bfloat16)
    score_scale = HEAD_DIM ** (-0.5)
    d_queries = (
        jnp.einsum("hts,shd->thd", d_scores, key_heads, preferred_element_type=jnp.float32)
        * score_scale
    )
    d_queries = d_queries.reshape(row_count, D).astype(jnp.bfloat16)
    d_keys = (
        jnp.einsum("hts,thd->shd", d_scores, query_heads, preferred_element_type=jnp.float32)
        * score_scale
    )
    d_keys = d_keys.reshape(row_count, D).astype(jnp.bfloat16)
    d_joint = jnp.concatenate([d_queries, d_keys, d_values], axis=1)
    d_input_weight = inner_rows(low_input, d_joint)
    d_query_bias = jnp.sum(d_queries.astype(jnp.float32), axis=0)
    d_value_bias = jnp.sum(d_values.astype(jnp.float32), axis=0)
    d_inputs = d_resid_one + outer_cols(d_joint, input_weight)
    mat_grad = jnp.concatenate(
        [
            d_input_weight.reshape(-1),
            d_output.reshape(-1),
            d_expand.reshape(-1),
            d_shrink.reshape(-1),
        ]
    )
    vec_grad = jnp.concatenate(
        [
            d_query_bias,
            d_value_bias,
            d_output_bias,
            d_first_gain,
            d_first_shift,
            d_expand_bias,
            d_shrink_bias,
            d_second_gain,
            d_second_shift,
        ]
    )
    return (d_inputs, mat_grad, vec_grad)


def contrast_rows(anchors, key_table, anchor_index, span_count, score_scale):
    key_count = key_table.shape[0]
    key_index = jnp.arange(key_count, dtype=jnp.int32)
    scores = outer_cols(anchors, key_table) * score_scale
    scores = jnp.where(anchor_index[:, None] == key_index[None, :], masked_score, scores)
    partner = (
        jnp.bitwise_xor(anchor_index // span_count, 1) * span_count + anchor_index % span_count
    )
    row_max = jnp.max(scores, axis=-1, keepdims=True)
    raised = jnp.exp(scores - row_max)
    summed = jnp.sum(raised, axis=-1, keepdims=True)
    logsum = row_max[:, 0] + jnp.log(summed[:, 0])
    target = key_index[None, :] == partner[:, None]
    positive = jnp.sum(jnp.where(target, scores, 0.0), axis=1)
    grads_low = (raised / summed - target.astype(jnp.float32)).astype(jnp.bfloat16)
    return (grads_low, logsum - positive)


def general_body(tokens, cotangent, lengths, mats, mats_m, mats_v, vecs, vecs_m, vecs_v):
    full_mats, full_vecs = (
        lax.all_gather(mats.astype(jnp.bfloat16), ("dp", "pair"), axis=1, tiled=True),
        lax.all_gather(vecs.astype(jnp.bfloat16), ("dp", "pair"), axis=1, tiled=True),
    )
    layer_one = unpack(full_mats[0], full_vecs[0])
    layer_two = unpack(full_mats[1], full_vecs[1])
    inputs = tokens[0].astype(jnp.float32)
    row_count = inputs.shape[0]
    span_lengths = lengths[0, 0]
    span_count = span_lengths.shape[0]
    positions = jnp.arange(row_count, dtype=jnp.int32)
    order = jnp.arange(span_count)
    starts = jnp.sum(jnp.where(order[None, :] < order[:, None], span_lengths[None, :], 0), axis=1)
    span_of = jnp.sum((positions[:, None] >= starts[None, :]).astype(jnp.int32), axis=1)
    same_span = span_of[:, None] == span_of[None, :]
    heads_mark = positions[None, :] == starts[:, None]
    is_cls = jnp.any(heads_mark, axis=0)[:, None]
    picker = heads_mark.astype(jnp.float32)
    doc_groups = lax.axis_size("dp")
    early_out, kept_one = layer_forward(layer_one, inputs, same_span)
    cls_rows = exact_dot(picker, early_out)
    mixture = jnp.where(is_cls, early_out, inputs)
    late_out, kept_two = layer_forward(layer_two, mixture, same_span)
    sent_cls = cls_rows.astype(jnp.bfloat16)
    every_cls = lax.all_gather(sent_cls, ("dp", "pair"), axis=0, tiled=True)
    key_count = every_cls.shape[0]
    score_scale = 2.0 / math.sqrt(D)
    offset = lax.axis_index(("dp", "pair")) * span_count
    own_index = offset + jnp.arange(span_count, dtype=jnp.int32)
    grads_low, loss_terms = contrast_rows(sent_cls, every_cls, own_index, span_count, score_scale)
    anchor_part = matmul(grads_low, every_cls) * score_scale
    key_part = lax.psum_scatter(
        inner_rows(grads_low, sent_cls) * score_scale,
        ("dp", "pair"),
        scatter_dimension=0,
        tiled=True,
    )
    cls_grad = anchor_part + key_part
    grad_late = cotangent[0].astype(jnp.float32)
    d_mixture, late_mats, late_vecs = layer_backward(layer_two, kept_two, grad_late, same_span)
    grad_early = jnp.where(is_cls, d_mixture, 0.0) + exact_dot(picker.T, cls_grad)
    d_inputs, early_mats, early_vecs = layer_backward(layer_one, kept_one, grad_early, same_span)
    token_grad = d_inputs + jnp.where(is_cls, 0.0, d_mixture)
    all_pieces = (
        lax.all_to_all(
            early_mats.reshape(doc_groups, -1).astype(jnp.bfloat16),
            "dp",
            split_axis=0,
            concat_axis=0,
            tiled=True,
        ).astype(jnp.float32),
        lax.all_to_all(
            late_mats.reshape(doc_groups, -1).astype(jnp.bfloat16),
            "dp",
            split_axis=0,
            concat_axis=0,
            tiled=True,
        ).astype(jnp.float32),
        lax.all_to_all(
            early_vecs.reshape(doc_groups, -1).astype(jnp.bfloat16),
            "dp",
            split_axis=0,
            concat_axis=0,
            tiled=True,
        ).astype(jnp.float32),
        lax.all_to_all(
            late_vecs.reshape(doc_groups, -1).astype(jnp.bfloat16),
            "dp",
            split_axis=0,
            concat_axis=0,
            tiled=True,
        ).astype(jnp.float32),
    )
    early_mats_part, late_mats_part, early_vecs_part, late_vecs_part = (
        lax.psum_scatter(
            jnp.sum(all_pieces[0], axis=0).astype(jnp.bfloat16),
            "pair",
            scatter_dimension=0,
            tiled=True,
        ).astype(jnp.float32),
        lax.psum_scatter(
            jnp.sum(all_pieces[1], axis=0).astype(jnp.bfloat16),
            "pair",
            scatter_dimension=0,
            tiled=True,
        ).astype(jnp.float32),
        lax.psum_scatter(
            jnp.sum(all_pieces[2], axis=0).astype(jnp.bfloat16),
            "pair",
            scatter_dimension=0,
            tiled=True,
        ).astype(jnp.float32),
        lax.psum_scatter(
            jnp.sum(all_pieces[3], axis=0).astype(jnp.bfloat16),
            "pair",
            scatter_dimension=0,
            tiled=True,
        ).astype(jnp.float32),
    )
    grad_mats = jnp.stack([early_mats_part, late_mats_part])
    grad_vecs = jnp.stack([early_vecs_part, late_vecs_part])
    square_sum = jnp.sum(grad_mats * grad_mats) + jnp.sum(grad_vecs * grad_vecs)
    total_sq, loss_sum = lax.psum((square_sum, jnp.sum(loss_terms)), ("dp", "pair"))
    grad_norm = jnp.sqrt(total_sq)
    clip_factor = jnp.minimum(1.0, math.sqrt(2 * (PL + QL)) / (grad_norm + 1e-06))
    new_mats, new_mats_m, new_mats_v = adamw_update(
        mats, mats_m, mats_v, grad_mats * clip_factor, 0.1, weight_decay
    )
    new_vecs, new_vecs_m, new_vecs_v = adamw_update(
        vecs, vecs_m, vecs_v, grad_vecs * clip_factor, 0.5, 0.0
    )
    contrastive = loss_sum / key_count
    return (
        late_out.astype(jnp.bfloat16)[None],
        token_grad[None],
        contrastive,
        grad_norm,
        new_mats,
        new_mats_m,
        new_mats_v,
        new_vecs,
        new_vecs_m,
        new_vecs_v,
    )


def solution(mesh):
    flat = P(None, ("dp", "pair"))
    rows = P("pair", "dp", None)
    here = dict(mesh.shape) == {"dp": 16, "pair": 2}
    return jax.shard_map(
        body if here else general_body,
        mesh=mesh,
        in_specs=(rows, rows, rows) + (flat,) * 6,
        out_specs=(rows, rows, P(), P()) + (flat,) * 6,
        check_vma=False,
    )
```

```python
import math

import jax
import jax.numpy as jnp
from jax import lax
from jax.experimental import pallas as pl
from jax.experimental.pallas import tpu as pltpu
from jax.sharding import PartitionSpec as P

D = 768
HEADS = 12
HEAD_DIM = 64
FF = 3072
STEP = 10
PL = 7077888
QL = 9216

norm_epsilon = 1e-12
masked_score = -1000000000.0
beta_one = 0.9
beta_two = 0.999
adam_epsilon = 1e-08
weight_decay = 0.01

F32 = jnp.float32
BF16 = jnp.bfloat16
TOK = 256
GRAN = 96
GRANS = PL // D // GRAN
VMEM_BYTES = 63_000_000

V_BQ, V_BV, V_BO, V_G1, V_C1, V_B1, V_B2, V_G2, V_C2 = 0, 1, 2, 3, 4, 5, 9, 10, 11

R_E, R_DF, R_H, R_DA, R_ATT, R_DO, R_U, R_DQ, R_Q, R_DATT, R_WK, R_PU, R_VEC = (
    0, 8, 10, 12, 20, 22, 24, 26, 28, 30, 32, 56, 80,
)
PAY = 96


def nn(a, b):
    return lax.dot_general(a, b, (((1,), (0,)), ((), ())), preferred_element_type=F32)


def nt(a, b):
    return lax.dot_general(a, b, (((1,), (1,)), ((), ())), preferred_element_type=F32)


def tn(a, b):
    return lax.dot_general(a, b, (((0,), (0,)), ((), ())), preferred_element_type=F32)


def iota(shape, axis):
    return lax.broadcasted_iota(jnp.int32, shape, axis)


def erf(x):
    x = jnp.clip(x, -3.832506856900711, 3.832506856900711)
    s = x * x
    top = 0.00022905065861350646
    for c in (0.0034082910107109506, 0.050955695062380861, 0.18520832239976145, 1.128379143519084):
        top = top * s + c
    low = -1.1791602954361697e-7
    for c in (
        0.000023547966471313185,
        0.0010179625278914885,
        0.014070470171167667,
        0.11098505178285362,
        0.49746925110067538,
        1.0,
    ):
        low = low * s + c
    return x * top / low


def gelu_both(a):
    phi = 0.5 + 0.5 * erf(a * math.sqrt(0.5))
    return a * phi, phi + a * jnp.exp(-0.5 * a * a) * (1.0 / math.sqrt(2.0 * math.pi))


def norm_forward(r):
    centred = r - jnp.mean(r, axis=-1, keepdims=True)
    rstd = lax.rsqrt(jnp.mean(centred * centred, axis=-1, keepdims=True) + norm_epsilon)
    return centred * rstd, rstd


def norm_backward(dy, gain, xhat, rstd):
    dx = dy * gain
    return rstd * (
        dx - jnp.mean(dx, axis=-1, keepdims=True) - xhat * jnp.mean(dx * xhat, axis=-1, keepdims=True)
    )


def colsum(v):
    return jnp.sum(v, axis=0, keepdims=True)


def flip(v, axis, bit):
    return lax.ppermute(v, axis, [(i, i ^ bit) for i in range(lax.axis_size(axis))])


def core_flip(v):
    return flip(v, "dp", 1)


def x_flip(v):
    return flip(v, "dp", 2)


def y_flip(v):
    return flip(v, "pair", 1)


def z_up(v):
    n = lax.axis_size("dp")
    return lax.ppermute(v, "dp", [(i, (i + 4) % n) for i in range(n)])


def z_turn(v, places):
    n = lax.axis_size("dp")
    return lax.ppermute(v, "dp", [(i, (i + 4 * places) % n) for i in range(n)])


def xor_flip(v, pair_bit, dp_bits):
    if not pair_bit:
        return flip(v, "dp", dp_bits)
    n = lax.axis_size("dp")
    return lax.ppermute(v, ("dp", "pair"), [(i, i ^ (2 * dp_bits + 1)) for i in range(2 * n)])


def fence(values):
    return list(lax.optimization_barrier(tuple(values)))


SMALL_STEPS = (((1, 0), (0, 1), (1, 1)), ((0, 2), (0, 4), (0, 6)), ((0, 8),))


def gather_step(v, step, device):
    got = [v] + [xor_flip(v, *bits) for bits in SMALL_STEPS[step]]
    here = (device >> (2 * step)) & (len(got) - 1)
    return lambda: jnp.concatenate([pick(here ^ p, got) for p in range(len(got))], 0)


SUM_STEPS = (((0, 1),), ((1, 0), (0, 2), (1, 2)), ((0, 4), (0, 8), (0, 12)))


def sum_quick(v):
    for bits in SUM_STEPS:
        got = [v] + [xor_flip(v, *b) for b in bits]
        v = got[0] + got[1] if len(got) == 2 else (got[0] + got[1]) + (got[2] + got[3])
    return v


def pick(index, cases):
    return lax.select_n(index, *cases)


GATHER_ROUNDS = (
    ("x0", "y0", "s1"),
    ("d0", "e0", "x1", "y1", "s2"),
    ("d1", "e1", "x2", "y2", "s3"),
    ("d2", "e2", "x3", "y3"),
    ("d3", "e3"),
)


SEND_VEC, SEND_ONE, SEND = 288, 304, 592


def gather_blocks(own):
    have = {"s0": own}
    across = ["s0"]
    for r, tasks in enumerate(GATHER_ROUNDS):
        sources = {}
        for name in tasks:
            kind, k = name[0], int(name[1])
            sources[name] = {"s": f"s{k - 1}", "x": f"s{k}", "y": f"s{k}", "d": f"x{k}", "e": f"y{k}"}[kind]
        names = list(dict.fromkeys([*sources.values(), *across]))
        if r:
            have.update(zip(names, fence([have[i] for i in names])))
        for name, source in sources.items():
            move = {
                "s": z_up, "x": x_flip, "y": y_flip, "d": lambda v: y_flip(v[:SEND_ONE]), "e": lambda v: x_flip(v[SEND_ONE:])
            }[name[0]]
            have[name] = move(have[source])
        if 0 < r < 4:
            names = [*across, *tasks[:2]]
            have.update(zip(names, fence([have[i] for i in names])))
        for i in across:
            have["c" + i] = core_flip(have[i])
        across = list(tasks)
    for i in across:
        have["c" + i] = core_flip(have[i])
    return [[have[c + kind + str(k)] for c in ("", "c") for k in range(4) for kind in kinds] for kinds in ("sxyd", "sxye")]


def add16(a, b):
    return (a.astype(F32) + b.astype(F32)).astype(BF16)


GROUPS = ((3, 2), (1, 0))
GROUP_ROWS = 2304
HALF = 1152
SX, SY, QX, QY, OWN = 0, 576, 1152, 1440, 1728


def by_kind(granule, emit):
    joint = granule < 24
    wide = (granule >= 32) & (granule < 64)
    pl.when(joint)(lambda: emit(3))
    pl.when(wide)(lambda: emit(4))
    pl.when(jnp.logical_not(joint | wide))(lambda: emit(1))


def pack_kernel(info, flat, vecs, out):
    out[SEND_VEC:SEND_ONE, :] = jnp.zeros((SEND_ONE - SEND_VEC, D), BF16)
    both = vecs[...]
    out[SEND_VEC:SEND_ONE, 0:288] = jnp.concatenate([both, jnp.zeros((14, 288), F32)], 0).astype(BF16)
    for gi in range(3):

        def emit(n, gi=gi):
            m = GRAN // n
            for layer in range(2):
                for j in range(6):
                    parts = [
                        flat[pl.ds(12 * (GRAN * gi + p) + 2 * j + layer, m, stride=12 * n), :] for p in range(n)
                    ]
                    tile = parts[0] if n == 1 else jnp.concatenate(parts, 0)
                    at = SEND_ONE * layer + GRAN * gi
                    out[at : at + GRAN, 128 * j : 128 * (j + 1)] = tile.astype(BF16)

        by_kind(3 * info[0] + gi, emit)


def owner(info, plane, kind, other):
    return (
        8 * plane
        + 4 * jnp.bitwise_xor(info[2], kind & 1)
        + 2 * jnp.bitwise_xor(info[3], other)
        + jnp.bitwise_xor(info[4], kind >> 1)
    )


def fill(info, pieces, diagonals, block, wbuf, vbuf, sem):
    vecs = []
    for other in (0, 1):
        for k in range(4):
            for kind in range(4):
                i = 16 * other + 4 * k + kind
                source = (pieces if kind < 3 else diagonals)[i].at[pl.ds(SEND_VEC, 16)]
                dev = owner(info, (info[1] + 4 - k) & 3, kind, other)
                vecs.append(pltpu.make_async_copy(source, vbuf.at[dev], sem.at[32 + i]))
    for copy in vecs:
        copy.start()

    def copies(plane, k):
        made = []
        for other in (0, 1):
            for kind in range(4):
                source = pieces[16 * other + 4 * k + kind].at[pl.ds(SEND_ONE if block and kind < 3 else 0, 288)]
                rows = pl.ds(pl.multiple_of(288 * owner(info, plane, kind, other), 16), 288)
                made.append(pltpu.make_async_copy(source, wbuf.at[rows], sem.at[8 * plane + 2 * kind + other]))
        return made

    for plane in range(4):
        for k in range(4):

            @pl.when(((info[1] + 4 - plane) & 3) == k)
            def _(plane=plane, k=k):
                for copy in copies(plane, k):
                    copy.start()

    def wait_vecs():
        for copy in vecs:
            copy.wait()

    def wait(plane):
        for copy in copies(plane, 0):
            copy.wait()

    return wait_vecs, wait


def order_vec(vbuf, block, vec):
    every = vbuf[:, 0:2, :].astype(F32)
    for q in range(QL // GRAN):
        to, lo = GRAN * (q % 8), GRAN * (q % 3)
        vec[q // 8 : q // 8 + 1, to : to + GRAN] = every[q // 3, block : block + 1, lo : lo + GRAN]


def split_w1(wbuf, w1):
    def step(i, carry):
        rows = wbuf[pl.ds(32 + 4 * i, 4)].astype(F32)
        for j in range(4):
            part = rows[:, 24 * j : 24 * (j + 1), :].reshape(GRAN, D).astype(BF16)
            w1[j, pl.ds(pl.multiple_of(GRAN * i, GRAN), GRAN), :] = part
        return carry

    lax.fori_loop(0, 8, step, 0)


def w_in(wbuf, j):
    return wbuf[0:24, 32 * j : 32 * (j + 1), :].reshape(D, D)


def w_out(wbuf):
    return wbuf[24:32].reshape(D, D)


def w_shrink(wbuf, j):
    return wbuf[64 + 8 * j : 72 + 8 * j].reshape(D, D)


def expander():
    r, c = iota((32, 16), 0), iota((32, 16), 1)
    return ((r < 24) & ((r & 1) == c)).astype(BF16)


def head_mask():
    r, lane = iota((32, D), 0), iota((32, D), 1)
    return (r < 24) & ((r >> 1) == (lane >> 6))


def spread(expand, mask, rows):
    return jnp.where(mask, nn(expand, rows), 0.0).astype(BF16)


def first_forward(
    info, u_ref, *refs
):
    pieces = diagonals = refs[:32]
    y_out, xh1_o, rs1_o, xh2_o, rs2_o, gp_o, e_o, h_o, att_o, u_o, q_o, pu_o, qk_o, p_o, vec, vbuf, wflat, w1, sem = refs[32:]
    wait_vecs, wait = fill(info, pieces, diagonals, 0, wflat, vbuf, sem)
    wbuf = wflat.reshape(GRANS, GRAN, D)
    start = info[5]
    u = u_ref[...]
    r, t = iota((16, TOK), 0), iota((16, TOK), 1)
    picker = (((r == 0) & (t == 0)) | ((r == 1) & (t == start))).astype(BF16)
    cls = nn(picker, u)
    cls16 = cls.astype(BF16)
    expand, mask = expander(), head_mask()
    r, t = iota((32, TOK), 0), iota((32, TOK), 1)
    inside = (t >= start).astype(jnp.int32) == (r & 1)
    real = r < 24
    wait_vecs()
    order_vec(vbuf, 0, vec)
    wait(0)
    q = (nn(cls16, w_in(wbuf, 0)) + vec[V_BQ : V_BQ + 1, :]).astype(BF16)
    qk = nt(spread(expand, mask, q), w_in(wbuf, 1)).astype(BF16)
    scores = jnp.where(inside, nt(qk, u) * HEAD_DIM**-0.5, masked_score)
    raised = jnp.exp(scores - jnp.max(scores, axis=-1, keepdims=True))
    portions = jnp.where(real, raised / jnp.sum(raised, axis=-1, keepdims=True), 0.0)
    low = portions.astype(BF16)
    pu = nn(low, u).astype(BF16)
    weight = jnp.sum(low.astype(F32), axis=-1, keepdims=True)
    heads = nn(pu, w_in(wbuf, 2)) + weight * vec[V_BV : V_BV + 1, :]
    att = tn(expand, jnp.where(mask, heads, 0.0).astype(BF16)).astype(BF16)
    wait(1)
    xhat, rstd = norm_forward(cls + nn(att, w_out(wbuf)) + vec[V_BO : V_BO + 1, :])
    xh1_o[...] = xhat
    rs1_o[...] = jnp.broadcast_to(rstd, (16, 128))
    h = xhat * vec[V_G1 : V_G1 + 1, :] + vec[V_C1 : V_C1 + 1, :]
    h16 = h.astype(BF16)
    f = vec[V_B2 : V_B2 + 1, :]
    wait(2)
    split_w1(wbuf, w1)
    wait(3)
    for j in range(4):
        e, gp = gelu_both(nn(h16, w1[j]) + vec[V_B1 + j : V_B1 + j + 1, :])
        e = e.astype(BF16)
        e_o[j] = e
        gp_o[j] = gp
        f = f + nn(e, w_shrink(wbuf, j))
    xhat, rstd = norm_forward(h + f)
    xh2_o[...] = xhat
    rs2_o[...] = jnp.broadcast_to(rstd, (16, 128))
    y_out[...] = xhat * vec[V_G2 : V_G2 + 1, :] + vec[V_C2 : V_C2 + 1, :]
    h_o[...] = h16
    att_o[...] = att
    u_o[...] = cls16
    q_o[...] = q
    pu_o[...] = pu
    qk_o[...] = qk
    p_o[...] = portions


def first_backward(
    info, u_ref, cls_all, dz, vg1, xh1, rs1, xh2, rs2, gp_i, e_i, h_i, att_i, ucls, q_i, pu_i, qk_i, p_i, *refs
):
    pieces = diagonals = refs[:32]
    tg_out, pay_out, loss_out, vec, vbuf, wflat, w1, rows16, dcls, pay, sem = refs[32:]
    wait_vecs, wait = fill(info, pieces, diagonals, 0, wflat, vbuf, sem)
    wbuf = wflat.reshape(GRANS, GRAN, D)
    start = info[5]
    u = u_ref[...]
    keys = cls_all[...]
    n_keys = keys.shape[0]
    scale = 2.0 / math.sqrt(D)
    r, c = iota((n_keys, n_keys), 0), iota((n_keys, n_keys), 1)
    scores = jnp.where(r == c, masked_score, nt(keys, keys) * scale)
    top = jnp.max(scores, axis=-1, keepdims=True)
    raised = jnp.exp(scores - top)
    total = jnp.sum(raised, axis=-1, keepdims=True)
    partner = jnp.bitwise_xor(r, 2) == c
    positive = jnp.sum(jnp.where(partner, scores, 0.0), axis=-1, keepdims=True)
    terms = top + jnp.log(total) - positive
    loss_out[0, 0] = jnp.sum(terms) * (1.0 / n_keys)
    pull = (raised / total - partner.astype(F32)).astype(BF16)
    dcls[...] = (nn(pull, keys) + tn(pull, keys)) * scale
    rows16[...] = jnp.zeros((16, D), F32)
    rows16[0:1, :] = dz[0:1, :] + dcls[pl.ds(2 * info[0], 1), :]
    rows16[1:2, :] = dz[pl.ds(start, 1), :] + dcls[pl.ds(2 * info[0] + 1, 1), :]
    dy = rows16[...]
    wait_vecs()
    order_vec(vbuf, 0, vec)
    for plane in range(4):
        wait(plane)
    split_w1(wbuf, w1)
    xhat = xh2[...]
    pay[R_VEC + 14 : R_VEC + 15, :] = colsum(dy * xhat)
    pay[R_VEC + 15 : R_VEC + 16, :] = colsum(dy)
    dr2 = norm_backward(dy, vec[V_G2 : V_G2 + 1, :], xhat, rs2[:, 0:1])
    df = dr2.astype(BF16)
    pay[R_DF : R_DF + 2, :] = df.astype(F32)[0:2, :]
    dh = dr2
    for j in range(4):
        da = (gp_i[j] * nt(df, w_shrink(wbuf, j))).astype(BF16)
        pay[R_E + 2 * j : R_E + 2 * j + 2, :] = e_i[j].astype(F32)[0:2, :]
        pay[R_DA + 2 * j : R_DA + 2 * j + 2, :] = da.astype(F32)[0:2, :]
        dh = dh + nt(da, w1[j])
    xhat = xh1[...]
    pay[R_VEC + 12 : R_VEC + 13, :] = colsum(dh * xhat)
    pay[R_VEC + 13 : R_VEC + 14, :] = colsum(dh)
    dr1 = norm_backward(dh, vec[V_G1 : V_G1 + 1, :], xhat, rs1[:, 0:1])
    do = dr1.astype(BF16)
    datt = nt(do, w_out(wbuf)).astype(BF16)
    expand, mask = expander(), head_mask()
    portions = p_i[...]
    low = portions.astype(BF16)
    each = spread(expand, mask, datt)
    dvk = nt(each, w_in(wbuf, 2)).astype(BF16)
    constant = jnp.sum(each.astype(F32) * vec[V_BV : V_BV + 1, :], axis=-1, keepdims=True)
    dp = nt(dvk, u) + constant
    ds = (portions * (dp - jnp.sum(dp * portions, axis=-1, keepdims=True))).astype(BF16)
    dsu = nn(ds, u)
    part = jnp.where(mask, nn(dsu.astype(BF16), w_in(wbuf, 1)) * HEAD_DIM**-0.5, 0.0).astype(BF16)
    dq = tn(expand, part).astype(BF16)
    rows16[...] = dr1 + nt(dq, w_in(wbuf, 0))
    du = tn(ds, qk_i[...]) * HEAD_DIM**-0.5 + tn(low, dvk)
    is_cls = (iota((TOK, 1), 0) == 0) | (iota((TOK, 1), 0) == start)
    tg_out[...] = du + jnp.where(is_cls, 0.0, dz[...])
    tg_out[0:1, :] = tg_out[0:1, :] + rows16[0:1, :]
    tg_out[pl.ds(start, 1), :] = tg_out[pl.ds(start, 1), :] + rows16[1:2, :]
    for row, rows in ((R_H, h_i), (R_ATT, att_i), (R_U, ucls), (R_Q, q_i)):
        pay[row : row + 2, :] = rows[...].astype(F32)[0:2, :]
    for row, rows in ((R_DO, do), (R_DQ, dq), (R_DATT, datt)):
        pay[row : row + 2, :] = rows.astype(F32)[0:2, :]
    pay[R_WK : R_WK + 24, :] = dsu[0:24, :] * HEAD_DIM**-0.5
    pay[R_PU : R_PU + 24, :] = pu_i[...].astype(F32)[0:24, :]
    pay[R_VEC : R_VEC + 12, :] = vg1[0:12, :]
    pay_out[...] = pay[...].astype(BF16)


def lanes(p):
    return pl.ds(pl.multiple_of(128 * p, 128), 128)


def send_groups(info, grads, planes, outs, sem):
    sends = []
    for other in (1, 0):
        for i, t in enumerate(planes):
            for kind, parts in ((3, ((SY + 144 * i, 0), (SX + 144 * i, 144))),
                                (1, ((QX + 144 * i, 0), (SX + 288 + 144 * i, 144))),
                                (2, ((SY + 288 + 144 * i, 0), (QY + 144 * i, 144))),
                                (0, ((OWN + 288 * i, 0),))):
                dev = owner(info, t, kind, other)
                rows = 288 if kind == 0 else 144
                for to, lo in parts:
                    source = grads.at[pl.ds(pl.multiple_of(288 * dev + lo, 16), rows)]
                    sends.append(pltpu.make_async_copy(source, outs[1 - other][to // HALF].at[pl.ds(to % HALF, rows)], sem.at[len(sends)]))
                    sends[-1].start()
    return sends


def second_block(info, u_ref, cot_ref, y_ref, *refs):
    pieces = refs[:32]
    diagonals = {4 * i + 3: refs[32 + i] for i in range(8)}
    head_out, dr_out, vg_out, zb, qs, ks, vs, att = refs[40:48]
    pm_out, w1_grad, theirs1, theirs2, mine1, mine2 = refs[48:54]
    (vec, vbuf, wflat, w1, grads, zf, pm, xh1, hb, ht, gp, es, das, xh2, acc, stage, dfs, sem, osem) = refs[54:]
    wait_vecs, wait = fill(info, pieces, diagonals, 1, wflat, vbuf, sem)
    wbuf = wflat.reshape(GRANS, GRAN, D)
    gbuf = grads.reshape(GRANS, GRAN, D)
    start = info[5]
    zf[...] = u_ref[...].astype(F32)
    zf[0:1, :] = y_ref[0:1, :]
    zf[pl.ds(start, 1), :] = y_ref[1:2, :]
    z16 = zf[...].astype(BF16)
    zb[...] = z16
    wait_vecs()
    order_vec(vbuf, 1, vec)
    wait(0)
    qs[...] = (nn(z16, w_in(wbuf, 0)) + vec[V_BQ : V_BQ + 1, :]).astype(BF16)
    ks[...] = nn(z16, w_in(wbuf, 1)).astype(BF16)
    vs[...] = (nn(z16, w_in(wbuf, 2)) + vec[V_BV : V_BV + 1, :]).astype(BF16)
    low_lane = iota((TOK, 128), 1) < HEAD_DIM
    same = (iota((TOK, TOK), 0) >= start) == (iota((TOK, TOK), 1) >= start)

    def attend(p, carry):
        qp, kp, vp = qs[:, lanes(p)], ks[:, lanes(p)], vs[:, lanes(p)]
        res = []
        for hh in range(2):
            qm = jnp.where(low_lane == (hh == 0), qp, jnp.zeros_like(qp))
            s = jnp.where(same, nt(qm, kp) * HEAD_DIM**-0.5, masked_score)
            raised = jnp.exp(s - jnp.max(s, axis=-1, keepdims=True))
            portions = raised / jnp.sum(raised, axis=-1, keepdims=True)
            pm[2 * p + hh] = portions
            res.append(nn(portions.astype(BF16), vp))
        att[:, lanes(p)] = jnp.where(low_lane, res[0], res[1]).astype(BF16)
        return carry

    lax.fori_loop(0, 6, attend, 0, unroll=True)
    saved = [pltpu.make_async_copy(pm, pm_out, osem.at[28])]
    saved[0].start()
    wait(1)
    xhat, rstd1 = norm_forward(zf[...] + (nn(att[...], w_out(wbuf)) + vec[V_BO : V_BO + 1, :]))
    xh1[...] = xhat
    h = xhat * vec[V_G1 : V_G1 + 1, :] + vec[V_C1 : V_C1 + 1, :]
    hb[...] = h.astype(BF16)
    ht[...] = h.T.astype(BF16)
    acc[...] = h + vec[V_B2 : V_B2 + 1, :]
    wait(2)
    split_w1(wbuf, w1)
    wait(3)
    for j in range(4):
        e, slope = gelu_both(nn(hb[...], w1[j]) + vec[V_B1 + j : V_B1 + j + 1, :])
        gp[j] = slope
        e = e.astype(BF16)
        es[j] = e
        acc[...] += nn(e, w_shrink(wbuf, j))
    xhat, rstd2 = norm_forward(acc[...])
    xh2[...] = xhat
    head_out[...] = (xhat * vec[V_G2 : V_G2 + 1, :] + vec[V_C2 : V_C2 + 1, :]).astype(BF16)

    vg_out[...] = jnp.zeros((16, D), F32)
    dy = cot_ref[...].astype(F32)
    vg_out[V_G2 : V_G2 + 1, :] = colsum(dy * xh2[...])
    vg_out[V_C2 : V_C2 + 1, :] = colsum(dy)
    dr = norm_backward(dy, vec[V_G2 : V_G2 + 1, :], xh2[...], rstd2)
    acc[...] = dr
    df = dr.astype(BF16)
    dfs[...] = df
    vg_out[V_B2 : V_B2 + 1, :] = colsum(df.astype(F32))
    for j in range(4):
        df = dfs[...]
        gbuf[64 + 8 * j : 72 + 8 * j] = tn(es[j], df).astype(BF16).reshape(8, GRAN, D)
        da = (gp[j] * nt(df, w_shrink(wbuf, j))).astype(BF16)
        das[j] = da
        vg_out[V_B1 + j : V_B1 + j + 1, :] = colsum(da.astype(F32))

    def expand_grad(i, carry):
        rows = ht[pl.ds(pl.multiple_of(192 * i, 192), 192), :]
        for j in range(4):
            stage[:, 24 * j : 24 * (j + 1), :] = nn(rows, das[j]).reshape(8, 24, D)
        gbuf[pl.ds(32 + 8 * i, 8)] = stage[...].astype(BF16)
        return carry

    lax.fori_loop(2, 4, expand_grad, 0)
    saved += send_groups(info, grads, GROUPS[0], ((theirs1, theirs2), (mine1, mine2)), osem)
    lax.fori_loop(0, 2, expand_grad, 0)
    saved.append(pltpu.make_async_copy(grads.at[pl.ds(3072, 1536)], w1_grad, osem.at[29]))
    saved[-1].start()
    for j in range(4):
        acc[...] += nt(das[j], w1[j])
    dh = acc[...]
    vg_out[V_G1 : V_G1 + 1, :] = colsum(dh * xh1[...])
    vg_out[V_C1 : V_C1 + 1, :] = colsum(dh)
    dr_out[...] = norm_backward(dh, vec[V_G1 : V_G1 + 1, :], xh1[...], rstd1)
    for copy in saved:
        copy.wait()


def second_attention(info, dr, vg_in, zb, qs, ks, vs, att, *refs):
    pieces = refs[:32]
    pm_in, w1_grad, dz_out, vg_out, theirs1, theirs2, mine1, mine2, wflat, grads, pm, datt, dqs, dks, dvs, sem = refs[32:]
    wbuf = wflat.reshape(GRANS // 2, GRAN, D)
    gbuf = grads.reshape(GRANS // 2, GRAN, D)
    waits = []
    for other in (0, 1):
        for k in range(4):
            for kind in range(4):
                i = 16 * other + 4 * k + kind
                dev = owner(info, (info[1] + 4 - k) & 3, kind, other)
                source = pieces[i].at[pl.ds(SEND_ONE if kind < 3 else 0, 288)]
                rows = pl.ds(pl.multiple_of(288 * jnp.minimum(dev, 15), 16), 288)
                copy = pltpu.make_async_copy(source, wflat.at[rows], sem.at[i])
                used = dev < 11
                pl.when(used)(copy.start)
                waits.append((used, copy))
    saved = [
        pltpu.make_async_copy(pm_in, pm, sem.at[32]),
        pltpu.make_async_copy(w1_grad, grads.at[pl.ds(3072, 1536)], sem.at[33]),
    ]
    for copy in saved:
        copy.start()
    vg_out[...] = vg_in[...]
    do = dr[...].astype(BF16)
    vg_out[V_BO : V_BO + 1, :] = colsum(do.astype(F32))
    gbuf[24:32] = tn(att[...], do).astype(BF16).reshape(8, GRAN, D)
    for used, copy in waits:
        pl.when(used)(copy.wait)
    datt[...] = nt(do, w_out(wbuf)).astype(BF16)
    saved[0].wait()
    low_lane = iota((TOK, 128), 1) < HEAD_DIM

    def attend_back(p, carry):
        qp, kp, vp, dp_ = qs[:, lanes(p)], ks[:, lanes(p)], vs[:, lanes(p)], datt[:, lanes(p)]
        dq, dk, dv = [], [], []
        for hh in range(2):
            portions = pm[2 * p + hh]
            dam = jnp.where(low_lane == (hh == 0), dp_, jnp.zeros_like(dp_))
            dp = nt(dam, vp)
            dv.append(tn(portions.astype(BF16), dp_))
            ds = (portions * (dp - jnp.sum(dp * portions, axis=-1, keepdims=True))).astype(BF16)
            dq.append(nn(ds, kp))
            dk.append(tn(ds, qp))
        dqs[:, lanes(p)] = (jnp.where(low_lane, dq[0], dq[1]) * HEAD_DIM**-0.5).astype(BF16)
        dks[:, lanes(p)] = (jnp.where(low_lane, dk[0], dk[1]) * HEAD_DIM**-0.5).astype(BF16)
        dvs[:, lanes(p)] = jnp.where(low_lane, dv[0], dv[1]).astype(BF16)
        return carry

    lax.fori_loop(0, 6, attend_back, 0, unroll=True)
    vg_out[V_BQ : V_BQ + 1, :] = colsum(dqs[...].astype(F32))
    vg_out[V_BV : V_BV + 1, :] = colsum(dvs[...].astype(F32))
    dz = dr[...]
    for j, part in enumerate((dqs, dks, dvs)):
        gbuf[0:24, 32 * j : 32 * (j + 1), :] = tn(zb[...], part[...]).astype(BF16).reshape(24, 32, D)
    saved[1].wait()
    sends = send_groups(info, grads, GROUPS[1], ((theirs1, theirs2), (mine1, mine2)), sem)
    for j, part in enumerate((dqs, dks, dvs)):
        dz = dz + nt(part[...], w_in(wbuf, j))
    dz_out[...] = dz
    for copy in sends:
        copy.wait()


def total_kernel(mine, came, over_x, over_y, last_x, last_y, first, second):
    for i, out in enumerate((first, second)):
        part = slice(144 * i, 144 * (i + 1))
        for half, (one, two) in enumerate(((last_x, over_y), (over_x, last_y))):
            own = slice(288 * i + 144 * half, 288 * i + 144 * (half + 1))
            both = mine[own, :].astype(F32) + came[own, :].astype(F32)
            out[144 * half : 144 * (half + 1), :] = (
                both + one[part, :].astype(F32) + two[part, :].astype(F32)
            ).astype(BF16)


def owner_grad(info, *refs):
    pieces = refs[:10]
    out, vec_out, pbuf, abuf, qbuf, sem = refs[10:]
    copies = []
    at = 0
    for i, piece in enumerate(pieces):
        copies.append(pltpu.make_async_copy(piece, pbuf.at[pl.ds(at, piece.shape[0])], sem.at[i]))
        at += piece.shape[0]
    for c in copies:
        c.start()
    for c in copies:
        c.wait()
    n_rows = 32 * PAY
    each = pbuf.reshape(32, PAY, D)
    r, c = iota((PAY, n_rows), 0), iota((PAY, n_rows), 1)
    place = c - PAY * ((c * 43691) >> 22)
    tot = nn((place == r).astype(BF16), pbuf[...])
    for row, first in [(V_BQ, R_DQ), (V_BV, R_DATT), (V_BO, R_DO), (V_B2, R_DF)] + [
        (V_B1 + j, R_DA + 2 * j) for j in range(4)
    ]:
        vec_out[row : row + 1, :] = tot[first : first + 1, :] + tot[first + 1 : first + 2, :]
    vec_out[V_G1 : V_C1 + 1, :] = tot[R_VEC + 12 : R_VEC + 14, :]
    vec_out[V_G2 : V_C2 + 1, :] = tot[R_VEC + 14 : R_VEC + 16, :]
    vec_out[12:24, :] = tot[R_VEC : R_VEC + 12, :]

    def pick_rows(*firsts):
        r, c = iota((64, n_rows), 0), iota((64, n_rows), 1)
        base = PAY * (r >> 1) + (r & 1)
        select = jnp.concatenate([(c == base + first).astype(BF16) for first in firsts], 0)
        got = nn(select, pbuf[...]).astype(BF16)
        return [got[64 * i : 64 * (i + 1), :] for i in range(len(firsts))]

    def chosen(count, offset, source):
        one_hot = (iota((count, D), 1) == iota((count, D), 0) + offset).astype(BF16)
        return nt(one_hot, source).astype(BF16)

    def put(gi, n, p, value):
        m = GRAN // n
        for j in range(6):
            out[pl.ds(6 * (GRAN * gi + p) + j, m, stride=6 * n), :] = value[:, 128 * j : 128 * (j + 1)]

    @pl.when(info[0] < 8)
    def _():
        off = GRAN * info[0]
        ucls, dq, q, datt = pick_rows(R_U, R_DQ, R_Q, R_DATT)
        parts = [nn(chosen(GRAN, off, ucls), dq)]
        r, c = iota((D, 64), 0), iota((D, 64), 1)
        inside = r - 24 * (c >> 1)
        expand = ((inside >= 0) & (inside < 24) & ((r & 1) == (c & 1))).astype(BF16)
        r = iota((D, D), 0)
        mine = (r - 24 * ((r * 2731) >> 16)) >> 1 == iota((D, D), 1) >> 6
        for right, lo, skip in ((q, 32, 0), (datt, 48, 8)):
            qbuf[...] = jnp.where(mine, nn(expand, right), 0.0).astype(BF16)

            def compact(i, carry, lo=lo, skip=skip):
                rows = each[pl.ds(8 * i, 8), lo : lo + 32, :].astype(F32)
                abuf[pl.ds(pl.multiple_of(192 * i, 192), 192), :] = (
                    rows[:, skip : skip + 24, :].reshape(192, D).astype(BF16)
                )
                return carry

            lax.fori_loop(0, 4, compact, 0)
            parts.append(nn(chosen(GRAN, off, abuf[...]), qbuf[...]))
        for gi in range(3):
            for p in range(3):
                put(gi, 3, p, parts[p][32 * gi : 32 * (gi + 1), :])

    for gi in range(3):
        g = 3 * info[0] + gi

        @pl.when((g >= 24) & (g < 32))
        def _(gi=gi, g=g):
            left, right = pick_rows(R_ATT, R_DO)
            put(gi, 1, 0, nn(chosen(GRAN, GRAN * (g - 24), left), right))

        @pl.when((g >= 32) & (g < 64))
        def _(gi=gi, g=g):
            left, *rights = pick_rows(R_H, *[R_DA + 2 * p for p in range(4)])
            left = chosen(32, 24 * (g - 32), left)
            for p in range(4):
                put(gi, 4, p, nn(left, rights[p])[0:24, :])

        @pl.when(g >= 64)
        def _(gi=gi, g=g):
            left, right = pick_rows(R_E + 2 * ((g - 64) >> 3), R_DF)
            put(gi, 1, 0, nn(chosen(GRAN, GRAN * ((g - 64) & 7), left), right))


def join_grads(info, g0, a, b, gv, out, square, buf):
    g = g0[...]
    out[pl.ds(0, 1728, stride=2), :] = g
    buf[...] = a[...].astype(F32) + b[...].astype(F32)
    total = buf[...]
    sq = jnp.sum((g * g).reshape(216, 8, 128), axis=0)
    for j in range(6):
        v = total[:, 128 * j : 128 * (j + 1)]
        sq = sq + jnp.sum((v * v).reshape(36, 8, 128), axis=0)
    whole = jnp.sum(colsum(sq), axis=1, keepdims=True)
    whole = whole + jnp.sum(colsum(gv[...] * gv[...]), axis=1, keepdims=True)
    square[...] = jnp.broadcast_to(whole, (8, 128))
    for gi in range(3):

        def emit(n, gi=gi):
            m = GRAN // n
            for p in range(n):
                for j in range(6):
                    out[pl.ds(12 * (GRAN * gi + p) + 2 * j + 1, m, stride=12 * n), :] = buf[
                        GRAN * gi + m * p : GRAN * gi + m * (p + 1), 128 * j : 128 * (j + 1)
                    ]

        by_kind(3 * info[0] + gi, emit)


def adamw_kernel(sq, w, m, v, g, vw, vm, vv, vg, w_new, m_new, v_new, vw_new, vm_new, vv_new, norm_out):
    norm = jnp.sqrt(sq[...])
    norm_out[0, 0] = norm[0, 0]
    coef = jnp.minimum(1.0, math.sqrt(2 * (PL + QL)) / (norm[0:1, 0:1] + 1e-06))
    w_new[...], m_new[...], v_new[...] = adamw_update(w[...], m[...], v[...], g[...] * coef, 0.1, weight_decay)
    vw_new[...], vm_new[...], vv_new[...] = adamw_update(vw[...], vm[...], vv[...], vg[...] * coef, 0.5, 0.0)


def adamw_update(weight, moment_one, moment_two, gradient, step_rate, decay_rate):
    first_new = beta_one * moment_one + (1.0 - beta_one) * gradient
    second_new = beta_two * moment_two + (1.0 - beta_two) * gradient * gradient
    first_hat = first_new / (1.0 - beta_one**STEP)
    second_hat = second_new / (1.0 - beta_two**STEP)
    weight_new = weight - step_rate * (first_hat / (jnp.sqrt(second_hat) + adam_epsilon) + decay_rate * weight)
    return (weight_new, first_new, second_new)


def order_kernel(info, a3, a2, mine, came, over_x, over_y, last_x, last_y, o1, o2, o3, o0, acc):
    acc[3], acc[2] = a3[...], a2[...]
    total_kernel(mine, came, over_x, over_y, last_x, last_y, acc.at[1], acc.at[0])
    for k, out in enumerate((o1, o2, o3, o0)):
        out[...] = acc[(info[1] + 3 - k) & 3]


SMEM = pl.BlockSpec(memory_space=pltpu.SMEM)
VMEM = pl.BlockSpec(memory_space=pltpu.VMEM)
ANY = pl.BlockSpec(memory_space=pl.ANY)


def struct(*shape, dtype=F32):
    return jax.ShapeDtypeStruct(shape, dtype)


def call(kernel, name, ins, in_specs, outs, out_specs, scratch=(), flops=0, moved=0):
    return pl.pallas_call(
        kernel,
        out_shape=outs,
        in_specs=in_specs,
        out_specs=out_specs,
        scratch_shapes=list(scratch),
        name=name,
        compiler_params=pltpu.CompilerParams(vmem_limit_bytes=VMEM_BYTES),
        cost_estimate=pl.CostEstimate(flops=flops, bytes_accessed=moved, transcendentals=0),
    )(*ins)


def flat_view(a):
    return a.reshape(2, -1, 128).transpose(1, 0, 2).reshape(-1, 128)


def flat_back(a):
    return a.reshape(-1, 2, 128).transpose(1, 0, 2).reshape(2, -1)


def body(tokens, cotangent, lengths, mats, mats_m, mats_v, vecs, vecs_m, vecs_v):
    dp, pair = lax.axis_index("dp"), lax.axis_index("pair")
    device = 2 * dp + pair
    z = dp >> 2
    info = jnp.stack(
        [device, z, (dp >> 1) & 1, dp & 1, pair, lengths[0, 0, 0], jnp.int32(0), jnp.int32(0)]
    ).astype(jnp.int32)
    u = tokens[0]
    cot = cotangent[0]
    flat = flat_view(mats)
    own = call(pack_kernel, "pack", (info, flat, vecs), [SMEM, VMEM, VMEM], struct(SEND, D, dtype=BF16), VMEM)
    pieces0, pieces1 = gather_blocks(own)
    row = struct(16, D)
    row16 = struct(16, D, dtype=BF16)
    saved_shapes = (
        row, struct(16, 128), row, struct(16, 128), struct(4, 16, D), struct(4, 16, D, dtype=BF16),
        row16, row16, row16, row16, struct(32, D, dtype=BF16), struct(32, D, dtype=BF16), struct(32, TOK),
    )
    weights = [
        pltpu.VMEM((16, D), F32),
        pltpu.VMEM((32, 16, D), BF16),
        pltpu.VMEM((GRANS * GRAN, D), BF16),
        pltpu.VMEM((4, D, D), BF16),
    ]
    y_cls, *saved = call(
        first_forward,
        "first_forward",
        (info, u, *pieces0),
        [SMEM, VMEM] + [ANY] * 32,
        (row, *saved_shapes),
        (VMEM,) * 14,
        weights + [pltpu.SemaphoreType.DMA((64,))],
        flops=2 * 32 * PL,
        moved=2 * PL,
    )
    part = struct(HALF, D, dtype=BF16)
    mid16 = pltpu.VMEM((TOK, D), BF16)
    mid = pltpu.VMEM((TOK, D), F32)
    low = struct(TOK, D, dtype=BF16)
    head_out, dr, vg1, zb, qs, ks, vs, att, pm, w1_grad, theirs_a1, theirs_a2, mine_a1, mine_a2 = call(
        second_block,
        "second_block",
        (info, u, cot, y_cls, *pieces1, *pieces0[3::4]),
        [SMEM, VMEM, VMEM, VMEM] + [ANY] * 40,
        (low, struct(TOK, D), row, low, low, low, low, low, struct(HEADS, TOK, TOK), struct(1536, D, dtype=BF16)) + (part,) * 4,
        (VMEM,) * 8 + (ANY,) * 6,
        weights
        + [
            pltpu.VMEM((GRANS * GRAN, D), BF16),
            mid,
            pltpu.VMEM((HEADS, TOK, TOK), F32),
            mid, mid16,
            pltpu.VMEM((D, TOK), BF16),
            pltpu.VMEM((4, TOK, D), F32),
            pltpu.VMEM((4, TOK, D), BF16),
            pltpu.VMEM((4, TOK, D), BF16),
            mid, mid,
            pltpu.VMEM((8, GRAN, D), F32),
            mid16,
            pltpu.SemaphoreType.DMA((64,)),
            pltpu.SemaphoreType.DMA((30,)),
        ],
        flops=4 * TOK * PL,
        moved=4 * PL,
    )

    def first_part(mine, came):
        return [add16(mine[lo:hi], came[lo:hi]) for lo, hi in ((SX, SY), (SY, QX))]

    def last_part(mine, came, over_x, over_y):
        return [
            (mine[lo : lo + 288].astype(F32) + came[lo : lo + 288].astype(F32) + over[:288].astype(F32)).astype(BF16)
            for lo, over in ((QX - HALF, over_y), (QY - HALF, over_x))
        ]

    own_rows, half = pl.BlockSpec((576, D), lambda i: (1, 0)), pl.BlockSpec((288, D), lambda i: (0, 0))
    second = pl.BlockSpec((288, D), lambda i: (1, 0))

    def plane_total(mine, came, over_x, over_y, last_x, last_y):
        return pl.pallas_call(
            total_kernel,
            grid=(1,),
            in_specs=[own_rows, own_rows, second, second, half, half],
            out_specs=[half, half],
            out_shape=[struct(288, D, dtype=BF16)] * 2,
            name="total",
        )(mine, came, over_x, over_y, last_x, last_y)

    cls = gather_step(y_cls[0:2].astype(BF16), 0, device)()
    theirs_a1, theirs_a2, cls = fence([theirs_a1, theirs_a2, cls])
    came_a1, came_a2 = core_flip(theirs_a1), core_flip(theirs_a2)
    cls = gather_step(cls, 1, device)()
    sx, sy, cls, dr = fence([*first_part(mine_a1, came_a1), cls, dr])
    over_xa, over_ya = x_flip(sx), y_flip(sy)
    dz, vg1, theirs_b1, theirs_b2, mine_b1, mine_b2 = call(
        second_attention,
        "second_attention",
        (info, dr, vg1, zb, qs, ks, vs, att, *pieces1, pm, w1_grad),
        [SMEM] + [VMEM] * 7 + [ANY] * 34,
        (struct(TOK, D), row) + (part,) * 4,
        (VMEM, VMEM) + (ANY,) * 4,
        [
            pltpu.VMEM((GRANS * GRAN // 2, D), BF16),
            pltpu.VMEM((GRANS * GRAN // 2, D), BF16),
            pltpu.VMEM((HEADS, TOK, TOK), F32),
            mid16, mid16, mid16, mid16,
            pltpu.SemaphoreType.DMA((34,)),
        ],
        flops=2 * TOK * PL,
        moved=2 * PL,
    )
    qx_a, qy_a, theirs_b1, theirs_b2, cls = fence(
        [*last_part(mine_a2, came_a2, over_xa, over_ya), theirs_b1, theirs_b2, cls]
    )
    last_xa, last_ya = x_flip(qx_a), y_flip(qy_a)
    came_b1 = core_flip(theirs_b1)
    every_cls = gather_step(cls, 2, device)()
    sx, sy, dz, theirs_b2 = fence([*first_part(mine_b1, came_b1), dz, theirs_b2])
    over_xb, over_yb = x_flip(sx), y_flip(sy)
    came_b2 = core_flip(theirs_b2)
    token_grad, payload, loss = call(
        first_backward,
        "first_backward",
        (info, u, every_cls, dz, vg1, *saved, *pieces0),
        [SMEM] + [VMEM] * 17 + [ANY] * 32,
        (struct(TOK, D), struct(PAY, D, dtype=BF16), struct(1, 1)),
        (VMEM, VMEM, SMEM),
        weights
        + [
            pltpu.VMEM((16, D), F32),
            pltpu.VMEM((64, D), F32),
            pltpu.VMEM((PAY, D), F32),
            pltpu.SemaphoreType.DMA((64,)),
        ],
        flops=2 * 32 * PL,
        moved=2 * PL,
    )
    qx_b, qy_b, pay, last_xa, last_ya = fence(
        [*last_part(mine_b2, came_b2, over_xb, over_yb), payload, last_xa, last_ya]
    )
    last_xb, last_yb = x_flip(qx_b), y_flip(qy_b)
    a3, a2 = plane_total(mine_a2, came_a2, over_xa, over_ya, last_xa, last_ya)
    slots = jnp.concatenate([pay, z_turn(pay, 1), z_turn(pay, 3), z_turn(pay, 2)], 0)
    in_turn = pl.pallas_call(
        order_kernel,
        grid=(1,),
        in_specs=[SMEM, half, half, own_rows, own_rows, second, second, half, half],
        out_specs=[half] * 4,
        out_shape=[struct(288, D, dtype=BF16)] * 4,
        scratch_shapes=[pltpu.VMEM((4, 288, D), BF16)],
        name="order",
    )(info, a3, a2, mine_b2, came_b2, over_xb, over_yb, last_xb, last_yb)
    moving = z_up(in_turn[0])
    over_x, over_y = x_flip(slots), y_flip(slots)
    rows = [slots, over_x, over_y]
    moving = z_up(add16(in_turn[1], moving))
    half = rows[0].shape[0] // 2
    rows += [y_flip(rows[1][:half]), x_flip(rows[2][half:])]
    rows += [core_flip(v) for v in rows]
    moving = z_up(add16(in_turn[2], moving))
    flat0, vec_sum = call(
        owner_grad,
        "owner_grad",
        (info, *rows),
        [SMEM] + [ANY] * 10,
        (struct(1728, 128), struct(24, D)),
        (VMEM, VMEM),
        [
            pltpu.VMEM((32 * PAY, D), BF16),
            pltpu.VMEM((D, D), BF16),
            pltpu.VMEM((D, D), BF16),
            pltpu.SemaphoreType.DMA((10,)),
        ],
        flops=2 * 768 * 768 * 768,
        moved=2 * 32 * PAY * D,
    )
    grad_vecs = lax.dynamic_slice(vec_sum.reshape(2, QL), (0, device * vecs.shape[1]), vecs.shape)
    grads, square = call(
        join_grads,
        "join_grads",
        (info, flat0, in_turn[3], moving, grad_vecs),
        [SMEM] + [VMEM] * 4,
        (struct(3456, 128), struct(8, 128)),
        (VMEM, VMEM),
        [pltpu.VMEM((288, D), F32)],
    )
    block = pl.BlockSpec((864, 128), lambda i: (i, 0))
    small = pl.BlockSpec(vecs.shape, lambda i: (0, 0))
    tile = pl.BlockSpec((8, 128), lambda i: (0, 0))
    *new, new_vecs, new_vecs_m, new_vecs_v, norm = pl.pallas_call(
        adamw_kernel,
        grid=(4,),
        in_specs=[tile] + [block] * 4 + [small] * 4,
        out_specs=(block,) * 3 + (small,) * 3 + (SMEM,),
        out_shape=(struct(3456, 128),) * 3 + (struct(*vecs.shape),) * 3 + (struct(1, 1),),
        name="adamw",
    )(sum_quick(square), flat, flat_view(mats_m), flat_view(mats_v), grads, vecs, vecs_m, vecs_v, grad_vecs)
    new_mats, new_mats_m, new_mats_v = [flat_back(a) for a in new]
    return (
        head_out[None],
        token_grad[None],
        loss.reshape(()),
        norm.reshape(()),
        new_mats,
        new_mats_m,
        new_mats_v,
        new_vecs,
        new_vecs_m,
        new_vecs_v,
    )


def matmul(left_side, right_side):
    return jnp.dot(left_side, right_side, preferred_element_type=jnp.float32)


def inner_rows(left_side, right_side):
    return lax.dot_general(
        left_side, right_side, (((0,), (0,)), ((), ())), preferred_element_type=jnp.float32
    )


def outer_cols(left_side, right_side):
    return lax.dot_general(
        left_side, right_side, (((1,), (1,)), ((), ())), preferred_element_type=jnp.float32
    )


def exact_dot(left_side, right_side):
    return jnp.dot(
        left_side, right_side, precision=lax.Precision.HIGHEST, preferred_element_type=jnp.float32
    )


def layer_norm(resid, gain, shift):
    centred = resid - jnp.mean(resid, axis=-1, keepdims=True)
    spread = jnp.mean(centred * centred, axis=-1, keepdims=True)
    return centred * lax.rsqrt(spread + norm_epsilon) * gain + shift


def gelu_exact(before):
    return jax.nn.gelu(before, approximate=False)


def unpack(mat_row, vec_row):
    edge_one = 3 * D * D
    edge_two = 4 * D * D
    edge_three = edge_two + D * FF
    input_weight = mat_row[:edge_one].reshape(D, 3 * D)
    output_weight = mat_row[edge_one:edge_two].reshape(D, D)
    expand_weight = mat_row[edge_two:edge_three].reshape(D, FF)
    shrink_weight = mat_row[edge_three:].reshape(FF, D)
    vector = vec_row.astype(jnp.float32)
    pieces = []
    cursor = 0
    for piece_len in (D, D, D, D, D, FF, D, D, D):
        pieces.append(vector[cursor : cursor + piece_len])
        cursor = cursor + piece_len
    return (input_weight, output_weight, expand_weight, shrink_weight) + tuple(pieces)


def head_scores(queries, key_rows, same_span):
    row_count = queries.shape[0]
    query_heads = queries.reshape(row_count, HEADS, HEAD_DIM)
    key_heads = key_rows.reshape(row_count, HEADS, HEAD_DIM)
    scores = jnp.einsum(
        "thd,shd->hts", query_heads, key_heads, preferred_element_type=jnp.float32
    ) * HEAD_DIM ** (-0.5)
    return jnp.where(same_span[None, :, :], scores, masked_score)


def layer_forward(params, inputs, same_span):
    (
        input_weight,
        output_weight,
        expand_weight,
        shrink_weight,
        query_bias,
        value_bias,
        output_bias,
        first_gain,
        first_shift,
        expand_bias,
        shrink_bias,
        second_gain,
        second_shift,
    ) = params
    row_count = inputs.shape[0]
    low_input = inputs.astype(jnp.bfloat16)
    joint = matmul(low_input, input_weight)
    queries = (joint[:, :D] + query_bias).astype(jnp.bfloat16)
    key_rows = joint[:, D : 2 * D].astype(jnp.bfloat16)
    values = (joint[:, 2 * D :] + value_bias).astype(jnp.bfloat16)
    scores = head_scores(queries, key_rows, same_span)
    row_max = jnp.max(scores, axis=-1, keepdims=True)
    raised = jnp.exp(scores - row_max)
    summed = jnp.sum(raised, axis=-1, keepdims=True)
    portions = raised / summed
    logsum = row_max + jnp.log(summed)
    value_heads = values.reshape(row_count, HEADS, HEAD_DIM)
    attended = jnp.einsum(
        "hts,shd->thd",
        portions.astype(jnp.bfloat16),
        value_heads,
        preferred_element_type=jnp.float32,
    )
    attended = attended.reshape(row_count, D).astype(jnp.bfloat16)
    resid_one = inputs + (matmul(attended, output_weight) + output_bias)
    hidden = layer_norm(resid_one, first_gain, first_shift)
    low_hidden = hidden.astype(jnp.bfloat16)
    before = matmul(low_hidden, expand_weight) + expand_bias
    activated = gelu_exact(before).astype(jnp.bfloat16)
    resid_two = hidden + (matmul(activated, shrink_weight) + shrink_bias)
    output = layer_norm(resid_two, second_gain, second_shift)
    kept = (
        low_input,
        queries,
        key_rows,
        values,
        logsum,
        attended,
        resid_one,
        low_hidden,
        before,
        activated,
        resid_two,
    )
    return (output, kept)


def layer_backward(params, kept, grad_out, same_span):
    (
        input_weight,
        output_weight,
        expand_weight,
        shrink_weight,
        query_bias,
        value_bias,
        output_bias,
        first_gain,
        first_shift,
        expand_bias,
        shrink_bias,
        second_gain,
        second_shift,
    ) = params
    (
        low_input,
        queries,
        key_rows,
        values,
        logsum,
        attended,
        resid_one,
        low_hidden,
        before,
        activated,
        resid_two,
    ) = kept
    row_count = low_input.shape[0]
    _, norm_pull_two = jax.vjp(layer_norm, resid_two, second_gain, second_shift)
    d_resid_two, d_second_gain, d_second_shift = norm_pull_two(grad_out)
    d_feed = d_resid_two.astype(jnp.bfloat16)
    d_shrink = inner_rows(activated, d_feed)
    d_shrink_bias = jnp.sum(d_feed.astype(jnp.float32), axis=0)
    _, gelu_pull = jax.vjp(gelu_exact, before)
    d_before = gelu_pull(outer_cols(d_feed, shrink_weight))[0].astype(jnp.bfloat16)
    d_expand = inner_rows(low_hidden, d_before)
    d_expand_bias = jnp.sum(d_before.astype(jnp.float32), axis=0)
    d_hidden = d_resid_two + outer_cols(d_before, expand_weight)
    _, norm_pull_one = jax.vjp(layer_norm, resid_one, first_gain, first_shift)
    d_resid_one, d_first_gain, d_first_shift = norm_pull_one(d_hidden)
    d_branch = d_resid_one.astype(jnp.bfloat16)
    d_output = inner_rows(attended, d_branch)
    d_output_bias = jnp.sum(d_branch.astype(jnp.float32), axis=0)
    d_attended = outer_cols(d_branch, output_weight).astype(jnp.bfloat16)
    portions = jnp.exp(head_scores(queries, key_rows, same_span) - logsum)
    query_heads = queries.reshape(row_count, HEADS, HEAD_DIM)
    key_heads = key_rows.reshape(row_count, HEADS, HEAD_DIM)
    value_heads = values.reshape(row_count, HEADS, HEAD_DIM)
    d_att_heads = d_attended.reshape(row_count, HEADS, HEAD_DIM)
    d_portions = jnp.einsum(
        "thd,shd->hts", d_att_heads, value_heads, preferred_element_type=jnp.float32
    )
    d_values = jnp.einsum(
        "hts,thd->shd",
        portions.astype(jnp.bfloat16),
        d_att_heads,
        preferred_element_type=jnp.float32,
    )
    d_values = d_values.reshape(row_count, D).astype(jnp.bfloat16)
    d_scores = portions * (d_portions - jnp.sum(d_portions * portions, axis=-1, keepdims=True))
    d_scores = d_scores.astype(jnp.bfloat16)
    score_scale = HEAD_DIM ** (-0.5)
    d_queries = (
        jnp.einsum("hts,shd->thd", d_scores, key_heads, preferred_element_type=jnp.float32)
        * score_scale
    )
    d_queries = d_queries.reshape(row_count, D).astype(jnp.bfloat16)
    d_keys = (
        jnp.einsum("hts,thd->shd", d_scores, query_heads, preferred_element_type=jnp.float32)
        * score_scale
    )
    d_keys = d_keys.reshape(row_count, D).astype(jnp.bfloat16)
    d_joint = jnp.concatenate([d_queries, d_keys, d_values], axis=1)
    d_input_weight = inner_rows(low_input, d_joint)
    d_query_bias = jnp.sum(d_queries.astype(jnp.float32), axis=0)
    d_value_bias = jnp.sum(d_values.astype(jnp.float32), axis=0)
    d_inputs = d_resid_one + outer_cols(d_joint, input_weight)
    mat_grad = jnp.concatenate(
        [
            d_input_weight.reshape(-1),
            d_output.reshape(-1),
            d_expand.reshape(-1),
            d_shrink.reshape(-1),
        ]
    )
    vec_grad = jnp.concatenate(
        [
            d_query_bias,
            d_value_bias,
            d_output_bias,
            d_first_gain,
            d_first_shift,
            d_expand_bias,
            d_shrink_bias,
            d_second_gain,
            d_second_shift,
        ]
    )
    return (d_inputs, mat_grad, vec_grad)


def contrast_rows(anchors, key_table, anchor_index, span_count, score_scale):
    key_count = key_table.shape[0]
    key_index = jnp.arange(key_count, dtype=jnp.int32)
    scores = outer_cols(anchors, key_table) * score_scale
    scores = jnp.where(anchor_index[:, None] == key_index[None, :], masked_score, scores)
    partner = (
        jnp.bitwise_xor(anchor_index // span_count, 1) * span_count + anchor_index % span_count
    )
    row_max = jnp.max(scores, axis=-1, keepdims=True)
    raised = jnp.exp(scores - row_max)
    summed = jnp.sum(raised, axis=-1, keepdims=True)
    logsum = row_max[:, 0] + jnp.log(summed[:, 0])
    target = key_index[None, :] == partner[:, None]
    positive = jnp.sum(jnp.where(target, scores, 0.0), axis=1)
    grads_low = (raised / summed - target.astype(jnp.float32)).astype(jnp.bfloat16)
    return (grads_low, logsum - positive)


def general_body(tokens, cotangent, lengths, mats, mats_m, mats_v, vecs, vecs_m, vecs_v):
    full_mats, full_vecs = (
        lax.all_gather(mats.astype(jnp.bfloat16), ("dp", "pair"), axis=1, tiled=True),
        lax.all_gather(vecs.astype(jnp.bfloat16), ("dp", "pair"), axis=1, tiled=True),
    )
    layer_one = unpack(full_mats[0], full_vecs[0])
    layer_two = unpack(full_mats[1], full_vecs[1])
    inputs = tokens[0].astype(jnp.float32)
    row_count = inputs.shape[0]
    span_lengths = lengths[0, 0]
    span_count = span_lengths.shape[0]
    positions = jnp.arange(row_count, dtype=jnp.int32)
    order = jnp.arange(span_count)
    starts = jnp.sum(jnp.where(order[None, :] < order[:, None], span_lengths[None, :], 0), axis=1)
    span_of = jnp.sum((positions[:, None] >= starts[None, :]).astype(jnp.int32), axis=1)
    same_span = span_of[:, None] == span_of[None, :]
    heads_mark = positions[None, :] == starts[:, None]
    is_cls = jnp.any(heads_mark, axis=0)[:, None]
    picker = heads_mark.astype(jnp.float32)
    doc_groups = lax.axis_size("dp")
    early_out, kept_one = layer_forward(layer_one, inputs, same_span)
    cls_rows = exact_dot(picker, early_out)
    mixture = jnp.where(is_cls, early_out, inputs)
    late_out, kept_two = layer_forward(layer_two, mixture, same_span)
    sent_cls = cls_rows.astype(jnp.bfloat16)
    every_cls = lax.all_gather(sent_cls, ("dp", "pair"), axis=0, tiled=True)
    key_count = every_cls.shape[0]
    score_scale = 2.0 / math.sqrt(D)
    offset = lax.axis_index(("dp", "pair")) * span_count
    own_index = offset + jnp.arange(span_count, dtype=jnp.int32)
    grads_low, loss_terms = contrast_rows(sent_cls, every_cls, own_index, span_count, score_scale)
    anchor_part = matmul(grads_low, every_cls) * score_scale
    key_part = lax.psum_scatter(
        inner_rows(grads_low, sent_cls) * score_scale,
        ("dp", "pair"),
        scatter_dimension=0,
        tiled=True,
    )
    cls_grad = anchor_part + key_part
    grad_late = cotangent[0].astype(jnp.float32)
    d_mixture, late_mats, late_vecs = layer_backward(layer_two, kept_two, grad_late, same_span)
    grad_early = jnp.where(is_cls, d_mixture, 0.0) + exact_dot(picker.T, cls_grad)
    d_inputs, early_mats, early_vecs = layer_backward(layer_one, kept_one, grad_early, same_span)
    token_grad = d_inputs + jnp.where(is_cls, 0.0, d_mixture)
    all_pieces = (
        lax.all_to_all(
            early_mats.reshape(doc_groups, -1).astype(jnp.bfloat16),
            "dp",
            split_axis=0,
            concat_axis=0,
            tiled=True,
        ).astype(jnp.float32),
        lax.all_to_all(
            late_mats.reshape(doc_groups, -1).astype(jnp.bfloat16),
            "dp",
            split_axis=0,
            concat_axis=0,
            tiled=True,
        ).astype(jnp.float32),
        lax.all_to_all(
            early_vecs.reshape(doc_groups, -1).astype(jnp.bfloat16),
            "dp",
            split_axis=0,
            concat_axis=0,
            tiled=True,
        ).astype(jnp.float32),
        lax.all_to_all(
            late_vecs.reshape(doc_groups, -1).astype(jnp.bfloat16),
            "dp",
            split_axis=0,
            concat_axis=0,
            tiled=True,
        ).astype(jnp.float32),
    )
    early_mats_part, late_mats_part, early_vecs_part, late_vecs_part = (
        lax.psum_scatter(
            jnp.sum(all_pieces[0], axis=0).astype(jnp.bfloat16),
            "pair",
            scatter_dimension=0,
            tiled=True,
        ).astype(jnp.float32),
        lax.psum_scatter(
            jnp.sum(all_pieces[1], axis=0).astype(jnp.bfloat16),
            "pair",
            scatter_dimension=0,
            tiled=True,
        ).astype(jnp.float32),
        lax.psum_scatter(
            jnp.sum(all_pieces[2], axis=0).astype(jnp.bfloat16),
            "pair",
            scatter_dimension=0,
            tiled=True,
        ).astype(jnp.float32),
        lax.psum_scatter(
            jnp.sum(all_pieces[3], axis=0).astype(jnp.bfloat16),
            "pair",
            scatter_dimension=0,
            tiled=True,
        ).astype(jnp.float32),
    )
    grad_mats = jnp.stack([early_mats_part, late_mats_part])
    grad_vecs = jnp.stack([early_vecs_part, late_vecs_part])
    square_sum = jnp.sum(grad_mats * grad_mats) + jnp.sum(grad_vecs * grad_vecs)
    total_sq, loss_sum = lax.psum((square_sum, jnp.sum(loss_terms)), ("dp", "pair"))
    grad_norm = jnp.sqrt(total_sq)
    clip_factor = jnp.minimum(1.0, math.sqrt(2 * (PL + QL)) / (grad_norm + 1e-06))
    new_mats, new_mats_m, new_mats_v = adamw_update(
        mats, mats_m, mats_v, grad_mats * clip_factor, 0.1, weight_decay
    )
    new_vecs, new_vecs_m, new_vecs_v = adamw_update(
        vecs, vecs_m, vecs_v, grad_vecs * clip_factor, 0.5, 0.0
    )
    contrastive = loss_sum / key_count
    return (
        late_out.astype(jnp.bfloat16)[None],
        token_grad[None],
        contrastive,
        grad_norm,
        new_mats,
        new_mats_m,
        new_mats_v,
        new_vecs,
        new_vecs_m,
        new_vecs_v,
    )


def solution(mesh):
    flat = P(None, ("dp", "pair"))
    rows = P("pair", "dp", None)
    here = dict(mesh.shape) == {"dp": 16, "pair": 2}
    return jax.shard_map(
        body if here else general_body,
        mesh=mesh,
        in_specs=(rows, rows, rows) + (flat,) * 6,
        out_specs=(rows, rows, P(), P()) + (flat,) * 6,
        check_vma=False,
    )
```

```python
import math

import jax
import jax.numpy as jnp
from jax import lax
from jax.experimental import pallas as pl
from jax.experimental.pallas import tpu as pltpu
from jax.sharding import PartitionSpec as P

D = 768
HEADS = 12
HEAD_DIM = 64
FF = 3072
STEP = 10
PL = 7077888
QL = 9216

norm_epsilon = 1e-12
masked_score = -1000000000.0
beta_one = 0.9
beta_two = 0.999
adam_epsilon = 1e-08
weight_decay = 0.01

F32 = jnp.float32
BF16 = jnp.bfloat16
TOK = 256
GRAN = 96
GRANS = PL // D // GRAN
VMEM_BYTES = 63_000_000

V_BQ, V_BV, V_BO, V_G1, V_C1, V_B1, V_B2, V_G2, V_C2 = 0, 1, 2, 3, 4, 5, 9, 10, 11

R_E, R_DF, R_H, R_DA, R_ATT, R_DO, R_U, R_DQ, R_Q, R_DATT, R_WK, R_PU, R_VEC = (
    0, 8, 10, 12, 20, 22, 24, 26, 28, 30, 32, 56, 80,
)
PAY = 96


def nn(a, b):
    return lax.dot_general(a, b, (((1,), (0,)), ((), ())), preferred_element_type=F32)


def nt(a, b):
    return lax.dot_general(a, b, (((1,), (1,)), ((), ())), preferred_element_type=F32)


def tn(a, b):
    return lax.dot_general(a, b, (((0,), (0,)), ((), ())), preferred_element_type=F32)


def iota(shape, axis):
    return lax.broadcasted_iota(jnp.int32, shape, axis)


def erf(x):
    x = jnp.clip(x, -3.832506856900711, 3.832506856900711)
    s = x * x
    top = 0.00022905065861350646
    for c in (0.0034082910107109506, 0.050955695062380861, 0.18520832239976145, 1.128379143519084):
        top = top * s + c
    low = -1.1791602954361697e-7
    for c in (
        0.000023547966471313185,
        0.0010179625278914885,
        0.014070470171167667,
        0.11098505178285362,
        0.49746925110067538,
        1.0,
    ):
        low = low * s + c
    return x * top / low


def gelu_both(a):
    phi = 0.5 + 0.5 * erf(a * math.sqrt(0.5))
    return a * phi, phi + a * jnp.exp(-0.5 * a * a) * (1.0 / math.sqrt(2.0 * math.pi))


def norm_forward(r):
    centred = r - jnp.mean(r, axis=-1, keepdims=True)
    rstd = lax.rsqrt(jnp.mean(centred * centred, axis=-1, keepdims=True) + norm_epsilon)
    return centred * rstd, rstd


def norm_backward(dy, gain, xhat, rstd):
    dx = dy * gain
    return rstd * (
        dx - jnp.mean(dx, axis=-1, keepdims=True) - xhat * jnp.mean(dx * xhat, axis=-1, keepdims=True)
    )


def colsum(v):
    return jnp.sum(v, axis=0, keepdims=True)


def flip(v, axis, bit):
    return lax.ppermute(v, axis, [(i, i ^ bit) for i in range(lax.axis_size(axis))])


def core_flip(v):
    return flip(v, "dp", 1)


def x_flip(v):
    return flip(v, "dp", 2)


def y_flip(v):
    return flip(v, "pair", 1)


def z_up(v):
    n = lax.axis_size("dp")
    return lax.ppermute(v, "dp", [(i, (i + 4) % n) for i in range(n)])


def z_turn(v, places):
    n = lax.axis_size("dp")
    return lax.ppermute(v, "dp", [(i, (i + 4 * places) % n) for i in range(n)])


def xor_flip(v, pair_bit, dp_bits):
    if not pair_bit:
        return flip(v, "dp", dp_bits)
    n = lax.axis_size("dp")
    return lax.ppermute(v, ("dp", "pair"), [(i, i ^ (2 * dp_bits + 1)) for i in range(2 * n)])


def fence(values):
    return list(lax.optimization_barrier(tuple(values)))


SMALL_STEPS = (((1, 0), (0, 1), (1, 1)), ((0, 2), (0, 4), (0, 6)), ((0, 8),))


def gather_step(v, step, device):
    got = [v] + [xor_flip(v, *bits) for bits in SMALL_STEPS[step]]
    here = (device >> (2 * step)) & (len(got) - 1)
    return lambda: jnp.concatenate([pick(here ^ p, got) for p in range(len(got))], 0)


SUM_STEPS = (((0, 1),), ((1, 0), (0, 2), (1, 2)), ((0, 4), (0, 8), (0, 12)))


def sum_quick(v):
    for bits in SUM_STEPS:
        got = [v] + [xor_flip(v, *b) for b in bits]
        v = got[0] + got[1] if len(got) == 2 else (got[0] + got[1]) + (got[2] + got[3])
    return v


def pick(index, cases):
    return lax.select_n(index, *cases)


GATHER_ROUNDS = (
    ("x0", "y0", "s1"),
    ("d0", "e0", "x1", "y1", "s2"),
    ("d1", "e1", "x2", "y2", "s3"),
    ("f2", "x3", "y3"),
    ("d3", "e3"),
)


SEND_VEC, SEND_ONE, SEND = 288, 304, 592


def gather_blocks(own):
    have = {"s0": own}
    across = ["s0"]
    for r, tasks in enumerate(GATHER_ROUNDS):
        sources = {}
        for name in tasks:
            kind, k = name[0], int(name[1])
            sources[name] = {"s": f"s{k - 1}", "x": f"s{k}", "y": f"s{k}", "d": f"x{k}", "e": f"y{k}", "f": f"x{k}"}[kind]
        if "y3" in sources:
            sources["y3"] = "y2"
        names = list(dict.fromkeys([*sources.values(), *across]))
        if r:
            have.update(zip(names, fence([have[i] for i in names])))
        for name, source in sources.items():
            move = {
                "s": z_up, "x": x_flip, "y": y_flip, "f": y_flip, "d": lambda v: y_flip(v[:SEND_ONE]), "e": lambda v: x_flip(v[SEND_ONE:])
            }[name[0]]
            have[name] = z_up(have[source]) if name == "y3" else move(have[source])
        if r in (1, 2):
            names = [*across, *tasks[:2]]
            have.update(zip(names, fence([have[i] for i in names])))
        for i in across:
            have["c" + i] = core_flip(have[i])
        across = list(tasks)
    names = ["cs3", "cx3", "cy3", *across]
    have.update(zip(names, fence([have[i] for i in names])))
    for i in across:
        have["c" + i] = core_flip(have[i])
    orders = [["sxy" + (last if k != 2 else "f") for k in range(4)] for last in "de"]
    return [[have[c + kind + str(k)] for c in ("", "c") for k in range(4) for kind in kinds[k]] for kinds in orders]


def add16(a, b):
    return (a.astype(F32) + b.astype(F32)).astype(BF16)


GROUPS = ((3, 2), (1, 0))
GROUP_ROWS = 2304
HALF = 1152
SX, SY, QX, QY, OWN = 0, 576, 1152, 1440, 1728


def by_kind(granule, emit):
    joint = granule < 24
    wide = (granule >= 32) & (granule < 64)
    pl.when(joint)(lambda: emit(3))
    pl.when(wide)(lambda: emit(4))
    pl.when(jnp.logical_not(joint | wide))(lambda: emit(1))


def pack_kernel(info, flat, vecs, out):
    out[SEND_VEC:SEND_ONE, :] = jnp.zeros((SEND_ONE - SEND_VEC, D), BF16)
    both = vecs[...]
    out[SEND_VEC:SEND_ONE, 0:288] = jnp.concatenate([both, jnp.zeros((14, 288), F32)], 0).astype(BF16)
    for gi in range(3):

        def emit(n, gi=gi):
            m = GRAN // n
            for layer in range(2):
                for j in range(6):
                    parts = [
                        flat[pl.ds(12 * (GRAN * gi + p) + 2 * j + layer, m, stride=12 * n), :] for p in range(n)
                    ]
                    tile = parts[0] if n == 1 else jnp.concatenate(parts, 0)
                    at = SEND_ONE * layer + GRAN * gi
                    out[at : at + GRAN, 128 * j : 128 * (j + 1)] = tile.astype(BF16)

        by_kind(3 * info[0] + gi, emit)


def owner(info, plane, kind, other):
    return (
        8 * plane
        + 4 * jnp.bitwise_xor(info[2], kind & 1)
        + 2 * jnp.bitwise_xor(info[3], other)
        + jnp.bitwise_xor(info[4], kind >> 1)
    )


def fill(info, pieces, diagonals, block, wbuf, vbuf, sem):
    vecs = []
    for other in (0, 1):
        for k in range(4):
            for kind in range(4):
                i = 16 * other + 4 * k + kind
                source = (pieces if kind < 3 else diagonals)[i].at[pl.ds(SEND_VEC, 16)]
                dev = owner(info, (info[1] + 4 - k) & 3, kind, other)
                vecs.append(pltpu.make_async_copy(source, vbuf.at[dev], sem.at[32 + i]))
    for copy in vecs:
        copy.start()

    def copies(plane, k):
        made = []
        for other in (0, 1):
            for kind in range(4):
                source = pieces[16 * other + 4 * k + kind].at[pl.ds(SEND_ONE if block and (kind < 3 or k == 2) else 0, 288)]
                rows = pl.ds(pl.multiple_of(288 * owner(info, plane, kind, other), 16), 288)
                made.append(pltpu.make_async_copy(source, wbuf.at[rows], sem.at[8 * plane + 2 * kind + other]))
        return made

    for plane in range(4):
        for k in range(4):

            @pl.when(((info[1] + 4 - plane) & 3) == k)
            def _(plane=plane, k=k):
                for copy in copies(plane, k):
                    copy.start()

    def wait_vecs():
        for copy in vecs:
            copy.wait()

    def wait(plane):
        for copy in copies(plane, 0):
            copy.wait()

    return wait_vecs, wait


def order_vec(vbuf, block, vec):
    every = vbuf[:, 0:2, :].astype(F32)
    for q in range(QL // GRAN):
        to, lo = GRAN * (q % 8), GRAN * (q % 3)
        vec[q // 8 : q // 8 + 1, to : to + GRAN] = every[q // 3, block : block + 1, lo : lo + GRAN]


def split_w1(wbuf, w1):
    def step(i, carry):
        rows = wbuf[pl.ds(32 + 4 * i, 4)].astype(F32)
        for j in range(4):
            part = rows[:, 24 * j : 24 * (j + 1), :].reshape(GRAN, D).astype(BF16)
            w1[j, pl.ds(pl.multiple_of(GRAN * i, GRAN), GRAN), :] = part
        return carry

    lax.fori_loop(0, 8, step, 0)


def w_in(wbuf, j):
    return wbuf[0:24, 32 * j : 32 * (j + 1), :].reshape(D, D)


def w_out(wbuf):
    return wbuf[24:32].reshape(D, D)


def w_shrink(wbuf, j):
    return wbuf[64 + 8 * j : 72 + 8 * j].reshape(D, D)


def expander():
    r, c = iota((32, 16), 0), iota((32, 16), 1)
    return ((r < 24) & ((r & 1) == c)).astype(BF16)


def head_mask():
    r, lane = iota((32, D), 0), iota((32, D), 1)
    return (r < 24) & ((r >> 1) == (lane >> 6))


def spread(expand, mask, rows):
    return jnp.where(mask, nn(expand, rows), 0.0).astype(BF16)


def first_forward(
    info, u_ref, *refs
):
    pieces = diagonals = refs[:32]
    y_out, cls_out, xh1_o, rs1_o, xh2_o, rs2_o, gp_o, e_o, h_o, att_o, u_o, q_o, pu_o, qk_o, p_o, vec, vbuf, wflat, w1, sem = refs[32:]
    wait_vecs, wait = fill(info, pieces, diagonals, 0, wflat, vbuf, sem)
    wbuf = wflat.reshape(GRANS, GRAN, D)
    start = info[5]
    u = u_ref[...]
    r, t = iota((16, TOK), 0), iota((16, TOK), 1)
    picker = (((r == 0) & (t == 0)) | ((r == 1) & (t == start))).astype(BF16)
    cls = nn(picker, u)
    cls16 = cls.astype(BF16)
    expand, mask = expander(), head_mask()
    r, t = iota((32, TOK), 0), iota((32, TOK), 1)
    inside = (t >= start).astype(jnp.int32) == (r & 1)
    real = r < 24
    wait_vecs()
    order_vec(vbuf, 0, vec)
    wait(0)
    q = (nn(cls16, w_in(wbuf, 0)) + vec[V_BQ : V_BQ + 1, :]).astype(BF16)
    qk = nt(spread(expand, mask, q), w_in(wbuf, 1)).astype(BF16)
    scores = jnp.where(inside, nt(qk, u) * HEAD_DIM**-0.5, masked_score)
    raised = jnp.exp(scores - jnp.max(scores, axis=-1, keepdims=True))
    portions = jnp.where(real, raised / jnp.sum(raised, axis=-1, keepdims=True), 0.0)
    low = portions.astype(BF16)
    pu = nn(low, u).astype(BF16)
    weight = jnp.sum(low.astype(F32), axis=-1, keepdims=True)
    heads = nn(pu, w_in(wbuf, 2)) + weight * vec[V_BV : V_BV + 1, :]
    att = tn(expand, jnp.where(mask, heads, 0.0).astype(BF16)).astype(BF16)
    wait(1)
    xhat, rstd = norm_forward(cls + nn(att, w_out(wbuf)) + vec[V_BO : V_BO + 1, :])
    xh1_o[...] = xhat
    rs1_o[...] = jnp.broadcast_to(rstd, (16, 128))
    h = xhat * vec[V_G1 : V_G1 + 1, :] + vec[V_C1 : V_C1 + 1, :]
    h16 = h.astype(BF16)
    f = vec[V_B2 : V_B2 + 1, :]
    wait(2)
    split_w1(wbuf, w1)
    wait(3)
    for j in range(4):
        e, gp = gelu_both(nn(h16, w1[j]) + vec[V_B1 + j : V_B1 + j + 1, :])
        e = e.astype(BF16)
        e_o[j] = e
        gp_o[j] = gp
        f = f + nn(e, w_shrink(wbuf, j))
    xhat, rstd = norm_forward(h + f)
    xh2_o[...] = xhat
    rs2_o[...] = jnp.broadcast_to(rstd, (16, 128))
    y = xhat * vec[V_G2 : V_G2 + 1, :] + vec[V_C2 : V_C2 + 1, :]
    y_out[...] = y
    cls_out[...] = y[0:2, :].astype(BF16)
    h_o[...] = h16
    att_o[...] = att
    u_o[...] = cls16
    q_o[...] = q
    pu_o[...] = pu
    qk_o[...] = qk
    p_o[...] = portions


def first_backward(
    info, u_ref, cls_all, dz, vg1, xh1, rs1, xh2, rs2, gp_i, e_i, h_i, att_i, ucls, q_i, pu_i, qk_i, p_i, *refs
):
    pieces = diagonals = refs[:32]
    tg_out, pay_out, loss_out, vec, vbuf, wflat, w1, rows16, dcls, pay, sem = refs[32:]
    wait_vecs, wait = fill(info, pieces, diagonals, 0, wflat, vbuf, sem)
    wbuf = wflat.reshape(GRANS, GRAN, D)
    start = info[5]
    u = u_ref[...]
    keys = cls_all[...]
    n_keys = keys.shape[0]
    scale = 2.0 / math.sqrt(D)
    r, c = iota((n_keys, n_keys), 0), iota((n_keys, n_keys), 1)
    scores = jnp.where(r == c, masked_score, nt(keys, keys) * scale)
    top = jnp.max(scores, axis=-1, keepdims=True)
    raised = jnp.exp(scores - top)
    total = jnp.sum(raised, axis=-1, keepdims=True)
    partner = jnp.bitwise_xor(r, 2) == c
    positive = jnp.sum(jnp.where(partner, scores, 0.0), axis=-1, keepdims=True)
    terms = top + jnp.log(total) - positive
    loss_out[0, 0] = jnp.sum(terms) * (1.0 / n_keys)
    pull = (raised / total - partner.astype(F32)).astype(BF16)
    dcls[...] = (nn(pull, keys) + tn(pull, keys)) * scale
    rows16[...] = jnp.zeros((16, D), F32)
    rows16[0:1, :] = dz[0:1, :] + dcls[pl.ds(2 * info[0], 1), :]
    rows16[1:2, :] = dz[pl.ds(start, 1), :] + dcls[pl.ds(2 * info[0] + 1, 1), :]
    dy = rows16[...]
    wait_vecs()
    order_vec(vbuf, 0, vec)
    for plane in range(4):
        wait(plane)
    split_w1(wbuf, w1)
    xhat = xh2[...]
    pay[R_VEC + 14 : R_VEC + 15, :] = colsum(dy * xhat)
    pay[R_VEC + 15 : R_VEC + 16, :] = colsum(dy)
    dr2 = norm_backward(dy, vec[V_G2 : V_G2 + 1, :], xhat, rs2[:, 0:1])
    df = dr2.astype(BF16)
    pay[R_DF : R_DF + 2, :] = df.astype(F32)[0:2, :]
    dh = dr2
    for j in range(4):
        da = (gp_i[j] * nt(df, w_shrink(wbuf, j))).astype(BF16)
        pay[R_E + 2 * j : R_E + 2 * j + 2, :] = e_i[j].astype(F32)[0:2, :]
        pay[R_DA + 2 * j : R_DA + 2 * j + 2, :] = da.astype(F32)[0:2, :]
        dh = dh + nt(da, w1[j])
    xhat = xh1[...]
    pay[R_VEC + 12 : R_VEC + 13, :] = colsum(dh * xhat)
    pay[R_VEC + 13 : R_VEC + 14, :] = colsum(dh)
    dr1 = norm_backward(dh, vec[V_G1 : V_G1 + 1, :], xhat, rs1[:, 0:1])
    do = dr1.astype(BF16)
    datt = nt(do, w_out(wbuf)).astype(BF16)
    expand, mask = expander(), head_mask()
    portions = p_i[...]
    low = portions.astype(BF16)
    each = spread(expand, mask, datt)
    dvk = nt(each, w_in(wbuf, 2)).astype(BF16)
    constant = jnp.sum(each.astype(F32) * vec[V_BV : V_BV + 1, :], axis=-1, keepdims=True)
    dp = nt(dvk, u) + constant
    ds = (portions * (dp - jnp.sum(dp * portions, axis=-1, keepdims=True))).astype(BF16)
    dsu = nn(ds, u)
    part = jnp.where(mask, nn(dsu.astype(BF16), w_in(wbuf, 1)) * HEAD_DIM**-0.5, 0.0).astype(BF16)
    dq = tn(expand, part).astype(BF16)
    rows16[...] = dr1 + nt(dq, w_in(wbuf, 0))
    du = tn(ds, qk_i[...]) * HEAD_DIM**-0.5 + tn(low, dvk)
    is_cls = (iota((TOK, 1), 0) == 0) | (iota((TOK, 1), 0) == start)
    tg_out[...] = du + jnp.where(is_cls, 0.0, dz[...])
    tg_out[0:1, :] = tg_out[0:1, :] + rows16[0:1, :]
    tg_out[pl.ds(start, 1), :] = tg_out[pl.ds(start, 1), :] + rows16[1:2, :]
    for row, rows in ((R_H, h_i), (R_ATT, att_i), (R_U, ucls), (R_Q, q_i)):
        pay[row : row + 2, :] = rows[...].astype(F32)[0:2, :]
    for row, rows in ((R_DO, do), (R_DQ, dq), (R_DATT, datt)):
        pay[row : row + 2, :] = rows.astype(F32)[0:2, :]
    pay[R_WK : R_WK + 24, :] = dsu[0:24, :] * HEAD_DIM**-0.5
    pay[R_PU : R_PU + 24, :] = pu_i[...].astype(F32)[0:24, :]
    pay[R_VEC : R_VEC + 12, :] = vg1[0:12, :]
    pay_out[...] = pay[...].astype(BF16)


def lanes(p):
    return pl.ds(pl.multiple_of(128 * p, 128), 128)


def send_groups(info, grads, planes, outs, sem):
    sends = []
    for other in (1, 0):
        for i, t in enumerate(planes):
            for kind, parts in ((3, ((SY + 144 * i, 0), (SX + 144 * i, 144))),
                                (1, ((QX + 144 * i, 0), (SX + 288 + 144 * i, 144))),
                                (2, ((SY + 288 + 144 * i, 0), (QY + 144 * i, 144))),
                                (0, ((OWN + 288 * i, 0),))):
                dev = owner(info, t, kind, other)
                rows = 288 if kind == 0 else 144
                for to, lo in parts:
                    source = grads.at[pl.ds(pl.multiple_of(288 * dev + lo, 16), rows)]
                    sends.append(pltpu.make_async_copy(source, outs[1 - other][to // HALF].at[pl.ds(to % HALF, rows)], sem.at[len(sends)]))
                    sends[-1].start()
    return sends


def second_block(info, u_ref, cot_ref, y_ref, *refs):
    pieces = refs[:32]
    diagonals = {4 * i + 3: refs[32 + i] for i in range(8)}
    head_out, dr_out, vg_out, zb, qs, ks, vs, att = refs[40:48]
    pm_out, w1_grad, theirs1, theirs2, mine1, mine2 = refs[48:54]
    (vec, vbuf, wflat, w1, grads, zf, pm, xh1, hb, ht, gp, es, das, xh2, acc, stage, dfs, sem, osem) = refs[54:]
    wait_vecs, wait = fill(info, pieces, diagonals, 1, wflat, vbuf, sem)
    wbuf = wflat.reshape(GRANS, GRAN, D)
    gbuf = grads.reshape(GRANS, GRAN, D)
    start = info[5]
    zf[...] = u_ref[...].astype(F32)
    zf[0:1, :] = y_ref[0:1, :]
    zf[pl.ds(start, 1), :] = y_ref[1:2, :]
    z16 = zf[...].astype(BF16)
    zb[...] = z16
    wait_vecs()
    order_vec(vbuf, 1, vec)
    wait(0)
    qs[...] = (nn(z16, w_in(wbuf, 0)) + vec[V_BQ : V_BQ + 1, :]).astype(BF16)
    ks[...] = nn(z16, w_in(wbuf, 1)).astype(BF16)
    vs[...] = (nn(z16, w_in(wbuf, 2)) + vec[V_BV : V_BV + 1, :]).astype(BF16)
    low_lane = iota((TOK, 128), 1) < HEAD_DIM
    same = (iota((TOK, TOK), 0) >= start) == (iota((TOK, TOK), 1) >= start)

    def attend(p, carry):
        qp, kp, vp = qs[:, lanes(p)], ks[:, lanes(p)], vs[:, lanes(p)]
        res = []
        for hh in range(2):
            qm = jnp.where(low_lane == (hh == 0), qp, jnp.zeros_like(qp))
            s = jnp.where(same, nt(qm, kp) * HEAD_DIM**-0.5, masked_score)
            raised = jnp.exp(s - jnp.max(s, axis=-1, keepdims=True))
            portions = raised / jnp.sum(raised, axis=-1, keepdims=True)
            pm[2 * p + hh] = portions
            res.append(nn(portions.astype(BF16), vp))
        att[:, lanes(p)] = jnp.where(low_lane, res[0], res[1]).astype(BF16)
        return carry

    lax.fori_loop(0, 6, attend, 0, unroll=True)
    saved = [pltpu.make_async_copy(pm, pm_out, osem.at[28])]
    saved[0].start()
    wait(1)
    xhat, rstd1 = norm_forward(zf[...] + (nn(att[...], w_out(wbuf)) + vec[V_BO : V_BO + 1, :]))
    xh1[...] = xhat
    h = xhat * vec[V_G1 : V_G1 + 1, :] + vec[V_C1 : V_C1 + 1, :]
    hb[...] = h.astype(BF16)
    ht[...] = h.T.astype(BF16)
    acc[...] = h + vec[V_B2 : V_B2 + 1, :]
    wait(2)
    split_w1(wbuf, w1)
    wait(3)
    for j in range(4):
        e, slope = gelu_both(nn(hb[...], w1[j]) + vec[V_B1 + j : V_B1 + j + 1, :])
        gp[j] = slope
        e = e.astype(BF16)
        es[j] = e
        acc[...] += nn(e, w_shrink(wbuf, j))
    xhat, rstd2 = norm_forward(acc[...])
    xh2[...] = xhat
    head_out[...] = (xhat * vec[V_G2 : V_G2 + 1, :] + vec[V_C2 : V_C2 + 1, :]).astype(BF16)

    vg_out[...] = jnp.zeros((16, D), F32)
    dy = cot_ref[...].astype(F32)
    vg_out[V_G2 : V_G2 + 1, :] = colsum(dy * xh2[...])
    vg_out[V_C2 : V_C2 + 1, :] = colsum(dy)
    dr = norm_backward(dy, vec[V_G2 : V_G2 + 1, :], xh2[...], rstd2)
    acc[...] = dr
    df = dr.astype(BF16)
    dfs[...] = df
    vg_out[V_B2 : V_B2 + 1, :] = colsum(df.astype(F32))
    for j in range(4):
        df = dfs[...]
        gbuf[64 + 8 * j : 72 + 8 * j] = tn(es[j], df).astype(BF16).reshape(8, GRAN, D)
        da = (gp[j] * nt(df, w_shrink(wbuf, j))).astype(BF16)
        das[j] = da
        vg_out[V_B1 + j : V_B1 + j + 1, :] = colsum(da.astype(F32))

    def expand_grad(i, carry):
        rows = ht[pl.ds(pl.multiple_of(192 * i, 192), 192), :]
        for j in range(4):
            stage[:, 24 * j : 24 * (j + 1), :] = nn(rows, das[j]).reshape(8, 24, D)
        gbuf[pl.ds(32 + 8 * i, 8)] = stage[...].astype(BF16)
        return carry

    lax.fori_loop(2, 4, expand_grad, 0)
    saved += send_groups(info, grads, GROUPS[0], ((theirs1, theirs2), (mine1, mine2)), osem)
    lax.fori_loop(0, 2, expand_grad, 0)
    saved.append(pltpu.make_async_copy(grads.at[pl.ds(3072, 1536)], w1_grad, osem.at[29]))
    saved[-1].start()
    for j in range(4):
        acc[...] += nt(das[j], w1[j])
    dh = acc[...]
    vg_out[V_G1 : V_G1 + 1, :] = colsum(dh * xh1[...])
    vg_out[V_C1 : V_C1 + 1, :] = colsum(dh)
    dr_out[...] = norm_backward(dh, vec[V_G1 : V_G1 + 1, :], xh1[...], rstd1)
    for copy in saved:
        copy.wait()


def second_attention(info, dr, vg_in, zb, qs, ks, vs, att, *refs):
    pieces = refs[:32]
    pm_in, w1_grad, dz_out, vg_out, theirs1, theirs2, mine1, mine2, wflat, grads, pm, datt, dqs, dks, dvs, sem = refs[32:]
    wbuf = wflat.reshape(GRANS // 2, GRAN, D)
    gbuf = grads.reshape(GRANS // 2, GRAN, D)
    waits = []
    for other in (0, 1):
        for k in range(4):
            for kind in range(4):
                i = 16 * other + 4 * k + kind
                dev = owner(info, (info[1] + 4 - k) & 3, kind, other)
                source = pieces[i].at[pl.ds(SEND_ONE if kind < 3 or k == 2 else 0, 288)]
                rows = pl.ds(pl.multiple_of(288 * jnp.minimum(dev, 15), 16), 288)
                copy = pltpu.make_async_copy(source, wflat.at[rows], sem.at[i])
                used = dev < 11
                pl.when(used)(copy.start)
                waits.append((used, copy))
    saved = [
        pltpu.make_async_copy(pm_in, pm, sem.at[32]),
        pltpu.make_async_copy(w1_grad, grads.at[pl.ds(3072, 1536)], sem.at[33]),
    ]
    for copy in saved:
        copy.start()
    vg_out[...] = vg_in[...]
    do = dr[...].astype(BF16)
    vg_out[V_BO : V_BO + 1, :] = colsum(do.astype(F32))
    gbuf[24:32] = tn(att[...], do).astype(BF16).reshape(8, GRAN, D)
    for used, copy in waits:
        pl.when(used)(copy.wait)
    datt[...] = nt(do, w_out(wbuf)).astype(BF16)
    saved[0].wait()
    low_lane = iota((TOK, 128), 1) < HEAD_DIM

    def attend_back(p, carry):
        qp, kp, vp, dp_ = qs[:, lanes(p)], ks[:, lanes(p)], vs[:, lanes(p)], datt[:, lanes(p)]
        dq, dk, dv = [], [], []
        for hh in range(2):
            portions = pm[2 * p + hh]
            dam = jnp.where(low_lane == (hh == 0), dp_, jnp.zeros_like(dp_))
            dp = nt(dam, vp)
            dv.append(tn(portions.astype(BF16), dp_))
            ds = (portions * (dp - jnp.sum(dp * portions, axis=-1, keepdims=True))).astype(BF16)
            dq.append(nn(ds, kp))
            dk.append(tn(ds, qp))
        dqs[:, lanes(p)] = (jnp.where(low_lane, dq[0], dq[1]) * HEAD_DIM**-0.5).astype(BF16)
        dks[:, lanes(p)] = (jnp.where(low_lane, dk[0], dk[1]) * HEAD_DIM**-0.5).astype(BF16)
        dvs[:, lanes(p)] = jnp.where(low_lane, dv[0], dv[1]).astype(BF16)
        return carry

    lax.fori_loop(0, 6, attend_back, 0, unroll=True)
    vg_out[V_BQ : V_BQ + 1, :] = colsum(dqs[...].astype(F32))
    vg_out[V_BV : V_BV + 1, :] = colsum(dvs[...].astype(F32))
    dz = dr[...]
    for j, part in enumerate((dqs, dks, dvs)):
        gbuf[0:24, 32 * j : 32 * (j + 1), :] = tn(zb[...], part[...]).astype(BF16).reshape(24, 32, D)
    saved[1].wait()
    sends = send_groups(info, grads, GROUPS[1], ((theirs1, theirs2), (mine1, mine2)), sem)
    for j, part in enumerate((dqs, dks, dvs)):
        dz = dz + nt(part[...], w_in(wbuf, j))
    dz_out[...] = dz
    for copy in sends:
        copy.wait()


def total_kernel(mine, came, over_x, over_y, last_x, last_y, first, second):
    for i, out in enumerate((first, second)):
        part = slice(144 * i, 144 * (i + 1))
        for half, (one, two) in enumerate(((last_x, over_y), (over_x, last_y))):
            own = slice(288 * i + 144 * half, 288 * i + 144 * (half + 1))
            both = mine[own, :].astype(F32) + came[own, :].astype(F32)
            out[144 * half : 144 * (half + 1), :] = (
                both + one[part, :].astype(F32) + two[part, :].astype(F32)
            ).astype(BF16)


def owner_grad(info, *refs):
    pieces = refs[:10]
    out, vec_out, pbuf, abuf, qbuf, sem = refs[10:]
    copies = []
    at = 0
    for i, piece in enumerate(pieces):
        copies.append(pltpu.make_async_copy(piece, pbuf.at[pl.ds(at, piece.shape[0])], sem.at[i]))
        at += piece.shape[0]
    for c in copies:
        c.start()
    for c in copies:
        c.wait()
    n_rows = 32 * PAY
    each = pbuf.reshape(32, PAY, D)
    r, c = iota((PAY, n_rows), 0), iota((PAY, n_rows), 1)
    place = c - PAY * ((c * 43691) >> 22)
    tot = nn((place == r).astype(BF16), pbuf[...])
    for row, first in [(V_BQ, R_DQ), (V_BV, R_DATT), (V_BO, R_DO), (V_B2, R_DF)] + [
        (V_B1 + j, R_DA + 2 * j) for j in range(4)
    ]:
        vec_out[row : row + 1, :] = tot[first : first + 1, :] + tot[first + 1 : first + 2, :]
    vec_out[V_G1 : V_C1 + 1, :] = tot[R_VEC + 12 : R_VEC + 14, :]
    vec_out[V_G2 : V_C2 + 1, :] = tot[R_VEC + 14 : R_VEC + 16, :]
    vec_out[12:24, :] = tot[R_VEC : R_VEC + 12, :]

    def pick_rows(*firsts):
        r, c = iota((64, n_rows), 0), iota((64, n_rows), 1)
        base = PAY * (r >> 1) + (r & 1)
        select = jnp.concatenate([(c == base + first).astype(BF16) for first in firsts], 0)
        got = nn(select, pbuf[...]).astype(BF16)
        return [got[64 * i : 64 * (i + 1), :] for i in range(len(firsts))]

    def chosen(count, offset, source):
        one_hot = (iota((count, D), 1) == iota((count, D), 0) + offset).astype(BF16)
        return nt(one_hot, source).astype(BF16)

    def put(gi, n, p, value):
        m = GRAN // n
        for j in range(6):
            out[pl.ds(6 * (GRAN * gi + p) + j, m, stride=6 * n), :] = value[:, 128 * j : 128 * (j + 1)]

    @pl.when(info[0] < 8)
    def _():
        off = GRAN * info[0]
        ucls, dq, q, datt = pick_rows(R_U, R_DQ, R_Q, R_DATT)
        parts = [nn(chosen(GRAN, off, ucls), dq)]
        r, c = iota((D, 64), 0), iota((D, 64), 1)
        inside = r - 24 * (c >> 1)
        expand = ((inside >= 0) & (inside < 24) & ((r & 1) == (c & 1))).astype(BF16)
        r = iota((D, D), 0)
        mine = (r - 24 * ((r * 2731) >> 16)) >> 1 == iota((D, D), 1) >> 6
        for right, lo, skip in ((q, 32, 0), (datt, 48, 8)):
            qbuf[...] = jnp.where(mine, nn(expand, right), 0.0).astype(BF16)

            def compact(i, carry, lo=lo, skip=skip):
                rows = each[pl.ds(8 * i, 8), lo : lo + 32, :].astype(F32)
                abuf[pl.ds(pl.multiple_of(192 * i, 192), 192), :] = (
                    rows[:, skip : skip + 24, :].reshape(192, D).astype(BF16)
                )
                return carry

            lax.fori_loop(0, 4, compact, 0)
            parts.append(nn(chosen(GRAN, off, abuf[...]), qbuf[...]))
        for gi in range(3):
            for p in range(3):
                put(gi, 3, p, parts[p][32 * gi : 32 * (gi + 1), :])

    for gi in range(3):
        g = 3 * info[0] + gi

        @pl.when((g >= 24) & (g < 32))
        def _(gi=gi, g=g):
            left, right = pick_rows(R_ATT, R_DO)
            put(gi, 1, 0, nn(chosen(GRAN, GRAN * (g - 24), left), right))

        @pl.when((g >= 32) & (g < 64))
        def _(gi=gi, g=g):
            left, *rights = pick_rows(R_H, *[R_DA + 2 * p for p in range(4)])
            left = chosen(32, 24 * (g - 32), left)
            for p in range(4):
                put(gi, 4, p, nn(left, rights[p])[0:24, :])

        @pl.when(g >= 64)
        def _(gi=gi, g=g):
            left, right = pick_rows(R_E + 2 * ((g - 64) >> 3), R_DF)
            put(gi, 1, 0, nn(chosen(GRAN, GRAN * ((g - 64) & 7), left), right))


def join_grads(info, g0, a, b, gv, out, square, buf):
    g = g0[...]
    out[pl.ds(0, 1728, stride=2), :] = g
    buf[...] = a[...].astype(F32) + b[...].astype(F32)
    total = buf[...]
    sq = jnp.sum((g * g).reshape(216, 8, 128), axis=0)
    for j in range(6):
        v = total[:, 128 * j : 128 * (j + 1)]
        sq = sq + jnp.sum((v * v).reshape(36, 8, 128), axis=0)
    whole = jnp.sum(colsum(sq), axis=1, keepdims=True)
    whole = whole + jnp.sum(colsum(gv[...] * gv[...]), axis=1, keepdims=True)
    square[...] = jnp.broadcast_to(whole, (8, 128))
    for gi in range(3):

        def emit(n, gi=gi):
            m = GRAN // n
            for p in range(n):
                for j in range(6):
                    out[pl.ds(12 * (GRAN * gi + p) + 2 * j + 1, m, stride=12 * n), :] = buf[
                        GRAN * gi + m * p : GRAN * gi + m * (p + 1), 128 * j : 128 * (j + 1)
                    ]

        by_kind(3 * info[0] + gi, emit)


def adamw_kernel(sq, w, m, v, g, vw, vm, vv, vg, w_new, m_new, v_new, vw_new, vm_new, vv_new, norm_out):
    norm = jnp.sqrt(sq[...])
    norm_out[0, 0] = norm[0, 0]
    coef = jnp.minimum(1.0, math.sqrt(2 * (PL + QL)) / (norm[0:1, 0:1] + 1e-06))
    w_new[...], m_new[...], v_new[...] = adamw_update(w[...], m[...], v[...], g[...] * coef, 0.1, weight_decay)
    vw_new[...], vm_new[...], vv_new[...] = adamw_update(vw[...], vm[...], vv[...], vg[...] * coef, 0.5, 0.0)


def adamw_update(weight, moment_one, moment_two, gradient, step_rate, decay_rate):
    first_new = beta_one * moment_one + (1.0 - beta_one) * gradient
    second_new = beta_two * moment_two + (1.0 - beta_two) * gradient * gradient
    first_hat = first_new / (1.0 - beta_one**STEP)
    second_hat = second_new / (1.0 - beta_two**STEP)
    weight_new = weight - step_rate * (first_hat / (jnp.sqrt(second_hat) + adam_epsilon) + decay_rate * weight)
    return (weight_new, first_new, second_new)


def order_kernel(info, a3, a2, mine, came, over_x, over_y, last_x, last_y, o1, o2, o3, o0, acc):
    acc[3], acc[2] = a3[...], a2[...]
    total_kernel(mine, came, over_x, over_y, last_x, last_y, acc.at[1], acc.at[0])
    for k, out in enumerate((o1, o2, o3, o0)):
        out[...] = acc[(info[1] + 3 - k) & 3]


SMEM = pl.BlockSpec(memory_space=pltpu.SMEM)
VMEM = pl.BlockSpec(memory_space=pltpu.VMEM)
ANY = pl.BlockSpec(memory_space=pl.ANY)


def struct(*shape, dtype=F32):
    return jax.ShapeDtypeStruct(shape, dtype)


def call(kernel, name, ins, in_specs, outs, out_specs, scratch=(), flops=0, moved=0):
    return pl.pallas_call(
        kernel,
        out_shape=outs,
        in_specs=in_specs,
        out_specs=out_specs,
        scratch_shapes=list(scratch),
        name=name,
        compiler_params=pltpu.CompilerParams(vmem_limit_bytes=VMEM_BYTES),
        cost_estimate=pl.CostEstimate(flops=flops, bytes_accessed=moved, transcendentals=0),
    )(*ins)


def flat_view(a):
    return a.reshape(2, -1, 128).transpose(1, 0, 2).reshape(-1, 128)


def flat_back(a):
    return a.reshape(-1, 2, 128).transpose(1, 0, 2).reshape(2, -1)


def body(tokens, cotangent, lengths, mats, mats_m, mats_v, vecs, vecs_m, vecs_v):
    dp, pair = lax.axis_index("dp"), lax.axis_index("pair")
    device = 2 * dp + pair
    z = dp >> 2
    info = jnp.stack(
        [device, z, (dp >> 1) & 1, dp & 1, pair, lengths[0, 0, 0], jnp.int32(0), jnp.int32(0)]
    ).astype(jnp.int32)
    u = tokens[0]
    cot = cotangent[0]
    flat = flat_view(mats)
    own = call(pack_kernel, "pack", (info, flat, vecs), [SMEM, VMEM, VMEM], struct(SEND, D, dtype=BF16), VMEM)
    pieces0, pieces1 = gather_blocks(own)
    row = struct(16, D)
    row16 = struct(16, D, dtype=BF16)
    saved_shapes = (
        row, struct(16, 128), row, struct(16, 128), struct(4, 16, D), struct(4, 16, D, dtype=BF16),
        row16, row16, row16, row16, struct(32, D, dtype=BF16), struct(32, D, dtype=BF16), struct(32, TOK),
    )
    weights = [
        pltpu.VMEM((16, D), F32),
        pltpu.VMEM((32, 16, D), BF16),
        pltpu.VMEM((GRANS * GRAN, D), BF16),
        pltpu.VMEM((4, D, D), BF16),
    ]
    y_cls, cls, *saved = call(
        first_forward,
        "first_forward",
        (info, u, *pieces0),
        [SMEM, VMEM] + [ANY] * 32,
        (row, struct(2, D, dtype=BF16), *saved_shapes),
        (VMEM,) * 15,
        weights + [pltpu.SemaphoreType.DMA((64,))],
        flops=2 * 32 * PL,
        moved=2 * PL,
    )
    part = struct(HALF, D, dtype=BF16)
    mid16 = pltpu.VMEM((TOK, D), BF16)
    mid = pltpu.VMEM((TOK, D), F32)
    low = struct(TOK, D, dtype=BF16)
    head_out, dr, vg1, zb, qs, ks, vs, att, pm, w1_grad, theirs_a1, theirs_a2, mine_a1, mine_a2 = call(
        second_block,
        "second_block",
        (info, u, cot, y_cls, *pieces1, *pieces0[3::4]),
        [SMEM, VMEM, VMEM, VMEM] + [ANY] * 40,
        (low, struct(TOK, D), row, low, low, low, low, low, struct(HEADS, TOK, TOK), struct(1536, D, dtype=BF16)) + (part,) * 4,
        (VMEM,) * 8 + (ANY,) * 6,
        weights
        + [
            pltpu.VMEM((GRANS * GRAN, D), BF16),
            mid,
            pltpu.VMEM((HEADS, TOK, TOK), F32),
            mid, mid16,
            pltpu.VMEM((D, TOK), BF16),
            pltpu.VMEM((4, TOK, D), F32),
            pltpu.VMEM((4, TOK, D), BF16),
            pltpu.VMEM((4, TOK, D), BF16),
            mid, mid,
            pltpu.VMEM((8, GRAN, D), F32),
            mid16,
            pltpu.SemaphoreType.DMA((64,)),
            pltpu.SemaphoreType.DMA((30,)),
        ],
        flops=4 * TOK * PL,
        moved=4 * PL,
    )

    def first_part(mine, came):
        return [add16(mine[lo:hi], came[lo:hi]) for lo, hi in ((SX, SY), (SY, QX))]

    def last_part(mine, came, over_x, over_y):
        return [
            (mine[lo : lo + 288].astype(F32) + came[lo : lo + 288].astype(F32) + over[:288].astype(F32)).astype(BF16)
            for lo, over in ((QX - HALF, over_y), (QY - HALF, over_x))
        ]

    own_rows, half = pl.BlockSpec((576, D), lambda i: (1, 0)), pl.BlockSpec((288, D), lambda i: (0, 0))
    second = pl.BlockSpec((288, D), lambda i: (1, 0))

    def plane_total(mine, came, over_x, over_y, last_x, last_y):
        return pl.pallas_call(
            total_kernel,
            grid=(1,),
            in_specs=[own_rows, own_rows, second, second, half, half],
            out_specs=[half, half],
            out_shape=[struct(288, D, dtype=BF16)] * 2,
            name="total",
        )(mine, came, over_x, over_y, last_x, last_y)

    cls = gather_step(cls, 0, device)()
    theirs_a1, theirs_a2, cls = fence([theirs_a1, theirs_a2, cls])
    came_a1, came_a2 = core_flip(theirs_a1), core_flip(theirs_a2)
    cls = gather_step(cls, 1, device)()
    sx, sy, cls, dr = fence([*first_part(mine_a1, came_a1), cls, dr])
    over_xa, over_ya = x_flip(sx), y_flip(sy)
    dz, vg1, theirs_b1, theirs_b2, mine_b1, mine_b2 = call(
        second_attention,
        "second_attention",
        (info, dr, vg1, zb, qs, ks, vs, att, *pieces1, pm, w1_grad),
        [SMEM] + [VMEM] * 7 + [ANY] * 34,
        (struct(TOK, D), row) + (part,) * 4,
        (VMEM, VMEM) + (ANY,) * 4,
        [
            pltpu.VMEM((GRANS * GRAN // 2, D), BF16),
            pltpu.VMEM((GRANS * GRAN // 2, D), BF16),
            pltpu.VMEM((HEADS, TOK, TOK), F32),
            mid16, mid16, mid16, mid16,
            pltpu.SemaphoreType.DMA((34,)),
        ],
        flops=2 * TOK * PL,
        moved=2 * PL,
    )
    qx_a, qy_a, theirs_b1, theirs_b2, cls = fence(
        [*last_part(mine_a2, came_a2, over_xa, over_ya), theirs_b1, theirs_b2, cls]
    )
    last_xa, last_ya = x_flip(qx_a), y_flip(qy_a)
    came_b1 = core_flip(theirs_b1)
    every_cls = gather_step(cls, 2, device)()
    sx, sy, dz, theirs_b2 = fence([*first_part(mine_b1, came_b1), dz, theirs_b2])
    over_xb, over_yb = x_flip(sx), y_flip(sy)
    came_b2 = core_flip(theirs_b2)
    token_grad, payload, loss = call(
        first_backward,
        "first_backward",
        (info, u, every_cls, dz, vg1, *saved, *pieces0),
        [SMEM] + [VMEM] * 17 + [ANY] * 32,
        (struct(TOK, D), struct(PAY, D, dtype=BF16), struct(1, 1)),
        (VMEM, VMEM, SMEM),
        weights
        + [
            pltpu.VMEM((16, D), F32),
            pltpu.VMEM((64, D), F32),
            pltpu.VMEM((PAY, D), F32),
            pltpu.SemaphoreType.DMA((64,)),
        ],
        flops=2 * 32 * PL,
        moved=2 * PL,
    )
    qx_b, qy_b, pay, last_xa, last_ya = fence(
        [*last_part(mine_b2, came_b2, over_xb, over_yb), payload, last_xa, last_ya]
    )
    last_xb, last_yb = x_flip(qx_b), y_flip(qy_b)
    a3, a2 = plane_total(mine_a2, came_a2, over_xa, over_ya, last_xa, last_ya)
    slots = jnp.concatenate([pay, z_turn(pay, 1), z_turn(pay, 3), z_turn(pay, 2)], 0)
    in_turn = pl.pallas_call(
        order_kernel,
        grid=(1,),
        in_specs=[SMEM, half, half, own_rows, own_rows, second, second, half, half],
        out_specs=[half] * 4,
        out_shape=[struct(288, D, dtype=BF16)] * 4,
        scratch_shapes=[pltpu.VMEM((4, 288, D), BF16)],
        name="order",
    )(info, a3, a2, mine_b2, came_b2, over_xb, over_yb, last_xb, last_yb)
    moving = z_up(in_turn[0])
    over_x, over_y = x_flip(slots), y_flip(slots)
    rows = [slots, over_x, over_y]
    moving = z_up(add16(in_turn[1], moving))
    half = rows[0].shape[0] // 2
    rows += [y_flip(rows[1][:half]), x_flip(rows[2][half:])]
    rows += [core_flip(v) for v in rows]
    moving = z_up(add16(in_turn[2], moving))
    flat0, vec_sum = call(
        owner_grad,
        "owner_grad",
        (info, *rows),
        [SMEM] + [ANY] * 10,
        (struct(1728, 128), struct(24, D)),
        (VMEM, VMEM),
        [
            pltpu.VMEM((32 * PAY, D), BF16),
            pltpu.VMEM((D, D), BF16),
            pltpu.VMEM((D, D), BF16),
            pltpu.SemaphoreType.DMA((10,)),
        ],
        flops=2 * 768 * 768 * 768,
        moved=2 * 32 * PAY * D,
    )
    grad_vecs = lax.dynamic_slice(vec_sum.reshape(2, QL), (0, device * vecs.shape[1]), vecs.shape)
    grads, square = call(
        join_grads,
        "join_grads",
        (info, flat0, in_turn[3], moving, grad_vecs),
        [SMEM] + [VMEM] * 4,
        (struct(3456, 128), struct(8, 128)),
        (VMEM, VMEM),
        [pltpu.VMEM((288, D), F32)],
    )
    block = pl.BlockSpec((864, 128), lambda i: (i, 0))
    small = pl.BlockSpec(vecs.shape, lambda i: (0, 0))
    tile = pl.BlockSpec((8, 128), lambda i: (0, 0))
    *new, new_vecs, new_vecs_m, new_vecs_v, norm = pl.pallas_call(
        adamw_kernel,
        grid=(4,),
        in_specs=[tile] + [block] * 4 + [small] * 4,
        out_specs=(block,) * 3 + (small,) * 3 + (SMEM,),
        out_shape=(struct(3456, 128),) * 3 + (struct(*vecs.shape),) * 3 + (struct(1, 1),),
        name="adamw",
    )(sum_quick(square), flat, flat_view(mats_m), flat_view(mats_v), grads, vecs, vecs_m, vecs_v, grad_vecs)
    new_mats, new_mats_m, new_mats_v = [flat_back(a) for a in new]
    return (
        head_out[None],
        token_grad[None],
        loss.reshape(()),
        norm.reshape(()),
        new_mats,
        new_mats_m,
        new_mats_v,
        new_vecs,
        new_vecs_m,
        new_vecs_v,
    )


def matmul(left_side, right_side):
    return jnp.dot(left_side, right_side, preferred_element_type=jnp.float32)


def inner_rows(left_side, right_side):
    return lax.dot_general(
        left_side, right_side, (((0,), (0,)), ((), ())), preferred_element_type=jnp.float32
    )


def outer_cols(left_side, right_side):
    return lax.dot_general(
        left_side, right_side, (((1,), (1,)), ((), ())), preferred_element_type=jnp.float32
    )


def exact_dot(left_side, right_side):
    return jnp.dot(
        left_side, right_side, precision=lax.Precision.HIGHEST, preferred_element_type=jnp.float32
    )


def layer_norm(resid, gain, shift):
    centred = resid - jnp.mean(resid, axis=-1, keepdims=True)
    spread = jnp.mean(centred * centred, axis=-1, keepdims=True)
    return centred * lax.rsqrt(spread + norm_epsilon) * gain + shift


def gelu_exact(before):
    return jax.nn.gelu(before, approximate=False)


def unpack(mat_row, vec_row):
    edge_one = 3 * D * D
    edge_two = 4 * D * D
    edge_three = edge_two + D * FF
    input_weight = mat_row[:edge_one].reshape(D, 3 * D)
    output_weight = mat_row[edge_one:edge_two].reshape(D, D)
    expand_weight = mat_row[edge_two:edge_three].reshape(D, FF)
    shrink_weight = mat_row[edge_three:].reshape(FF, D)
    vector = vec_row.astype(jnp.float32)
    pieces = []
    cursor = 0
    for piece_len in (D, D, D, D, D, FF, D, D, D):
        pieces.append(vector[cursor : cursor + piece_len])
        cursor = cursor + piece_len
    return (input_weight, output_weight, expand_weight, shrink_weight) + tuple(pieces)


def head_scores(queries, key_rows, same_span):
    row_count = queries.shape[0]
    query_heads = queries.reshape(row_count, HEADS, HEAD_DIM)
    key_heads = key_rows.reshape(row_count, HEADS, HEAD_DIM)
    scores = jnp.einsum(
        "thd,shd->hts", query_heads, key_heads, preferred_element_type=jnp.float32
    ) * HEAD_DIM ** (-0.5)
    return jnp.where(same_span[None, :, :], scores, masked_score)


def layer_forward(params, inputs, same_span):
    (
        input_weight,
        output_weight,
        expand_weight,
        shrink_weight,
        query_bias,
        value_bias,
        output_bias,
        first_gain,
        first_shift,
        expand_bias,
        shrink_bias,
        second_gain,
        second_shift,
    ) = params
    row_count = inputs.shape[0]
    low_input = inputs.astype(jnp.bfloat16)
    joint = matmul(low_input, input_weight)
    queries = (joint[:, :D] + query_bias).astype(jnp.bfloat16)
    key_rows = joint[:, D : 2 * D].astype(jnp.bfloat16)
    values = (joint[:, 2 * D :] + value_bias).astype(jnp.bfloat16)
    scores = head_scores(queries, key_rows, same_span)
    row_max = jnp.max(scores, axis=-1, keepdims=True)
    raised = jnp.exp(scores - row_max)
    summed = jnp.sum(raised, axis=-1, keepdims=True)
    portions = raised / summed
    logsum = row_max + jnp.log(summed)
    value_heads = values.reshape(row_count, HEADS, HEAD_DIM)
    attended = jnp.einsum(
        "hts,shd->thd",
        portions.astype(jnp.bfloat16),
        value_heads,
        preferred_element_type=jnp.float32,
    )
    attended = attended.reshape(row_count, D).astype(jnp.bfloat16)
    resid_one = inputs + (matmul(attended, output_weight) + output_bias)
    hidden = layer_norm(resid_one, first_gain, first_shift)
    low_hidden = hidden.astype(jnp.bfloat16)
    before = matmul(low_hidden, expand_weight) + expand_bias
    activated = gelu_exact(before).astype(jnp.bfloat16)
    resid_two = hidden + (matmul(activated, shrink_weight) + shrink_bias)
    output = layer_norm(resid_two, second_gain, second_shift)
    kept = (
        low_input,
        queries,
        key_rows,
        values,
        logsum,
        attended,
        resid_one,
        low_hidden,
        before,
        activated,
        resid_two,
    )
    return (output, kept)


def layer_backward(params, kept, grad_out, same_span):
    (
        input_weight,
        output_weight,
        expand_weight,
        shrink_weight,
        query_bias,
        value_bias,
        output_bias,
        first_gain,
        first_shift,
        expand_bias,
        shrink_bias,
        second_gain,
        second_shift,
    ) = params
    (
        low_input,
        queries,
        key_rows,
        values,
        logsum,
        attended,
        resid_one,
        low_hidden,
        before,
        activated,
        resid_two,
    ) = kept
    row_count = low_input.shape[0]
    _, norm_pull_two = jax.vjp(layer_norm, resid_two, second_gain, second_shift)
    d_resid_two, d_second_gain, d_second_shift = norm_pull_two(grad_out)
    d_feed = d_resid_two.astype(jnp.bfloat16)
    d_shrink = inner_rows(activated, d_feed)
    d_shrink_bias = jnp.sum(d_feed.astype(jnp.float32), axis=0)
    _, gelu_pull = jax.vjp(gelu_exact, before)
    d_before = gelu_pull(outer_cols(d_feed, shrink_weight))[0].astype(jnp.bfloat16)
    d_expand = inner_rows(low_hidden, d_before)
    d_expand_bias = jnp.sum(d_before.astype(jnp.float32), axis=0)
    d_hidden = d_resid_two + outer_cols(d_before, expand_weight)
    _, norm_pull_one = jax.vjp(layer_norm, resid_one, first_gain, first_shift)
    d_resid_one, d_first_gain, d_first_shift = norm_pull_one(d_hidden)
    d_branch = d_resid_one.astype(jnp.bfloat16)
    d_output = inner_rows(attended, d_branch)
    d_output_bias = jnp.sum(d_branch.astype(jnp.float32), axis=0)
    d_attended = outer_cols(d_branch, output_weight).astype(jnp.bfloat16)
    portions = jnp.exp(head_scores(queries, key_rows, same_span) - logsum)
    query_heads = queries.reshape(row_count, HEADS, HEAD_DIM)
    key_heads = key_rows.reshape(row_count, HEADS, HEAD_DIM)
    value_heads = values.reshape(row_count, HEADS, HEAD_DIM)
    d_att_heads = d_attended.reshape(row_count, HEADS, HEAD_DIM)
    d_portions = jnp.einsum(
        "thd,shd->hts", d_att_heads, value_heads, preferred_element_type=jnp.float32
    )
    d_values = jnp.einsum(
        "hts,thd->shd",
        portions.astype(jnp.bfloat16),
        d_att_heads,
        preferred_element_type=jnp.float32,
    )
    d_values = d_values.reshape(row_count, D).astype(jnp.bfloat16)
    d_scores = portions * (d_portions - jnp.sum(d_portions * portions, axis=-1, keepdims=True))
    d_scores = d_scores.astype(jnp.bfloat16)
    score_scale = HEAD_DIM ** (-0.5)
    d_queries = (
        jnp.einsum("hts,shd->thd", d_scores, key_heads, preferred_element_type=jnp.float32)
        * score_scale
    )
    d_queries = d_queries.reshape(row_count, D).astype(jnp.bfloat16)
    d_keys = (
        jnp.einsum("hts,thd->shd", d_scores, query_heads, preferred_element_type=jnp.float32)
        * score_scale
    )
    d_keys = d_keys.reshape(row_count, D).astype(jnp.bfloat16)
    d_joint = jnp.concatenate([d_queries, d_keys, d_values], axis=1)
    d_input_weight = inner_rows(low_input, d_joint)
    d_query_bias = jnp.sum(d_queries.astype(jnp.float32), axis=0)
    d_value_bias = jnp.sum(d_values.astype(jnp.float32), axis=0)
    d_inputs = d_resid_one + outer_cols(d_joint, input_weight)
    mat_grad = jnp.concatenate(
        [
            d_input_weight.reshape(-1),
            d_output.reshape(-1),
            d_expand.reshape(-1),
            d_shrink.reshape(-1),
        ]
    )
    vec_grad = jnp.concatenate(
        [
            d_query_bias,
            d_value_bias,
            d_output_bias,
            d_first_gain,
            d_first_shift,
            d_expand_bias,
            d_shrink_bias,
            d_second_gain,
            d_second_shift,
        ]
    )
    return (d_inputs, mat_grad, vec_grad)


def contrast_rows(anchors, key_table, anchor_index, span_count, score_scale):
    key_count = key_table.shape[0]
    key_index = jnp.arange(key_count, dtype=jnp.int32)
    scores = outer_cols(anchors, key_table) * score_scale
    scores = jnp.where(anchor_index[:, None] == key_index[None, :], masked_score, scores)
    partner = (
        jnp.bitwise_xor(anchor_index // span_count, 1) * span_count + anchor_index % span_count
    )
    row_max = jnp.max(scores, axis=-1, keepdims=True)
    raised = jnp.exp(scores - row_max)
    summed = jnp.sum(raised, axis=-1, keepdims=True)
    logsum = row_max[:, 0] + jnp.log(summed[:, 0])
    target = key_index[None, :] == partner[:, None]
    positive = jnp.sum(jnp.where(target, scores, 0.0), axis=1)
    grads_low = (raised / summed - target.astype(jnp.float32)).astype(jnp.bfloat16)
    return (grads_low, logsum - positive)


def general_body(tokens, cotangent, lengths, mats, mats_m, mats_v, vecs, vecs_m, vecs_v):
    full_mats, full_vecs = (
        lax.all_gather(mats.astype(jnp.bfloat16), ("dp", "pair"), axis=1, tiled=True),
        lax.all_gather(vecs.astype(jnp.bfloat16), ("dp", "pair"), axis=1, tiled=True),
    )
    layer_one = unpack(full_mats[0], full_vecs[0])
    layer_two = unpack(full_mats[1], full_vecs[1])
    inputs = tokens[0].astype(jnp.float32)
    row_count = inputs.shape[0]
    span_lengths = lengths[0, 0]
    span_count = span_lengths.shape[0]
    positions = jnp.arange(row_count, dtype=jnp.int32)
    order = jnp.arange(span_count)
    starts = jnp.sum(jnp.where(order[None, :] < order[:, None], span_lengths[None, :], 0), axis=1)
    span_of = jnp.sum((positions[:, None] >= starts[None, :]).astype(jnp.int32), axis=1)
    same_span = span_of[:, None] == span_of[None, :]
    heads_mark = positions[None, :] == starts[:, None]
    is_cls = jnp.any(heads_mark, axis=0)[:, None]
    picker = heads_mark.astype(jnp.float32)
    doc_groups = lax.axis_size("dp")
    early_out, kept_one = layer_forward(layer_one, inputs, same_span)
    cls_rows = exact_dot(picker, early_out)
    mixture = jnp.where(is_cls, early_out, inputs)
    late_out, kept_two = layer_forward(layer_two, mixture, same_span)
    sent_cls = cls_rows.astype(jnp.bfloat16)
    every_cls = lax.all_gather(sent_cls, ("dp", "pair"), axis=0, tiled=True)
    key_count = every_cls.shape[0]
    score_scale = 2.0 / math.sqrt(D)
    offset = lax.axis_index(("dp", "pair")) * span_count
    own_index = offset + jnp.arange(span_count, dtype=jnp.int32)
    grads_low, loss_terms = contrast_rows(sent_cls, every_cls, own_index, span_count, score_scale)
    anchor_part = matmul(grads_low, every_cls) * score_scale
    key_part = lax.psum_scatter(
        inner_rows(grads_low, sent_cls) * score_scale,
        ("dp", "pair"),
        scatter_dimension=0,
        tiled=True,
    )
    cls_grad = anchor_part + key_part
    grad_late = cotangent[0].astype(jnp.float32)
    d_mixture, late_mats, late_vecs = layer_backward(layer_two, kept_two, grad_late, same_span)
    grad_early = jnp.where(is_cls, d_mixture, 0.0) + exact_dot(picker.T, cls_grad)
    d_inputs, early_mats, early_vecs = layer_backward(layer_one, kept_one, grad_early, same_span)
    token_grad = d_inputs + jnp.where(is_cls, 0.0, d_mixture)
    all_pieces = (
        lax.all_to_all(
            early_mats.reshape(doc_groups, -1).astype(jnp.bfloat16),
            "dp",
            split_axis=0,
            concat_axis=0,
            tiled=True,
        ).astype(jnp.float32),
        lax.all_to_all(
            late_mats.reshape(doc_groups, -1).astype(jnp.bfloat16),
            "dp",
            split_axis=0,
            concat_axis=0,
            tiled=True,
        ).astype(jnp.float32),
        lax.all_to_all(
            early_vecs.reshape(doc_groups, -1).astype(jnp.bfloat16),
            "dp",
            split_axis=0,
            concat_axis=0,
            tiled=True,
        ).astype(jnp.float32),
        lax.all_to_all(
            late_vecs.reshape(doc_groups, -1).astype(jnp.bfloat16),
            "dp",
            split_axis=0,
            concat_axis=0,
            tiled=True,
        ).astype(jnp.float32),
    )
    early_mats_part, late_mats_part, early_vecs_part, late_vecs_part = (
        lax.psum_scatter(
            jnp.sum(all_pieces[0], axis=0).astype(jnp.bfloat16),
            "pair",
            scatter_dimension=0,
            tiled=True,
        ).astype(jnp.float32),
        lax.psum_scatter(
            jnp.sum(all_pieces[1], axis=0).astype(jnp.bfloat16),
            "pair",
            scatter_dimension=0,
            tiled=True,
        ).astype(jnp.float32),
        lax.psum_scatter(
            jnp.sum(all_pieces[2], axis=0).astype(jnp.bfloat16),
            "pair",
            scatter_dimension=0,
            tiled=True,
        ).astype(jnp.float32),
        lax.psum_scatter(
            jnp.sum(all_pieces[3], axis=0).astype(jnp.bfloat16),
            "pair",
            scatter_dimension=0,
            tiled=True,
        ).astype(jnp.float32),
    )
    grad_mats = jnp.stack([early_mats_part, late_mats_part])
    grad_vecs = jnp.stack([early_vecs_part, late_vecs_part])
    square_sum = jnp.sum(grad_mats * grad_mats) + jnp.sum(grad_vecs * grad_vecs)
    total_sq, loss_sum = lax.psum((square_sum, jnp.sum(loss_terms)), ("dp", "pair"))
    grad_norm = jnp.sqrt(total_sq)
    clip_factor = jnp.minimum(1.0, math.sqrt(2 * (PL + QL)) / (grad_norm + 1e-06))
    new_mats, new_mats_m, new_mats_v = adamw_update(
        mats, mats_m, mats_v, grad_mats * clip_factor, 0.1, weight_decay
    )
    new_vecs, new_vecs_m, new_vecs_v = adamw_update(
        vecs, vecs_m, vecs_v, grad_vecs * clip_factor, 0.5, 0.0
    )
    contrastive = loss_sum / key_count
    return (
        late_out.astype(jnp.bfloat16)[None],
        token_grad[None],
        contrastive,
        grad_norm,
        new_mats,
        new_mats_m,
        new_mats_v,
        new_vecs,
        new_vecs_m,
        new_vecs_v,
    )


def solution(mesh):
    flat = P(None, ("dp", "pair"))
    rows = P("pair", "dp", None)
    here = dict(mesh.shape) == {"dp": 16, "pair": 2}
    return jax.shard_map(
        body if here else general_body,
        mesh=mesh,
        in_specs=(rows, rows, rows) + (flat,) * 6,
        out_specs=(rows, rows, P(), P()) + (flat,) * 6,
        check_vma=False,
    )
```

```python
import math

import jax
import jax.numpy as jnp
from jax import lax
from jax.experimental import pallas as pl
from jax.experimental.pallas import tpu as pltpu
from jax.sharding import PartitionSpec as P

D = 768
HEADS = 12
HEAD_DIM = 64
FF = 3072
STEP = 10
PL = 7077888
QL = 9216

norm_epsilon = 1e-12
masked_score = -1000000000.0
beta_one = 0.9
beta_two = 0.999
adam_epsilon = 1e-08
weight_decay = 0.01

F32 = jnp.float32
BF16 = jnp.bfloat16
TOK = 256
GRAN = 96
GRANS = PL // D // GRAN
VMEM_BYTES = 66_400_000

V_BQ, V_BV, V_BO, V_G1, V_C1, V_B1, V_B2, V_G2, V_C2 = 0, 1, 2, 3, 4, 5, 9, 10, 11

R_E, R_DF, R_H, R_DA, R_ATT, R_DO, R_U, R_DQ, R_Q, R_DATT, R_WK, R_PU, R_VEC = (
    0, 8, 10, 12, 20, 22, 24, 26, 28, 30, 32, 56, 80,
)
PAY = 96


def nn(a, b):
    return lax.dot_general(a, b, (((1,), (0,)), ((), ())), preferred_element_type=F32)


def nt(a, b):
    return lax.dot_general(a, b, (((1,), (1,)), ((), ())), preferred_element_type=F32)


def tn(a, b):
    return lax.dot_general(a, b, (((0,), (0,)), ((), ())), preferred_element_type=F32)


def iota(shape, axis):
    return lax.broadcasted_iota(jnp.int32, shape, axis)


def erf(x):
    x = jnp.clip(x, -3.832506856900711, 3.832506856900711)
    s = x * x
    top = 0.00022905065861350646
    for c in (0.0034082910107109506, 0.050955695062380861, 0.18520832239976145, 1.128379143519084):
        top = top * s + c
    low = -1.1791602954361697e-7
    for c in (
        0.000023547966471313185,
        0.0010179625278914885,
        0.014070470171167667,
        0.11098505178285362,
        0.49746925110067538,
        1.0,
    ):
        low = low * s + c
    return x * top / low


def gelu_both(a):
    phi = 0.5 + 0.5 * erf(a * math.sqrt(0.5))
    return a * phi, phi + a * jnp.exp(-0.5 * a * a) * (1.0 / math.sqrt(2.0 * math.pi))


def norm_forward(r):
    centred = r - jnp.mean(r, axis=-1, keepdims=True)
    rstd = lax.rsqrt(jnp.mean(centred * centred, axis=-1, keepdims=True) + norm_epsilon)
    return centred * rstd, rstd


def norm_backward(dy, gain, xhat, rstd):
    dx = dy * gain
    return rstd * (
        dx - jnp.mean(dx, axis=-1, keepdims=True) - xhat * jnp.mean(dx * xhat, axis=-1, keepdims=True)
    )


def colsum(v):
    return jnp.sum(v, axis=0, keepdims=True)


def flip(v, axis, bit):
    return lax.ppermute(v, axis, [(i, i ^ bit) for i in range(lax.axis_size(axis))])


def core_flip(v):
    return flip(v, "dp", 1)


def x_flip(v):
    return flip(v, "dp", 2)


def y_flip(v):
    return flip(v, "pair", 1)


def z_up(v):
    n = lax.axis_size("dp")
    return lax.ppermute(v, "dp", [(i, (i + 4) % n) for i in range(n)])


def z_turn(v, places):
    n = lax.axis_size("dp")
    return lax.ppermute(v, "dp", [(i, (i + 4 * places) % n) for i in range(n)])


def xor_flip(v, pair_bit, dp_bits):
    if not pair_bit:
        return flip(v, "dp", dp_bits)
    n = lax.axis_size("dp")
    return lax.ppermute(v, ("dp", "pair"), [(i, i ^ (2 * dp_bits + 1)) for i in range(2 * n)])


def fence(values):
    return list(lax.optimization_barrier(tuple(values)))


SMALL_STEPS = (((1, 0), (0, 1), (1, 1)), ((0, 2), (0, 4), (0, 6)), ((0, 8),))


def gather_step(v, step, device):
    got = [v] + [xor_flip(v, *bits) for bits in SMALL_STEPS[step]]
    here = (device >> (2 * step)) & (len(got) - 1)
    return lambda: jnp.concatenate([pick(here ^ p, got) for p in range(len(got))], 0)


SUM_STEPS = (((0, 1),), ((1, 0), (0, 2), (1, 2)), ((0, 4), (0, 8), (0, 12)))


def sum_quick(v):
    for bits in SUM_STEPS:
        got = [v] + [xor_flip(v, *b) for b in bits]
        v = got[0] + got[1] if len(got) == 2 else (got[0] + got[1]) + (got[2] + got[3])
    return got


def pick(index, cases):
    return lax.select_n(index, *cases)


GATHER_ROUNDS = (
    ("x0", "y0", "s1"),
    ("d0", "e0", "x1", "y1", "s2"),
    ("d1", "e1", "x2", "y2", "s3"),
    ("f2", "x3", "y3"),
    ("d3", "e3"),
)


SEND_VEC, SEND_ONE, SEND = 288, 304, 592


def gather_blocks(own):
    have = {"s0": own}
    across = ["s0"]
    for r, tasks in enumerate(GATHER_ROUNDS):
        sources = {}
        for name in tasks:
            kind, k = name[0], int(name[1])
            sources[name] = {"s": f"s{k - 1}", "x": f"s{k}", "y": f"s{k}", "d": f"x{k}", "e": f"y{k}", "f": f"x{k}"}[kind]
        if "y3" in sources:
            sources["y3"] = "y2"
        names = list(dict.fromkeys([*sources.values(), *across]))
        if r:
            have.update(zip(names, fence([have[i] for i in names])))
        for name, source in sources.items():
            move = {
                "s": z_up, "x": x_flip, "y": y_flip, "f": y_flip, "d": lambda v: y_flip(v[:SEND_ONE]), "e": lambda v: x_flip(v[SEND_ONE:])
            }[name[0]]
            have[name] = z_up(have[source]) if name == "y3" else move(have[source])
        if r in (1, 2):
            names = [*across, *tasks[:2]]
            have.update(zip(names, fence([have[i] for i in names])))
        for i in across:
            have["c" + i] = core_flip(have[i])
        across = list(tasks)
    names = ["cs3", "cx3", "cy3", *across]
    have.update(zip(names, fence([have[i] for i in names])))
    for i in across:
        have["c" + i] = core_flip(have[i])
    orders = [["sxy" + (last if k != 2 else "f") for k in range(4)] for last in "de"]
    return [[have[c + kind + str(k)] for c in ("", "c") for k in range(4) for kind in kinds[k]] for kinds in orders]


def add16(a, b):
    return (a.astype(F32) + b.astype(F32)).astype(BF16)


GROUPS = ((3, 2), (1, 0))
GROUP_ROWS = 2304
HALF = 1152
SX, SY, QX, QY, OWN = 0, 576, 1152, 1440, 1728


def by_kind(granule, emit):
    joint = granule < 24
    wide = (granule >= 32) & (granule < 64)
    pl.when(joint)(lambda: emit(3))
    pl.when(wide)(lambda: emit(4))
    pl.when(jnp.logical_not(joint | wide))(lambda: emit(1))


def pack_kernel(info, flat, vecs, out):
    out[SEND_VEC:SEND_ONE, :] = jnp.zeros((SEND_ONE - SEND_VEC, D), BF16)
    both = vecs[...]
    out[SEND_VEC:SEND_ONE, 0:288] = jnp.concatenate([both, jnp.zeros((14, 288), F32)], 0).astype(BF16)
    for gi in range(3):

        def emit(n, gi=gi):
            m = GRAN // n
            for layer in range(2):
                for j in range(6):
                    parts = [
                        flat[pl.ds(12 * (GRAN * gi + p) + 2 * j + layer, m, stride=12 * n), :] for p in range(n)
                    ]
                    tile = parts[0] if n == 1 else jnp.concatenate(parts, 0)
                    at = SEND_ONE * layer + GRAN * gi
                    out[at : at + GRAN, 128 * j : 128 * (j + 1)] = tile.astype(BF16)

        by_kind(3 * info[0] + gi, emit)


def owner(info, plane, kind, other):
    return (
        8 * plane
        + 4 * jnp.bitwise_xor(info[2], kind & 1)
        + 2 * jnp.bitwise_xor(info[3], other)
        + jnp.bitwise_xor(info[4], kind >> 1)
    )


def fill(info, pieces, diagonals, block, wbuf, vbuf, sem):
    vecs = []
    for other in (0, 1):
        for k in range(4):
            for kind in range(4):
                i = 16 * other + 4 * k + kind
                source = (pieces if kind < 3 else diagonals)[i].at[pl.ds(SEND_VEC, 16)]
                dev = owner(info, (info[1] + 4 - k) & 3, kind, other)
                vecs.append(pltpu.make_async_copy(source, vbuf.at[dev], sem.at[32 + i]))
    for copy in vecs:
        copy.start()

    def copies(plane, k):
        made = []
        for other in (0, 1):
            for kind in range(4):
                source = pieces[16 * other + 4 * k + kind].at[pl.ds(SEND_ONE if block and (kind < 3 or k == 2) else 0, 288)]
                rows = pl.ds(pl.multiple_of(288 * owner(info, plane, kind, other), 16), 288)
                made.append(pltpu.make_async_copy(source, wbuf.at[rows], sem.at[8 * plane + 2 * kind + other]))
        return made

    for plane in range(4):
        for k in range(4):

            @pl.when(((info[1] + 4 - plane) & 3) == k)
            def _(plane=plane, k=k):
                for copy in copies(plane, k):
                    copy.start()

    def wait_vecs():
        for copy in vecs:
            copy.wait()

    def wait(plane):
        for copy in copies(plane, 0):
            copy.wait()

    return wait_vecs, wait


def order_vec(vbuf, block, vec):
    every = vbuf[:, 0:2, :].astype(F32)
    for q in range(QL // GRAN):
        to, lo = GRAN * (q % 8), GRAN * (q % 3)
        vec[q // 8 : q // 8 + 1, to : to + GRAN] = every[q // 3, block : block + 1, lo : lo + GRAN]


def split_w1(wbuf, w1):
    def step(i, carry):
        rows = wbuf[pl.ds(32 + 4 * i, 4)].astype(F32)
        for j in range(4):
            part = rows[:, 24 * j : 24 * (j + 1), :].reshape(GRAN, D).astype(BF16)
            w1[j, pl.ds(pl.multiple_of(GRAN * i, GRAN), GRAN), :] = part
        return carry

    lax.fori_loop(0, 8, step, 0)


def w_in(wbuf, j):
    return wbuf[0:24, 32 * j : 32 * (j + 1), :].reshape(D, D)


def w_out(wbuf):
    return wbuf[24:32].reshape(D, D)


def w_shrink(wbuf, j):
    return wbuf[64 + 8 * j : 72 + 8 * j].reshape(D, D)


def expander():
    r, c = iota((32, 16), 0), iota((32, 16), 1)
    return ((r < 24) & ((r & 1) == c)).astype(BF16)


def head_mask():
    r, lane = iota((32, D), 0), iota((32, D), 1)
    return (r < 24) & ((r >> 1) == (lane >> 6))


def spread(expand, mask, rows):
    return jnp.where(mask, nn(expand, rows), 0.0).astype(BF16)


def first_forward(
    info, u_ref, *refs
):
    pieces = diagonals = refs[:32]
    y_out, cls_out, xh1_o, rs1_o, xh2_o, rs2_o, gp_o, e_o, h_o, att_o, u_o, q_o, pu_o, qk_o, p_o, vec, vbuf, wflat, w1, sem = refs[32:]
    wait_vecs, wait = fill(info, pieces, diagonals, 0, wflat, vbuf, sem)
    wbuf = wflat.reshape(GRANS, GRAN, D)
    start = info[5]
    u = u_ref[...]
    r, t = iota((16, TOK), 0), iota((16, TOK), 1)
    picker = (((r == 0) & (t == 0)) | ((r == 1) & (t == start))).astype(BF16)
    cls = nn(picker, u)
    cls16 = cls.astype(BF16)
    expand, mask = expander(), head_mask()
    r, t = iota((32, TOK), 0), iota((32, TOK), 1)
    inside = (t >= start).astype(jnp.int32) == (r & 1)
    real = r < 24
    wait_vecs()
    order_vec(vbuf, 0, vec)
    wait(0)
    q = (nn(cls16, w_in(wbuf, 0)) + vec[V_BQ : V_BQ + 1, :]).astype(BF16)
    qk = nt(spread(expand, mask, q), w_in(wbuf, 1)).astype(BF16)
    scores = jnp.where(inside, nt(qk, u) * HEAD_DIM**-0.5, masked_score)
    raised = jnp.exp(scores - jnp.max(scores, axis=-1, keepdims=True))
    portions = jnp.where(real, raised / jnp.sum(raised, axis=-1, keepdims=True), 0.0)
    low = portions.astype(BF16)
    pu = nn(low, u).astype(BF16)
    weight = jnp.sum(low.astype(F32), axis=-1, keepdims=True)
    heads = nn(pu, w_in(wbuf, 2)) + weight * vec[V_BV : V_BV + 1, :]
    att = tn(expand, jnp.where(mask, heads, 0.0).astype(BF16)).astype(BF16)
    wait(1)
    xhat, rstd = norm_forward(cls + nn(att, w_out(wbuf)) + vec[V_BO : V_BO + 1, :])
    xh1_o[...] = xhat
    rs1_o[...] = jnp.broadcast_to(rstd, (16, 128))
    h = xhat * vec[V_G1 : V_G1 + 1, :] + vec[V_C1 : V_C1 + 1, :]
    h16 = h.astype(BF16)
    f = vec[V_B2 : V_B2 + 1, :]
    wait(2)
    split_w1(wbuf, w1)
    wait(3)
    for j in range(4):
        e, gp = gelu_both(nn(h16, w1[j]) + vec[V_B1 + j : V_B1 + j + 1, :])
        e = e.astype(BF16)
        e_o[j] = e
        gp_o[j] = gp
        f = f + nn(e, w_shrink(wbuf, j))
    xhat, rstd = norm_forward(h + f)
    xh2_o[...] = xhat
    rs2_o[...] = jnp.broadcast_to(rstd, (16, 128))
    y = xhat * vec[V_G2 : V_G2 + 1, :] + vec[V_C2 : V_C2 + 1, :]
    y_out[...] = y
    cls_out[...] = y[0:2, :].astype(BF16)
    h_o[...] = h16
    att_o[...] = att
    u_o[...] = cls16
    q_o[...] = q
    pu_o[...] = pu
    qk_o[...] = qk
    p_o[...] = portions


def first_backward(
    info, u_ref, cls_all, dz, vg1, xh1, rs1, xh2, rs2, gp_i, e_i, h_i, att_i, ucls, q_i, pu_i, qk_i, p_i, *refs
):
    pieces = diagonals = refs[:32]
    tg_out, pay_out, loss_out, vec, vbuf, wflat, w1, rows16, dcls, pay, sem = refs[32:]
    wait_vecs, wait = fill(info, pieces, diagonals, 0, wflat, vbuf, sem)
    wbuf = wflat.reshape(GRANS, GRAN, D)
    start = info[5]
    u = u_ref[...]
    keys = cls_all[...]
    n_keys = keys.shape[0]
    scale = 2.0 / math.sqrt(D)
    r, c = iota((n_keys, n_keys), 0), iota((n_keys, n_keys), 1)
    scores = jnp.where(r == c, masked_score, nt(keys, keys) * scale)
    top = jnp.max(scores, axis=-1, keepdims=True)
    raised = jnp.exp(scores - top)
    total = jnp.sum(raised, axis=-1, keepdims=True)
    partner = jnp.bitwise_xor(r, 2) == c
    positive = jnp.sum(jnp.where(partner, scores, 0.0), axis=-1, keepdims=True)
    terms = top + jnp.log(total) - positive
    loss_out[0, 0] = jnp.sum(terms) * (1.0 / n_keys)
    pull = (raised / total - partner.astype(F32)).astype(BF16)
    dcls[...] = (nn(pull, keys) + tn(pull, keys)) * scale
    rows16[...] = jnp.zeros((16, D), F32)
    rows16[0:1, :] = dz[0:1, :] + dcls[pl.ds(2 * info[0], 1), :]
    rows16[1:2, :] = dz[pl.ds(start, 1), :] + dcls[pl.ds(2 * info[0] + 1, 1), :]
    dy = rows16[...]
    wait_vecs()
    order_vec(vbuf, 0, vec)
    for plane in range(4):
        wait(plane)
    split_w1(wbuf, w1)
    xhat = xh2[...]
    pay[R_VEC + 14 : R_VEC + 15, :] = colsum(dy * xhat)
    pay[R_VEC + 15 : R_VEC + 16, :] = colsum(dy)
    dr2 = norm_backward(dy, vec[V_G2 : V_G2 + 1, :], xhat, rs2[:, 0:1])
    df = dr2.astype(BF16)
    pay[R_DF : R_DF + 2, :] = df.astype(F32)[0:2, :]
    dh = dr2
    for j in range(4):
        da = (gp_i[j] * nt(df, w_shrink(wbuf, j))).astype(BF16)
        pay[R_E + 2 * j : R_E + 2 * j + 2, :] = e_i[j].astype(F32)[0:2, :]
        pay[R_DA + 2 * j : R_DA + 2 * j + 2, :] = da.astype(F32)[0:2, :]
        dh = dh + nt(da, w1[j])
    xhat = xh1[...]
    pay[R_VEC + 12 : R_VEC + 13, :] = colsum(dh * xhat)
    pay[R_VEC + 13 : R_VEC + 14, :] = colsum(dh)
    dr1 = norm_backward(dh, vec[V_G1 : V_G1 + 1, :], xhat, rs1[:, 0:1])
    do = dr1.astype(BF16)
    datt = nt(do, w_out(wbuf)).astype(BF16)
    expand, mask = expander(), head_mask()
    portions = p_i[...]
    low = portions.astype(BF16)
    each = spread(expand, mask, datt)
    dvk = nt(each, w_in(wbuf, 2)).astype(BF16)
    constant = jnp.sum(each.astype(F32) * vec[V_BV : V_BV + 1, :], axis=-1, keepdims=True)
    dp = nt(dvk, u) + constant
    ds = (portions * (dp - jnp.sum(dp * portions, axis=-1, keepdims=True))).astype(BF16)
    dsu = nn(ds, u)
    part = jnp.where(mask, nn(dsu.astype(BF16), w_in(wbuf, 1)) * HEAD_DIM**-0.5, 0.0).astype(BF16)
    dq = tn(expand, part).astype(BF16)
    rows16[...] = dr1 + nt(dq, w_in(wbuf, 0))
    du = tn(ds, qk_i[...]) * HEAD_DIM**-0.5 + tn(low, dvk)
    is_cls = (iota((TOK, 1), 0) == 0) | (iota((TOK, 1), 0) == start)
    tg_out[...] = du + jnp.where(is_cls, 0.0, dz[...])
    tg_out[0:1, :] = tg_out[0:1, :] + rows16[0:1, :]
    tg_out[pl.ds(start, 1), :] = tg_out[pl.ds(start, 1), :] + rows16[1:2, :]
    for row, rows in ((R_H, h_i), (R_ATT, att_i), (R_U, ucls), (R_Q, q_i)):
        pay[row : row + 2, :] = rows[...].astype(F32)[0:2, :]
    for row, rows in ((R_DO, do), (R_DQ, dq), (R_DATT, datt)):
        pay[row : row + 2, :] = rows.astype(F32)[0:2, :]
    pay[R_WK : R_WK + 24, :] = dsu[0:24, :] * HEAD_DIM**-0.5
    pay[R_PU : R_PU + 24, :] = pu_i[...].astype(F32)[0:24, :]
    pay[R_VEC : R_VEC + 12, :] = vg1[0:12, :]
    pay_out[...] = pay[...].astype(BF16)


def lanes(p):
    return pl.ds(pl.multiple_of(128 * p, 128), 128)


def send_groups(info, grads, planes, outs, sem):
    sends = []
    for other in (1, 0):
        for i, t in enumerate(planes):
            for kind, parts in ((3, ((SY + 144 * i, 0), (SX + 144 * i, 144))),
                                (1, ((QX + 144 * i, 0), (SX + 288 + 144 * i, 144))),
                                (2, ((SY + 288 + 144 * i, 0), (QY + 144 * i, 144))),
                                (0, ((OWN + 288 * i, 0),))):
                dev = owner(info, t, kind, other)
                rows = 288 if kind == 0 else 144
                for to, lo in parts:
                    source = grads.at[pl.ds(pl.multiple_of(288 * dev + lo, 16), rows)]
                    sends.append(pltpu.make_async_copy(source, outs[1 - other][to // HALF].at[pl.ds(to % HALF, rows)], sem.at[len(sends)]))
                    sends[-1].start()
    return sends


def second_block(info, u_ref, cot_ref, y_ref, *refs):
    pieces = refs[:32]
    diagonals = {4 * i + 3: refs[32 + i] for i in range(8)}
    head_out, dr_out, vg_out = refs[40:43]
    mids_out = refs[43:48]
    pm_out, w1_grad, theirs1, theirs2, mine1, mine2 = refs[48:54]
    (vec, vbuf, wflat, w1, grads, zf, pm, xh1, hb, ht, gp, es, das, xh2, acc, stage, dfs, zb, qs, ks, vs, att, sem, osem) = refs[54:]
    wait_vecs, wait = fill(info, pieces, diagonals, 1, wflat, vbuf, sem)
    wbuf = wflat.reshape(GRANS, GRAN, D)
    gbuf = grads.reshape(GRANS, GRAN, D)
    start = info[5]
    zf[...] = u_ref[...].astype(F32)
    zf[0:1, :] = y_ref[0:1, :]
    zf[pl.ds(start, 1), :] = y_ref[1:2, :]
    z16 = zf[...].astype(BF16)
    zb[...] = z16
    wait_vecs()
    order_vec(vbuf, 1, vec)
    wait(0)
    qs[...] = (nn(z16, w_in(wbuf, 0)) + vec[V_BQ : V_BQ + 1, :]).astype(BF16)
    ks[...] = nn(z16, w_in(wbuf, 1)).astype(BF16)
    vs[...] = (nn(z16, w_in(wbuf, 2)) + vec[V_BV : V_BV + 1, :]).astype(BF16)
    low_lane = iota((TOK, 128), 1) < HEAD_DIM
    same = (iota((TOK, TOK), 0) >= start) == (iota((TOK, TOK), 1) >= start)

    def attend(p, carry):
        qp, kp, vp = qs[:, lanes(p)], ks[:, lanes(p)], vs[:, lanes(p)]
        res = []
        for hh in range(2):
            qm = jnp.where(low_lane == (hh == 0), qp, jnp.zeros_like(qp))
            s = jnp.where(same, nt(qm, kp) * HEAD_DIM**-0.5, masked_score)
            raised = jnp.exp(s - jnp.max(s, axis=-1, keepdims=True))
            portions = raised / jnp.sum(raised, axis=-1, keepdims=True)
            pm[2 * p + hh] = portions
            res.append(nn(portions.astype(BF16), vp))
        att[:, lanes(p)] = jnp.where(low_lane, res[0], res[1]).astype(BF16)
        return carry

    lax.fori_loop(0, 6, attend, 0, unroll=True)
    saved = [pltpu.make_async_copy(pm, pm_out, osem.at[28])]
    for i, (source, out) in enumerate(zip((zb, qs, ks, vs, att), mids_out)):
        saved.append(pltpu.make_async_copy(source, out, osem.at[30 + i]))
    for copy in saved:
        copy.start()
    wait(1)
    xhat, rstd1 = norm_forward(zf[...] + (nn(att[...], w_out(wbuf)) + vec[V_BO : V_BO + 1, :]))
    xh1[...] = xhat
    h = xhat * vec[V_G1 : V_G1 + 1, :] + vec[V_C1 : V_C1 + 1, :]
    hb[...] = h.astype(BF16)
    ht[...] = h.T.astype(BF16)
    acc[...] = h + vec[V_B2 : V_B2 + 1, :]
    wait(2)
    split_w1(wbuf, w1)
    wait(3)
    for j in range(4):
        e, slope = gelu_both(nn(hb[...], w1[j]) + vec[V_B1 + j : V_B1 + j + 1, :])
        gp[j] = slope
        e = e.astype(BF16)
        es[j] = e
        acc[...] += nn(e, w_shrink(wbuf, j))
    xhat, rstd2 = norm_forward(acc[...])
    xh2[...] = xhat
    head_out[...] = (xhat * vec[V_G2 : V_G2 + 1, :] + vec[V_C2 : V_C2 + 1, :]).astype(BF16)

    vg_out[...] = jnp.zeros((16, D), F32)
    dy = cot_ref[...].astype(F32)
    vg_out[V_G2 : V_G2 + 1, :] = colsum(dy * xh2[...])
    vg_out[V_C2 : V_C2 + 1, :] = colsum(dy)
    dr = norm_backward(dy, vec[V_G2 : V_G2 + 1, :], xh2[...], rstd2)
    acc[...] = dr
    df = dr.astype(BF16)
    dfs[...] = df
    vg_out[V_B2 : V_B2 + 1, :] = colsum(df.astype(F32))
    for j in range(4):
        df = dfs[...]
        gbuf[64 + 8 * j : 72 + 8 * j] = tn(es[j], df).astype(BF16).reshape(8, GRAN, D)
        da = (gp[j] * nt(df, w_shrink(wbuf, j))).astype(BF16)
        das[j] = da
        vg_out[V_B1 + j : V_B1 + j + 1, :] = colsum(da.astype(F32))

    def expand_grad(i, carry):
        rows = ht[pl.ds(pl.multiple_of(192 * i, 192), 192), :]
        for j in range(4):
            stage[:, 24 * j : 24 * (j + 1), :] = nn(rows, das[j]).reshape(8, 24, D)
        gbuf[pl.ds(32 + 8 * i, 8)] = stage[...].astype(BF16)
        return carry

    lax.fori_loop(2, 4, expand_grad, 0)
    saved += send_groups(info, grads, GROUPS[0], ((theirs1, theirs2), (mine1, mine2)), osem)
    lax.fori_loop(0, 2, expand_grad, 0)
    saved.append(pltpu.make_async_copy(grads.at[pl.ds(3072, 1536)], w1_grad, osem.at[29]))
    saved[-1].start()
    for j in range(4):
        acc[...] += nt(das[j], w1[j])
    dh = acc[...]
    vg_out[V_G1 : V_G1 + 1, :] = colsum(dh * xh1[...])
    vg_out[V_C1 : V_C1 + 1, :] = colsum(dh)
    dr_out[...] = norm_backward(dh, vec[V_G1 : V_G1 + 1, :], xh1[...], rstd1)
    for copy in saved:
        copy.wait()


def second_attention(info, dr, vg_in, zb, qs, ks, vs, att, *refs):
    pieces = refs[:32]
    pm_in, w1_grad, dz_out, vg_out, theirs1, theirs2, mine1, mine2, wflat, grads, pm, datt, dqs, dks, dvs, sem = refs[32:]
    wbuf = wflat.reshape(GRANS // 2, GRAN, D)
    gbuf = grads.reshape(GRANS // 2, GRAN, D)
    waits = []
    for other in (0, 1):
        for k in range(4):
            for kind in range(4):
                i = 16 * other + 4 * k + kind
                dev = owner(info, (info[1] + 4 - k) & 3, kind, other)
                source = pieces[i].at[pl.ds(SEND_ONE if kind < 3 or k == 2 else 0, 288)]
                rows = pl.ds(pl.multiple_of(288 * jnp.minimum(dev, 15), 16), 288)
                copy = pltpu.make_async_copy(source, wflat.at[rows], sem.at[i])
                used = dev < 11
                pl.when(used)(copy.start)
                waits.append((used, copy))
    saved = [
        pltpu.make_async_copy(pm_in, pm, sem.at[32]),
        pltpu.make_async_copy(w1_grad, grads.at[pl.ds(3072, 1536)], sem.at[33]),
    ]
    for copy in saved:
        copy.start()
    vg_out[...] = vg_in[...]
    do = dr[...].astype(BF16)
    vg_out[V_BO : V_BO + 1, :] = colsum(do.astype(F32))
    gbuf[24:32] = tn(att[...], do).astype(BF16).reshape(8, GRAN, D)
    for used, copy in waits:
        pl.when(used)(copy.wait)
    datt[...] = nt(do, w_out(wbuf)).astype(BF16)
    saved[0].wait()
    low_lane = iota((TOK, 128), 1) < HEAD_DIM

    def attend_back(p, carry):
        qp, kp, vp, dp_ = qs[:, lanes(p)], ks[:, lanes(p)], vs[:, lanes(p)], datt[:, lanes(p)]
        dq, dk, dv = [], [], []
        for hh in range(2):
            portions = pm[2 * p + hh]
            dam = jnp.where(low_lane == (hh == 0), dp_, jnp.zeros_like(dp_))
            dp = nt(dam, vp)
            dv.append(tn(portions.astype(BF16), dp_))
            ds = (portions * (dp - jnp.sum(dp * portions, axis=-1, keepdims=True))).astype(BF16)
            dq.append(nn(ds, kp))
            dk.append(tn(ds, qp))
        dqs[:, lanes(p)] = (jnp.where(low_lane, dq[0], dq[1]) * HEAD_DIM**-0.5).astype(BF16)
        dks[:, lanes(p)] = (jnp.where(low_lane, dk[0], dk[1]) * HEAD_DIM**-0.5).astype(BF16)
        dvs[:, lanes(p)] = jnp.where(low_lane, dv[0], dv[1]).astype(BF16)
        return carry

    lax.fori_loop(0, 6, attend_back, 0, unroll=True)
    vg_out[V_BQ : V_BQ + 1, :] = colsum(dqs[...].astype(F32))
    vg_out[V_BV : V_BV + 1, :] = colsum(dvs[...].astype(F32))
    dz = dr[...]
    for j, part in enumerate((dqs, dks, dvs)):
        gbuf[0:24, 32 * j : 32 * (j + 1), :] = tn(zb[...], part[...]).astype(BF16).reshape(24, 32, D)
    saved[1].wait()
    sends = send_groups(info, grads, GROUPS[1], ((theirs1, theirs2), (mine1, mine2)), sem)
    for j, part in enumerate((dqs, dks, dvs)):
        dz = dz + nt(part[...], w_in(wbuf, j))
    dz_out[...] = dz
    for copy in sends:
        copy.wait()


def total_kernel(mine, came, over_x, over_y, last_x, last_y, first, second):
    for i, out in enumerate((first, second)):
        part = slice(144 * i, 144 * (i + 1))
        for half, (one, two) in enumerate(((last_x, over_y), (over_x, last_y))):
            own = slice(288 * i + 144 * half, 288 * i + 144 * (half + 1))
            both = mine[own, :].astype(F32) + came[own, :].astype(F32)
            out[144 * half : 144 * (half + 1), :] = (
                both + one[part, :].astype(F32) + two[part, :].astype(F32)
            ).astype(BF16)


def owner_grad(info, *refs):
    pieces = refs[:10]
    out, vec_out, pbuf, abuf, qbuf, sem = refs[10:]
    copies = []
    at = 0
    for i, piece in enumerate(pieces):
        copies.append(pltpu.make_async_copy(piece, pbuf.at[pl.ds(at, piece.shape[0])], sem.at[i]))
        at += piece.shape[0]
    for c in copies:
        c.start()
    for c in copies:
        c.wait()
    n_rows = 32 * PAY
    each = pbuf.reshape(32, PAY, D)
    r, c = iota((PAY, n_rows), 0), iota((PAY, n_rows), 1)
    place = c - PAY * ((c * 43691) >> 22)
    tot = nn((place == r).astype(BF16), pbuf[...])
    for row, first in [(V_BQ, R_DQ), (V_BV, R_DATT), (V_BO, R_DO), (V_B2, R_DF)] + [
        (V_B1 + j, R_DA + 2 * j) for j in range(4)
    ]:
        vec_out[row : row + 1, :] = tot[first : first + 1, :] + tot[first + 1 : first + 2, :]
    vec_out[V_G1 : V_C1 + 1, :] = tot[R_VEC + 12 : R_VEC + 14, :]
    vec_out[V_G2 : V_C2 + 1, :] = tot[R_VEC + 14 : R_VEC + 16, :]
    vec_out[12:24, :] = tot[R_VEC : R_VEC + 12, :]

    def pick_rows(*firsts):
        r, c = iota((64, n_rows), 0), iota((64, n_rows), 1)
        base = PAY * (r >> 1) + (r & 1)
        select = jnp.concatenate([(c == base + first).astype(BF16) for first in firsts], 0)
        got = nn(select, pbuf[...]).astype(BF16)
        return [got[64 * i : 64 * (i + 1), :] for i in range(len(firsts))]

    def chosen(count, offset, source):
        one_hot = (iota((count, D), 1) == iota((count, D), 0) + offset).astype(BF16)
        return nt(one_hot, source).astype(BF16)

    def put(gi, n, p, value):
        m = GRAN // n
        for j in range(6):
            out[pl.ds(6 * (GRAN * gi + p) + j, m, stride=6 * n), :] = value[:, 128 * j : 128 * (j + 1)]

    @pl.when(info[0] < 8)
    def _():
        off = GRAN * info[0]
        ucls, dq, q, datt = pick_rows(R_U, R_DQ, R_Q, R_DATT)
        parts = [nn(chosen(GRAN, off, ucls), dq)]
        r, c = iota((D, 64), 0), iota((D, 64), 1)
        inside = r - 24 * (c >> 1)
        expand = ((inside >= 0) & (inside < 24) & ((r & 1) == (c & 1))).astype(BF16)
        r = iota((D, D), 0)
        mine = (r - 24 * ((r * 2731) >> 16)) >> 1 == iota((D, D), 1) >> 6
        for right, lo, skip in ((q, 32, 0), (datt, 48, 8)):
            qbuf[...] = jnp.where(mine, nn(expand, right), 0.0).astype(BF16)

            def compact(i, carry, lo=lo, skip=skip):
                rows = each[pl.ds(8 * i, 8), lo : lo + 32, :].astype(F32)
                abuf[pl.ds(pl.multiple_of(192 * i, 192), 192), :] = (
                    rows[:, skip : skip + 24, :].reshape(192, D).astype(BF16)
                )
                return carry

            lax.fori_loop(0, 4, compact, 0)
            parts.append(nn(chosen(GRAN, off, abuf[...]), qbuf[...]))
        for gi in range(3):
            for p in range(3):
                put(gi, 3, p, parts[p][32 * gi : 32 * (gi + 1), :])

    for gi in range(3):
        g = 3 * info[0] + gi

        @pl.when((g >= 24) & (g < 32))
        def _(gi=gi, g=g):
            left, right = pick_rows(R_ATT, R_DO)
            put(gi, 1, 0, nn(chosen(GRAN, GRAN * (g - 24), left), right))

        @pl.when((g >= 32) & (g < 64))
        def _(gi=gi, g=g):
            left, *rights = pick_rows(R_H, *[R_DA + 2 * p for p in range(4)])
            left = chosen(32, 24 * (g - 32), left)
            for p in range(4):
                put(gi, 4, p, nn(left, rights[p])[0:24, :])

        @pl.when(g >= 64)
        def _(gi=gi, g=g):
            left, right = pick_rows(R_E + 2 * ((g - 64) >> 3), R_DF)
            put(gi, 1, 0, nn(chosen(GRAN, GRAN * ((g - 64) & 7), left), right))


def join_grads(info, g0, a, b, gv, out, square, buf):
    g = g0[...]
    out[pl.ds(0, 1728, stride=2), :] = g
    buf[...] = a[...].astype(F32) + b[...].astype(F32)
    total = buf[...]
    sq = jnp.sum((g * g).reshape(216, 8, 128), axis=0)
    for j in range(6):
        v = total[:, 128 * j : 128 * (j + 1)]
        sq = sq + jnp.sum((v * v).reshape(36, 8, 128), axis=0)
    whole = jnp.sum(colsum(sq), axis=1, keepdims=True)
    whole = whole + jnp.sum(colsum(gv[...] * gv[...]), axis=1, keepdims=True)
    square[...] = jnp.broadcast_to(whole, (8, 128))
    for gi in range(3):

        def emit(n, gi=gi):
            m = GRAN // n
            for p in range(n):
                for j in range(6):
                    out[pl.ds(12 * (GRAN * gi + p) + 2 * j + 1, m, stride=12 * n), :] = buf[
                        GRAN * gi + m * p : GRAN * gi + m * (p + 1), 128 * j : 128 * (j + 1)
                    ]

        by_kind(3 * info[0] + gi, emit)


def adamw_kernel(sq0, sq1, sq2, sq3, w, m, v, g, vw, vm, vv, vg, w_new, m_new, v_new, vw_new, vm_new, vv_new, norm_out):
    norm = jnp.sqrt((sq0[...] + sq1[...]) + (sq2[...] + sq3[...]))
    norm_out[0, 0] = norm[0, 0]
    coef = jnp.minimum(1.0, math.sqrt(2 * (PL + QL)) / (norm[0:1, 0:1] + 1e-06))
    w_new[...], m_new[...], v_new[...] = adamw_update(w[...], m[...], v[...], g[...] * coef, 0.1, weight_decay)
    vw_new[...], vm_new[...], vv_new[...] = adamw_update(vw[...], vm[...], vv[...], vg[...] * coef, 0.5, 0.0)


def adamw_update(weight, moment_one, moment_two, gradient, step_rate, decay_rate):
    first_new = beta_one * moment_one + (1.0 - beta_one) * gradient
    second_new = beta_two * moment_two + (1.0 - beta_two) * gradient * gradient
    first_hat = first_new / (1.0 - beta_one**STEP)
    second_hat = second_new / (1.0 - beta_two**STEP)
    weight_new = weight - step_rate * (first_hat / (jnp.sqrt(second_hat) + adam_epsilon) + decay_rate * weight)
    return (weight_new, first_new, second_new)


def order_kernel(info, a3, a2, mine, came, over_x, over_y, last_x, last_y, o1, o2, o3, o0, acc):
    acc[3], acc[2] = a3[...], a2[...]
    total_kernel(mine, came, over_x, over_y, last_x, last_y, acc.at[1], acc.at[0])
    for k, out in enumerate((o1, o2, o3, o0)):
        out[...] = acc[(info[1] + 3 - k) & 3]


SMEM = pl.BlockSpec(memory_space=pltpu.SMEM)
VMEM = pl.BlockSpec(memory_space=pltpu.VMEM)
ANY = pl.BlockSpec(memory_space=pl.ANY)


def struct(*shape, dtype=F32):
    return jax.ShapeDtypeStruct(shape, dtype)


def call(kernel, name, ins, in_specs, outs, out_specs, scratch=(), flops=0, moved=0):
    return pl.pallas_call(
        kernel,
        out_shape=outs,
        in_specs=in_specs,
        out_specs=out_specs,
        scratch_shapes=list(scratch),
        name=name,
        compiler_params=pltpu.CompilerParams(vmem_limit_bytes=VMEM_BYTES),
        cost_estimate=pl.CostEstimate(flops=flops, bytes_accessed=moved, transcendentals=0),
    )(*ins)


def flat_view(a):
    return a.reshape(2, -1, 128).transpose(1, 0, 2).reshape(-1, 128)


def flat_back(a):
    return a.reshape(-1, 2, 128).transpose(1, 0, 2).reshape(2, -1)


def body(tokens, cotangent, lengths, mats, mats_m, mats_v, vecs, vecs_m, vecs_v):
    dp, pair = lax.axis_index("dp"), lax.axis_index("pair")
    device = 2 * dp + pair
    z = dp >> 2
    info = jnp.stack(
        [device, z, (dp >> 1) & 1, dp & 1, pair, lengths[0, 0, 0], jnp.int32(0), jnp.int32(0)]
    ).astype(jnp.int32)
    u = tokens[0]
    cot = cotangent[0]
    flat = flat_view(mats)
    own = call(pack_kernel, "pack", (device.reshape(1), flat, vecs), [SMEM, VMEM, VMEM], struct(SEND, D, dtype=BF16), VMEM)
    pieces0, pieces1 = gather_blocks(own)
    row = struct(16, D)
    row16 = struct(16, D, dtype=BF16)
    saved_shapes = (
        row, struct(16, 128), row, struct(16, 128), struct(4, 16, D), struct(4, 16, D, dtype=BF16),
        row16, row16, row16, row16, struct(32, D, dtype=BF16), struct(32, D, dtype=BF16), struct(32, TOK),
    )
    weights = [
        pltpu.VMEM((16, D), F32),
        pltpu.VMEM((32, 16, D), BF16),
        pltpu.VMEM((GRANS * GRAN, D), BF16),
        pltpu.VMEM((4, D, D), BF16),
    ]
    y_cls, cls, *saved = call(
        first_forward,
        "first_forward",
        (info, u, *pieces0),
        [SMEM, VMEM] + [ANY] * 32,
        (row, struct(2, D, dtype=BF16), *saved_shapes),
        (VMEM,) * 15,
        weights + [pltpu.SemaphoreType.DMA((64,))],
        flops=2 * 32 * PL,
        moved=2 * PL,
    )
    part = struct(HALF, D, dtype=BF16)
    mid16 = pltpu.VMEM((TOK, D), BF16)
    mid = pltpu.VMEM((TOK, D), F32)
    low = struct(TOK, D, dtype=BF16)
    head_out, dr, vg1, zb, qs, ks, vs, att, pm, w1_grad, theirs_a1, theirs_a2, mine_a1, mine_a2 = call(
        second_block,
        "second_block",
        (info, u, cot, y_cls, *pieces1, *pieces0[3::4]),
        [SMEM, VMEM, VMEM, VMEM] + [ANY] * 40,
        (low, struct(TOK, D), row, low, low, low, low, low, struct(HEADS, TOK, TOK), struct(1536, D, dtype=BF16)) + (part,) * 4,
        (VMEM,) * 3 + (ANY,) * 11,
        weights
        + [
            pltpu.VMEM((GRANS * GRAN, D), BF16),
            mid,
            pltpu.VMEM((HEADS, TOK, TOK), F32),
            mid, mid16,
            pltpu.VMEM((D, TOK), BF16),
            pltpu.VMEM((4, TOK, D), F32),
            pltpu.VMEM((4, TOK, D), BF16),
            pltpu.VMEM((4, TOK, D), BF16),
            mid, mid,
            pltpu.VMEM((8, GRAN, D), F32),
            mid16,
            mid16, mid16, mid16, mid16, mid16,
            pltpu.SemaphoreType.DMA((64,)),
            pltpu.SemaphoreType.DMA((35,)),
        ],
        flops=4 * TOK * PL,
        moved=4 * PL,
    )

    def first_part(mine, came):
        return [add16(mine[lo:hi], came[lo:hi]) for lo, hi in ((SX, SY), (SY, QX))]

    def last_part(mine, came, over_x, over_y):
        return [
            (mine[lo : lo + 288].astype(F32) + came[lo : lo + 288].astype(F32) + over[:288].astype(F32)).astype(BF16)
            for lo, over in ((QX - HALF, over_y), (QY - HALF, over_x))
        ]

    own_rows, half = pl.BlockSpec((576, D), lambda i: (1, 0)), pl.BlockSpec((288, D), lambda i: (0, 0))
    second = pl.BlockSpec((288, D), lambda i: (1, 0))

    def plane_total(mine, came, over_x, over_y, last_x, last_y):
        return pl.pallas_call(
            total_kernel,
            grid=(1,),
            in_specs=[own_rows, own_rows, second, second, half, half],
            out_specs=[half, half],
            out_shape=[struct(288, D, dtype=BF16)] * 2,
            name="total",
        )(mine, came, over_x, over_y, last_x, last_y)

    cls = gather_step(cls, 0, device)()
    theirs_a1, theirs_a2, cls = fence([theirs_a1, theirs_a2, cls])
    came_a1, came_a2 = core_flip(theirs_a1), core_flip(theirs_a2)
    cls = gather_step(cls, 1, device)()
    sx, sy, cls, dr = fence([*first_part(mine_a1, came_a1), cls, dr])
    over_xa, over_ya = x_flip(sx), y_flip(sy)
    dz, vg1, theirs_b1, theirs_b2, mine_b1, mine_b2 = call(
        second_attention,
        "second_attention",
        (info, dr, vg1, zb, qs, ks, vs, att, *pieces1, pm, w1_grad),
        [SMEM] + [VMEM] * 7 + [ANY] * 34,
        (struct(TOK, D), row) + (part,) * 4,
        (VMEM, VMEM) + (ANY,) * 4,
        [
            pltpu.VMEM((GRANS * GRAN // 2, D), BF16),
            pltpu.VMEM((GRANS * GRAN // 2, D), BF16),
            pltpu.VMEM((HEADS, TOK, TOK), F32),
            mid16, mid16, mid16, mid16,
            pltpu.SemaphoreType.DMA((34,)),
        ],
        flops=2 * TOK * PL,
        moved=2 * PL,
    )
    qx_a, qy_a, theirs_b1, theirs_b2, cls = fence(
        [*last_part(mine_a2, came_a2, over_xa, over_ya), theirs_b1, theirs_b2, cls]
    )
    last_xa, last_ya = x_flip(qx_a), y_flip(qy_a)
    came_b1 = core_flip(theirs_b1)
    every_cls = gather_step(cls, 2, device)()
    sx, sy, dz, theirs_b2 = fence([*first_part(mine_b1, came_b1), dz, theirs_b2])
    over_xb, over_yb = x_flip(sx), y_flip(sy)
    came_b2 = core_flip(theirs_b2)
    token_grad, payload, loss = call(
        first_backward,
        "first_backward",
        (info, u, every_cls, dz, vg1, *saved, *pieces0),
        [SMEM] + [VMEM] * 17 + [ANY] * 32,
        (struct(TOK, D), struct(PAY, D, dtype=BF16), struct(1, 1)),
        (VMEM, VMEM, SMEM),
        weights
        + [
            pltpu.VMEM((16, D), F32),
            pltpu.VMEM((64, D), F32),
            pltpu.VMEM((PAY, D), F32),
            pltpu.SemaphoreType.DMA((64,)),
        ],
        flops=2 * 32 * PL,
        moved=2 * PL,
    )
    qx_b, qy_b, pay, last_xa, last_ya = fence(
        [*last_part(mine_b2, came_b2, over_xb, over_yb), payload, last_xa, last_ya]
    )
    last_xb, last_yb = x_flip(qx_b), y_flip(qy_b)
    a3, a2 = plane_total(mine_a2, came_a2, over_xa, over_ya, last_xa, last_ya)
    slots = jnp.concatenate([pay, z_turn(pay, 1), z_turn(pay, 3), z_turn(pay, 2)], 0)
    in_turn = pl.pallas_call(
        order_kernel,
        grid=(1,),
        in_specs=[SMEM, half, half, own_rows, own_rows, second, second, half, half],
        out_specs=[half] * 4,
        out_shape=[struct(288, D, dtype=BF16)] * 4,
        scratch_shapes=[pltpu.VMEM((4, 288, D), BF16)],
        name="order",
    )(info, a3, a2, mine_b2, came_b2, over_xb, over_yb, last_xb, last_yb)
    moving = z_up(in_turn[0])
    over_x, over_y = x_flip(slots), y_flip(slots)
    rows = [slots, over_x, over_y]
    moving = z_up(add16(in_turn[1], moving))
    half = rows[0].shape[0] // 2
    rows += [y_flip(rows[1][:half]), x_flip(rows[2][half:])]
    rows += [core_flip(v) for v in rows]
    moving = z_up(add16(in_turn[2], moving))
    flat0, vec_sum = call(
        owner_grad,
        "owner_grad",
        (info, *rows),
        [SMEM] + [ANY] * 10,
        (struct(1728, 128), struct(24, D)),
        (VMEM, VMEM),
        [
            pltpu.VMEM((32 * PAY, D), BF16),
            pltpu.VMEM((D, D), BF16),
            pltpu.VMEM((D, D), BF16),
            pltpu.SemaphoreType.DMA((10,)),
        ],
        flops=2 * 768 * 768 * 768,
        moved=2 * 32 * PAY * D,
    )
    grad_vecs = lax.dynamic_slice(vec_sum.reshape(2, QL), (0, device * vecs.shape[1]), vecs.shape)
    grads, square = call(
        join_grads,
        "join_grads",
        (info, flat0, in_turn[3], moving, grad_vecs),
        [SMEM] + [VMEM] * 4,
        (struct(3456, 128), struct(8, 128)),
        (VMEM, VMEM),
        [pltpu.VMEM((288, D), F32)],
    )
    block = pl.BlockSpec((864, 128), lambda i: (i, 0))
    small = pl.BlockSpec(vecs.shape, lambda i: (0, 0))
    tile = pl.BlockSpec((8, 128), lambda i: (0, 0))
    *new, new_vecs, new_vecs_m, new_vecs_v, norm = pl.pallas_call(
        adamw_kernel,
        grid=(4,),
        in_specs=[tile] * 4 + [block] * 4 + [small] * 4,
        out_specs=(block,) * 3 + (small,) * 3 + (SMEM,),
        out_shape=(struct(3456, 128),) * 3 + (struct(*vecs.shape),) * 3 + (struct(1, 1),),
        name="adamw",
    )(*sum_quick(square), flat, flat_view(mats_m), flat_view(mats_v), grads, vecs, vecs_m, vecs_v, grad_vecs)
    new_mats, new_mats_m, new_mats_v = [flat_back(a) for a in new]
    return (
        head_out[None],
        token_grad[None],
        loss.reshape(()),
        norm.reshape(()),
        new_mats,
        new_mats_m,
        new_mats_v,
        new_vecs,
        new_vecs_m,
        new_vecs_v,
    )


def matmul(left_side, right_side):
    return jnp.dot(left_side, right_side, preferred_element_type=jnp.float32)


def inner_rows(left_side, right_side):
    return lax.dot_general(
        left_side, right_side, (((0,), (0,)), ((), ())), preferred_element_type=jnp.float32
    )


def outer_cols(left_side, right_side):
    return lax.dot_general(
        left_side, right_side, (((1,), (1,)), ((), ())), preferred_element_type=jnp.float32
    )


def exact_dot(left_side, right_side):
    return jnp.dot(
        left_side, right_side, precision=lax.Precision.HIGHEST, preferred_element_type=jnp.float32
    )


def layer_norm(resid, gain, shift):
    centred = resid - jnp.mean(resid, axis=-1, keepdims=True)
    spread = jnp.mean(centred * centred, axis=-1, keepdims=True)
    return centred * lax.rsqrt(spread + norm_epsilon) * gain + shift


def gelu_exact(before):
    return jax.nn.gelu(before, approximate=False)


def unpack(mat_row, vec_row):
    edge_one = 3 * D * D
    edge_two = 4 * D * D
    edge_three = edge_two + D * FF
    input_weight = mat_row[:edge_one].reshape(D, 3 * D)
    output_weight = mat_row[edge_one:edge_two].reshape(D, D)
    expand_weight = mat_row[edge_two:edge_three].reshape(D, FF)
    shrink_weight = mat_row[edge_three:].reshape(FF, D)
    vector = vec_row.astype(jnp.float32)
    pieces = []
    cursor = 0
    for piece_len in (D, D, D, D, D, FF, D, D, D):
        pieces.append(vector[cursor : cursor + piece_len])
        cursor = cursor + piece_len
    return (input_weight, output_weight, expand_weight, shrink_weight) + tuple(pieces)


def head_scores(queries, key_rows, same_span):
    row_count = queries.shape[0]
    query_heads = queries.reshape(row_count, HEADS, HEAD_DIM)
    key_heads = key_rows.reshape(row_count, HEADS, HEAD_DIM)
    scores = jnp.einsum(
        "thd,shd->hts", query_heads, key_heads, preferred_element_type=jnp.float32
    ) * HEAD_DIM ** (-0.5)
    return jnp.where(same_span[None, :, :], scores, masked_score)


def layer_forward(params, inputs, same_span):
    (
        input_weight,
        output_weight,
        expand_weight,
        shrink_weight,
        query_bias,
        value_bias,
        output_bias,
        first_gain,
        first_shift,
        expand_bias,
        shrink_bias,
        second_gain,
        second_shift,
    ) = params
    row_count = inputs.shape[0]
    low_input = inputs.astype(jnp.bfloat16)
    joint = matmul(low_input, input_weight)
    queries = (joint[:, :D] + query_bias).astype(jnp.bfloat16)
    key_rows = joint[:, D : 2 * D].astype(jnp.bfloat16)
    values = (joint[:, 2 * D :] + value_bias).astype(jnp.bfloat16)
    scores = head_scores(queries, key_rows, same_span)
    row_max = jnp.max(scores, axis=-1, keepdims=True)
    raised = jnp.exp(scores - row_max)
    summed = jnp.sum(raised, axis=-1, keepdims=True)
    portions = raised / summed
    logsum = row_max + jnp.log(summed)
    value_heads = values.reshape(row_count, HEADS, HEAD_DIM)
    attended = jnp.einsum(
        "hts,shd->thd",
        portions.astype(jnp.bfloat16),
        value_heads,
        preferred_element_type=jnp.float32,
    )
    attended = attended.reshape(row_count, D).astype(jnp.bfloat16)
    resid_one = inputs + (matmul(attended, output_weight) + output_bias)
    hidden = layer_norm(resid_one, first_gain, first_shift)
    low_hidden = hidden.astype(jnp.bfloat16)
    before = matmul(low_hidden, expand_weight) + expand_bias
    activated = gelu_exact(before).astype(jnp.bfloat16)
    resid_two = hidden + (matmul(activated, shrink_weight) + shrink_bias)
    output = layer_norm(resid_two, second_gain, second_shift)
    kept = (
        low_input,
        queries,
        key_rows,
        values,
        logsum,
        attended,
        resid_one,
        low_hidden,
        before,
        activated,
        resid_two,
    )
    return (output, kept)


def layer_backward(params, kept, grad_out, same_span):
    (
        input_weight,
        output_weight,
        expand_weight,
        shrink_weight,
        query_bias,
        value_bias,
        output_bias,
        first_gain,
        first_shift,
        expand_bias,
        shrink_bias,
        second_gain,
        second_shift,
    ) = params
    (
        low_input,
        queries,
        key_rows,
        values,
        logsum,
        attended,
        resid_one,
        low_hidden,
        before,
        activated,
        resid_two,
    ) = kept
    row_count = low_input.shape[0]
    _, norm_pull_two = jax.vjp(layer_norm, resid_two, second_gain, second_shift)
    d_resid_two, d_second_gain, d_second_shift = norm_pull_two(grad_out)
    d_feed = d_resid_two.astype(jnp.bfloat16)
    d_shrink = inner_rows(activated, d_feed)
    d_shrink_bias = jnp.sum(d_feed.astype(jnp.float32), axis=0)
    _, gelu_pull = jax.vjp(gelu_exact, before)
    d_before = gelu_pull(outer_cols(d_feed, shrink_weight))[0].astype(jnp.bfloat16)
    d_expand = inner_rows(low_hidden, d_before)
    d_expand_bias = jnp.sum(d_before.astype(jnp.float32), axis=0)
    d_hidden = d_resid_two + outer_cols(d_before, expand_weight)
    _, norm_pull_one = jax.vjp(layer_norm, resid_one, first_gain, first_shift)
    d_resid_one, d_first_gain, d_first_shift = norm_pull_one(d_hidden)
    d_branch = d_resid_one.astype(jnp.bfloat16)
    d_output = inner_rows(attended, d_branch)
    d_output_bias = jnp.sum(d_branch.astype(jnp.float32), axis=0)
    d_attended = outer_cols(d_branch, output_weight).astype(jnp.bfloat16)
    portions = jnp.exp(head_scores(queries, key_rows, same_span) - logsum)
    query_heads = queries.reshape(row_count, HEADS, HEAD_DIM)
    key_heads = key_rows.reshape(row_count, HEADS, HEAD_DIM)
    value_heads = values.reshape(row_count, HEADS, HEAD_DIM)
    d_att_heads = d_attended.reshape(row_count, HEADS, HEAD_DIM)
    d_portions = jnp.einsum(
        "thd,shd->hts", d_att_heads, value_heads, preferred_element_type=jnp.float32
    )
    d_values = jnp.einsum(
        "hts,thd->shd",
        portions.astype(jnp.bfloat16),
        d_att_heads,
        preferred_element_type=jnp.float32,
    )
    d_values = d_values.reshape(row_count, D).astype(jnp.bfloat16)
    d_scores = portions * (d_portions - jnp.sum(d_portions * portions, axis=-1, keepdims=True))
    d_scores = d_scores.astype(jnp.bfloat16)
    score_scale = HEAD_DIM ** (-0.5)
    d_queries = (
        jnp.einsum("hts,shd->thd", d_scores, key_heads, preferred_element_type=jnp.float32)
        * score_scale
    )
    d_queries = d_queries.reshape(row_count, D).astype(jnp.bfloat16)
    d_keys = (
        jnp.einsum("hts,thd->shd", d_scores, query_heads, preferred_element_type=jnp.float32)
        * score_scale
    )
    d_keys = d_keys.reshape(row_count, D).astype(jnp.bfloat16)
    d_joint = jnp.concatenate([d_queries, d_keys, d_values], axis=1)
    d_input_weight = inner_rows(low_input, d_joint)
    d_query_bias = jnp.sum(d_queries.astype(jnp.float32), axis=0)
    d_value_bias = jnp.sum(d_values.astype(jnp.float32), axis=0)
    d_inputs = d_resid_one + outer_cols(d_joint, input_weight)
    mat_grad = jnp.concatenate(
        [
            d_input_weight.reshape(-1),
            d_output.reshape(-1),
            d_expand.reshape(-1),
            d_shrink.reshape(-1),
        ]
    )
    vec_grad = jnp.concatenate(
        [
            d_query_bias,
            d_value_bias,
            d_output_bias,
            d_first_gain,
            d_first_shift,
            d_expand_bias,
            d_shrink_bias,
            d_second_gain,
            d_second_shift,
        ]
    )
    return (d_inputs, mat_grad, vec_grad)


def contrast_rows(anchors, key_table, anchor_index, span_count, score_scale):
    key_count = key_table.shape[0]
    key_index = jnp.arange(key_count, dtype=jnp.int32)
    scores = outer_cols(anchors, key_table) * score_scale
    scores = jnp.where(anchor_index[:, None] == key_index[None, :], masked_score, scores)
    partner = (
        jnp.bitwise_xor(anchor_index // span_count, 1) * span_count + anchor_index % span_count
    )
    row_max = jnp.max(scores, axis=-1, keepdims=True)
    raised = jnp.exp(scores - row_max)
    summed = jnp.sum(raised, axis=-1, keepdims=True)
    logsum = row_max[:, 0] + jnp.log(summed[:, 0])
    target = key_index[None, :] == partner[:, None]
    positive = jnp.sum(jnp.where(target, scores, 0.0), axis=1)
    grads_low = (raised / summed - target.astype(jnp.float32)).astype(jnp.bfloat16)
    return (grads_low, logsum - positive)


def general_body(tokens, cotangent, lengths, mats, mats_m, mats_v, vecs, vecs_m, vecs_v):
    full_mats, full_vecs = (
        lax.all_gather(mats.astype(jnp.bfloat16), ("dp", "pair"), axis=1, tiled=True),
        lax.all_gather(vecs.astype(jnp.bfloat16), ("dp", "pair"), axis=1, tiled=True),
    )
    layer_one = unpack(full_mats[0], full_vecs[0])
    layer_two = unpack(full_mats[1], full_vecs[1])
    inputs = tokens[0].astype(jnp.float32)
    row_count = inputs.shape[0]
    span_lengths = lengths[0, 0]
    span_count = span_lengths.shape[0]
    positions = jnp.arange(row_count, dtype=jnp.int32)
    order = jnp.arange(span_count)
    starts = jnp.sum(jnp.where(order[None, :] < order[:, None], span_lengths[None, :], 0), axis=1)
    span_of = jnp.sum((positions[:, None] >= starts[None, :]).astype(jnp.int32), axis=1)
    same_span = span_of[:, None] == span_of[None, :]
    heads_mark = positions[None, :] == starts[:, None]
    is_cls = jnp.any(heads_mark, axis=0)[:, None]
    picker = heads_mark.astype(jnp.float32)
    doc_groups = lax.axis_size("dp")
    early_out, kept_one = layer_forward(layer_one, inputs, same_span)
    cls_rows = exact_dot(picker, early_out)
    mixture = jnp.where(is_cls, early_out, inputs)
    late_out, kept_two = layer_forward(layer_two, mixture, same_span)
    sent_cls = cls_rows.astype(jnp.bfloat16)
    every_cls = lax.all_gather(sent_cls, ("dp", "pair"), axis=0, tiled=True)
    key_count = every_cls.shape[0]
    score_scale = 2.0 / math.sqrt(D)
    offset = lax.axis_index(("dp", "pair")) * span_count
    own_index = offset + jnp.arange(span_count, dtype=jnp.int32)
    grads_low, loss_terms = contrast_rows(sent_cls, every_cls, own_index, span_count, score_scale)
    anchor_part = matmul(grads_low, every_cls) * score_scale
    key_part = lax.psum_scatter(
        inner_rows(grads_low, sent_cls) * score_scale,
        ("dp", "pair"),
        scatter_dimension=0,
        tiled=True,
    )
    cls_grad = anchor_part + key_part
    grad_late = cotangent[0].astype(jnp.float32)
    d_mixture, late_mats, late_vecs = layer_backward(layer_two, kept_two, grad_late, same_span)
    grad_early = jnp.where(is_cls, d_mixture, 0.0) + exact_dot(picker.T, cls_grad)
    d_inputs, early_mats, early_vecs = layer_backward(layer_one, kept_one, grad_early, same_span)
    token_grad = d_inputs + jnp.where(is_cls, 0.0, d_mixture)
    all_pieces = (
        lax.all_to_all(
            early_mats.reshape(doc_groups, -1).astype(jnp.bfloat16),
            "dp",
            split_axis=0,
            concat_axis=0,
            tiled=True,
        ).astype(jnp.float32),
        lax.all_to_all(
            late_mats.reshape(doc_groups, -1).astype(jnp.bfloat16),
            "dp",
            split_axis=0,
            concat_axis=0,
            tiled=True,
        ).astype(jnp.float32),
        lax.all_to_all(
            early_vecs.reshape(doc_groups, -1).astype(jnp.bfloat16),
            "dp",
            split_axis=0,
            concat_axis=0,
            tiled=True,
        ).astype(jnp.float32),
        lax.all_to_all(
            late_vecs.reshape(doc_groups, -1).astype(jnp.bfloat16),
            "dp",
            split_axis=0,
            concat_axis=0,
            tiled=True,
        ).astype(jnp.float32),
    )
    early_mats_part, late_mats_part, early_vecs_part, late_vecs_part = (
        lax.psum_scatter(
            jnp.sum(all_pieces[0], axis=0).astype(jnp.bfloat16),
            "pair",
            scatter_dimension=0,
            tiled=True,
        ).astype(jnp.float32),
        lax.psum_scatter(
            jnp.sum(all_pieces[1], axis=0).astype(jnp.bfloat16),
            "pair",
            scatter_dimension=0,
            tiled=True,
        ).astype(jnp.float32),
        lax.psum_scatter(
            jnp.sum(all_pieces[2], axis=0).astype(jnp.bfloat16),
            "pair",
            scatter_dimension=0,
            tiled=True,
        ).astype(jnp.float32),
        lax.psum_scatter(
            jnp.sum(all_pieces[3], axis=0).astype(jnp.bfloat16),
            "pair",
            scatter_dimension=0,
            tiled=True,
        ).astype(jnp.float32),
    )
    grad_mats = jnp.stack([early_mats_part, late_mats_part])
    grad_vecs = jnp.stack([early_vecs_part, late_vecs_part])
    square_sum = jnp.sum(grad_mats * grad_mats) + jnp.sum(grad_vecs * grad_vecs)
    total_sq, loss_sum = lax.psum((square_sum, jnp.sum(loss_terms)), ("dp", "pair"))
    grad_norm = jnp.sqrt(total_sq)
    clip_factor = jnp.minimum(1.0, math.sqrt(2 * (PL + QL)) / (grad_norm + 1e-06))
    new_mats, new_mats_m, new_mats_v = adamw_update(
        mats, mats_m, mats_v, grad_mats * clip_factor, 0.1, weight_decay
    )
    new_vecs, new_vecs_m, new_vecs_v = adamw_update(
        vecs, vecs_m, vecs_v, grad_vecs * clip_factor, 0.5, 0.0
    )
    contrastive = loss_sum / key_count
    return (
        late_out.astype(jnp.bfloat16)[None],
        token_grad[None],
        contrastive,
        grad_norm,
        new_mats,
        new_mats_m,
        new_mats_v,
        new_vecs,
        new_vecs_m,
        new_vecs_v,
    )


def solution(mesh):
    flat = P(None, ("dp", "pair"))
    rows = P("pair", "dp", None)
    here = dict(mesh.shape) == {"dp": 16, "pair": 2}
    return jax.shard_map(
        body if here else general_body,
        mesh=mesh,
        in_specs=(rows, rows, rows) + (flat,) * 6,
        out_specs=(rows, rows, P(), P()) + (flat,) * 6,
        check_vma=False,
    )
```
